32 devices in a mesh: dp: 4 (over x, core), fsdp: 8 (over z, y).
Axes of the slice: x: 2, y: 2, z: 4, core: 2. Of those that a mesh axis runs over, the one named last changes fastest.
Arguments:
- inputs: bfloat16 [32, 1024, 768], P(('dp', 'fsdp')), may hold values from -6 to 6
- history: bfloat16 [4, 32, 1024, 768], P(None, ('dp', 'fsdp')), may hold values from -6 to 6
- cotangent: bfloat16 [32, 1024, 768], P(('dp', 'fsdp')), may hold values from -6 to 6
- lengths: int32 [32], P(('dp', 'fsdp')), may hold values from 128 to 1024, as said below
- joint_weight: bfloat16 [768, 2304], P(('dp', 'fsdp')), may hold values from -0.21875 to 0.21875
- joint_bias: bfloat16 [2304], P(('dp', 'fsdp')), may hold values from -1.5 to 1.5
- output_weight: bfloat16 [768, 768], P(('dp', 'fsdp')), may hold values from -0.875 to 0.875
- output_bias: bfloat16 [768], P(('dp', 'fsdp')), may hold values from -1.5 to 1.5
- first_gain: bfloat16 [768], P(('dp', 'fsdp')), may hold values from 0.5 to 1.5
- first_shift: bfloat16 [768], P(('dp', 'fsdp')), may hold values from -1.5 to 1.5
- second_gain: bfloat16 [768], P(('dp', 'fsdp')), may hold values from 0.5 to 1.5
- second_shift: bfloat16 [768], P(('dp', 'fsdp')), may hold values from -1.5 to 1.5
- upward_weight: bfloat16 [768, 3072], P(('dp', 'fsdp')), may hold values from -0.21875 to 0.21875
- upward_bias: bfloat16 [3072], P(('dp', 'fsdp')), may hold values from -1.5 to 1.5
- downward_weight: bfloat16 [3072, 768], P(('dp', 'fsdp')), may hold values from -0.109375 to 0.109375
- downward_bias: bfloat16 [768], P(('dp', 'fsdp')), may hold values from -1.5 to 1.5
- depth_weights: float32 [5], replicated, may hold values from 0.3 to 1
Outputs:
- layer_output: bfloat16 [32, 1024, 768], P(('dp', 'fsdp'))
- input_gradient: float32 [32, 1024, 768], P(('dp', 'fsdp'))
- history_gradient: float32 [4, 32, 1024, 768], P(None, ('dp', 'fsdp'))
- joint_weight_gradient: float32 [768, 2304], P(('dp', 'fsdp'))
- joint_bias_gradient: float32 [2304], P(('dp', 'fsdp'))
- output_weight_gradient: float32 [768, 768], P(('dp', 'fsdp'))
- output_bias_gradient: float32 [768], P(('dp', 'fsdp'))
- first_gain_gradient: float32 [768], P(('dp', 'fsdp'))
- first_shift_gradient: float32 [768], P(('dp', 'fsdp'))
- second_gain_gradient: float32 [768], P(('dp', 'fsdp'))
- second_shift_gradient: float32 [768], P(('dp', 'fsdp'))
- upward_weight_gradient: float32 [768, 3072], P(('dp', 'fsdp'))
- upward_bias_gradient: float32 [3072], P(('dp', 'fsdp'))
- downward_weight_gradient: float32 [3072, 768], P(('dp', 'fsdp'))
- downward_bias_gradient: float32 [768], P(('dp', 'fsdp'))
- depth_gradient: float32 [5], replicated
The draws below stay inside these ranges and needn't reach their ends.
Inputs may be any that keep to these rules, and one draw needn't show every extreme that they name: `lengths`: each row's real tokens fill a prefix of it; some row has exactly 1024 and some row exactly 128.
All inputs are finite; a program needn't handle non-finite values.
Results may differ from the reference program's by a relative error of at most 0.012.
Values may be sent and summed in bfloat16 or wider, within the bound.
A program may use at most 256 MiB of HBM per device.

```python
import math
import jax
import jax.numpy as jnp
from jax import lax

D = 768
HEADS = 12
HEAD_DIM = 64
FF = 3072
SEQ = 1024
HIST = 4
ROWS = 32


def draw_lengths(key, part):
    key = jax.random.fold_in(key, 11)
    row_index = jnp.arange(ROWS, dtype=jnp.int32)
    quarter = SEQ // 4
    eighth = SEQ // 8
    base_len = quarter + (SEQ - quarter) * row_index // max(ROWS - 1, 1)
    floor_len = jnp.maximum(base_len - eighth, eighth)
    raw_bits = jax.random.randint(key, (ROWS,), 0, 1 << 20, dtype=jnp.int32)
    drawn_len = floor_len + raw_bits % (base_len - floor_len + 1)
    drawn_len = jnp.where(row_index == 0, eighth, drawn_len)
    return jnp.where(row_index == ROWS - 1, SEQ, drawn_len).astype(jnp.int32)


def shard_levels(rng, extent, cuts, least, high):
    level, own = 1.0, jax.random.fold_in(rng, 6)
    for axis_at, parts in cuts:
        heights = jnp.exp(jax.random.uniform(jax.random.fold_in(own, axis_at), (parts,), jnp.float32, least / len(cuts), high / len(cuts)))
        level = level * jnp.repeat(heights, extent[axis_at] // parts).reshape([-1 if axis == axis_at else 1 for axis in range(len(extent))])
    return level


def gaussian(stream_key, extent, scale, limit, cuts=(), kind=jnp.bfloat16):
    loudness = shard_levels(stream_key, extent, cuts, -0.22, 0.18) if cuts else 1.0
    values = jax.random.normal(stream_key, extent, jnp.float32) * scale * loudness
    return jnp.minimum(jnp.maximum(values, -limit), limit).astype(kind)


def setup_inputs(seed: int = 0) -> dict:
    keys = jax.random.split(jax.random.key(seed), 18)
    inputs = gaussian(keys[0], (ROWS, SEQ, D), 1.0, 6.0, ((0, 32),))
    history = gaussian(keys[1], (HIST, ROWS, SEQ, D), 1.0, 6.0, ((1, 32),))
    cotangent = gaussian(keys[2], (ROWS, SEQ, D), 1.0, 6.0, ((0, 32),))
    lengths = draw_lengths(jax.random.fold_in(keys[17], 71), 0)
    joint_weight = gaussian(keys[4], (D, 3 * D), D ** -0.5, 0.21875, ((0, 32),))
    joint_bias = gaussian(keys[5], (3 * D,), 0.3, 1.5, ((0, 32),))
    output_weight = gaussian(keys[6], (D, D), (D // 16) ** -0.5, 0.875, ((0, 32),))
    output_bias = gaussian(keys[7], (D,), 0.3, 1.5, ((0, 32),))
    first_gain = jnp.clip(1.0 + 0.1 * jax.random.normal(keys[8], (D,), jnp.float32), 0.5, 1.5).astype(jnp.bfloat16)
    first_shift = gaussian(keys[9], (D,), 0.3, 1.5, ((0, 32),))
    second_gain = jnp.clip(1.0 + 0.1 * jax.random.normal(keys[10], (D,), jnp.float32), 0.5, 1.5).astype(jnp.bfloat16)
    second_shift = gaussian(keys[11], (D,), 0.3, 1.5, ((0, 32),))
    upward_weight = gaussian(keys[12], (D, FF), D ** -0.5, 0.21875, ((0, 32),))
    upward_bias = gaussian(keys[13], (FF,), 0.3, 1.5, ((0, 32),))
    downward_weight = gaussian(keys[14], (FF, D), FF ** -0.5, 0.109375, ((0, 32),))
    downward_bias = gaussian(keys[15], (D,), 0.3, 1.5, ((0, 32),))
    depth_weights = jnp.clip(jax.random.uniform(keys[16], (HIST + 1,), jnp.float32, 0.3, 1.0), 0.3, 1.0)
    return {"inputs": inputs, "history": history, "cotangent": cotangent, "lengths": lengths, "joint_weight": joint_weight, "joint_bias": joint_bias, "output_weight": output_weight, "output_bias": output_bias, "first_gain": first_gain, "first_shift": first_shift, "second_gain": second_gain, "second_shift": second_shift, "upward_weight": upward_weight, "upward_bias": upward_bias, "downward_weight": downward_weight, "downward_bias": downward_bias, "depth_weights": depth_weights}


@jax.custom_vjp
def low(v):
    return lax.optimization_barrier(v.astype(jnp.bfloat16)).astype(jnp.float32)

@jax.custom_vjp
def low_back(v):
    return v

def low_keep(v):
    return (low(v), None)

def low_pass(kept, grad):
    return (grad,)

def back_keep(v):
    return (v, None)

def back_low(kept, grad):
    return (low(grad),)
low.defvjp(low_keep, low_pass)
low_back.defvjp(back_keep, back_low)
epsilon = 1e-05
highest = lax.Precision.HIGHEST

def layer_norm(values, gain, shift):
    row_mean = lax.optimization_barrier(jnp.mean(values, axis=-1, keepdims=True))
    centred = values - row_mean
    variance = lax.optimization_barrier(jnp.mean(centred * centred, axis=-1, keepdims=True))
    return centred * lax.rsqrt(variance + epsilon) * gain + shift

def rotary_tables():
    half_dim = HEAD_DIM // 2
    exponent = jnp.arange(half_dim, dtype=jnp.float32) * (-2.0 / HEAD_DIM)
    frequency = jnp.power(10000.0, exponent)
    angles = jnp.arange(SEQ, dtype=jnp.float32)[:, None] * frequency[None, :]
    return (jnp.cos(angles)[:, None, :], jnp.sin(angles)[:, None, :])

def rotate(values, cosine, sine):
    half_dim = values.shape[-1] // 2
    first = values[..., :half_dim]
    second = values[..., half_dim:]
    return jnp.concatenate([first * cosine - second * sine, second * cosine + first * sine], axis=-1)

def forward_group(inputs, history, depth, params, lengths):
    joint_weight, joint_bias, output_weight, output_bias, first_gain, first_shift, second_gain, second_shift, upward_weight, upward_bias, downward_weight, downward_bias = params
    group = inputs.shape[0]
    normed = low(layer_norm(inputs, first_gain, first_shift))
    joined = low_back(jnp.einsum('rtd,de->rte', normed, joint_weight, precision=highest) + joint_bias)
    split = joined.reshape(group, SEQ, 3, HEADS, HEAD_DIM)
    cosine, sine = rotary_tables()
    queries = low(rotate(split[:, :, 0], cosine, sine))
    keys_turned = low(rotate(split[:, :, 1], cosine, sine))
    values = low(split[:, :, 2])
    scores = low_back(jnp.einsum('rqhd,rkhd->rhqk', queries, keys_turned, precision=highest) * HEAD_DIM ** (-0.5))
    positions = jnp.arange(SEQ, dtype=jnp.int32)
    causal = positions[None, :] <= positions[:, None]
    present = positions[None, :] < lengths[:, None]
    allowed = causal[None, None, :, :] & present[:, None, None, :]
    scores = jnp.where(allowed, scores, -1e+30)
    row_top = lax.optimization_barrier(jnp.max(scores, axis=-1, keepdims=True))
    weights = jnp.exp(scores - row_top)
    probs = low(weights / lax.optimization_barrier(jnp.sum(weights, axis=-1, keepdims=True)))
    heads = low(low_back(jnp.einsum('rhqk,rkhd->rqhd', probs, values, precision=highest)))
    heads = heads.reshape(group, SEQ, D)
    attended = low_back(jnp.einsum('rtd,de->rte', heads, output_weight, precision=highest) + output_bias)
    middle = inputs + attended
    normed_two = low(layer_norm(middle, second_gain, second_shift))
    upward = low_back(jnp.einsum('rtd,df->rtf', normed_two, upward_weight, precision=highest) + upward_bias)
    hidden = low(jax.nn.gelu(upward, approximate=True))
    block_out = middle + low_back(jnp.einsum('rtf,fd->rtd', hidden, downward_weight, precision=highest) + downward_bias)
    earlier = lax.optimization_barrier(jnp.sum(depth[:HIST, None, None, None] * history, axis=0))
    return earlier + depth[HIST] * block_out

def reference(inputs, history, cotangent, lengths, joint_weight, joint_bias, output_weight, output_bias, first_gain, first_shift, second_gain, second_shift, upward_weight, upward_bias, downward_weight, downward_bias, depth_weights):
    params = tuple((param.astype(jnp.float32) for param in (joint_weight, joint_bias, output_weight, output_bias, first_gain, first_shift, second_gain, second_shift, upward_weight, upward_bias, downward_weight, downward_bias)))
    depth = depth_weights.astype(jnp.float32)
    count = jnp.sum(lengths).astype(jnp.float32)
    factor = ROWS * SEQ / count
    group = math.gcd(ROWS, 2)
    blocks = ROWS // group
    positions = jnp.arange(SEQ, dtype=jnp.int32)
    block_inputs = inputs.reshape(blocks, group, SEQ, D)
    block_history = jnp.swapaxes(history.reshape(HIST, blocks, group, SEQ, D), 0, 1)
    block_cotangent = cotangent.reshape(blocks, group, SEQ, D)
    block_lengths = lengths.reshape(blocks, group)

    def one_group(carry, pieces):
        part_inputs, part_history, part_cotangent, part_lengths = pieces
        real_mask = (positions[None, :] < part_lengths[:, None]).astype(jnp.float32)
        seed_grad = part_cotangent.astype(jnp.float32) * real_mask[:, :, None] * factor

        def forward(inputs_f, history_f, depth_f, params_f):
            return forward_group(inputs_f, history_f, depth_f, params_f, part_lengths)
        result, pullback = jax.vjp(forward, part_inputs.astype(jnp.float32), part_history.astype(jnp.float32), depth, params)
        inputs_grad, history_grad, depth_grad, params_grad = pullback(seed_grad)
        carry = jax.tree.map(jnp.add, carry, (depth_grad, params_grad))
        return (carry, (result.astype(jnp.bfloat16), inputs_grad, history_grad))
    initial = (jnp.zeros_like(depth), tuple((jnp.zeros_like(param) for param in params)))
    (depth_total, grads), (outputs, input_grads, history_grads) = lax.scan(one_group, initial, (block_inputs, block_history, block_cotangent, block_lengths))
    layer_output = outputs.reshape(ROWS, SEQ, D)
    input_gradient = input_grads.reshape(ROWS, SEQ, D)
    history_gradient = jnp.swapaxes(history_grads, 0, 1).reshape(HIST, ROWS, SEQ, D)
    return (layer_output, input_gradient, history_gradient, grads[0], grads[1], grads[2], grads[3], grads[4], grads[5], grads[6], grads[7], grads[8], grads[9], grads[10], grads[11], depth_total)
```

```python
import functools
import math

import jax
import jax.numpy as jnp
import numpy as np
from jax import lax
from jax.experimental import pallas as pl
from jax.experimental.pallas import tpu as pltpu
from jax.sharding import PartitionSpec as P

D = 768
HEADS = 12
HEAD_DIM = 64
FF = 3072
SEQ = 1024
HIST = 4
AXES = ("dp", "fsdp")
EPS = 1e-05
NEG = -1e30
LIFT = 80
QB = 256
C0 = math.sqrt(2.0 / math.pi)
C1 = 0.044715

f32 = jnp.float32
bf16 = jnp.bfloat16
ANY = pl.BlockSpec(memory_space=pl.ANY)
VM = pl.BlockSpec(memory_space=pltpu.VMEM)
SM = pl.BlockSpec(memory_space=pltpu.SMEM)

JOINT_BIAS, OUTPUT_BIAS, GAIN_1, SHIFT_1, GAIN_2, SHIFT_2, UP_BIAS, DOWN_BIAS = range(8)


def dot(left, right, left_dim=1, right_dim=0):
    return lax.dot_general(
        left, right, (((left_dim,), (right_dim,)), ((), ())), preferred_element_type=f32
    )


def at(start, size, unit=128):
    return pl.ds(pl.multiple_of(start, unit), size)


def normalize(values):
    mean = jnp.mean(values, axis=-1, keepdims=True)
    centred = values - mean
    variance = jnp.mean(centred * centred, axis=-1, keepdims=True)
    scale = lax.rsqrt(variance + EPS)
    return centred * scale, scale


def fold(values):
    rows, cols = values.shape
    return jnp.sum(values.reshape(rows // 8, 8, cols), axis=0)


def split_three(row):
    high = row.astype(bf16).astype(f32)
    rest = row - high
    mid = rest.astype(bf16).astype(f32)
    return high, mid, rest - mid


def tail(rows, width):
    index = lax.broadcasted_iota(jnp.int32, (16, width), 0)
    out = jnp.zeros((16, width), f32)
    for place, row in enumerate(rows):
        out = jnp.where(index == place, row, out)
    return out.astype(bf16)


def forward_kernel(
    length_ref,
    depth_ref,
    x_ref,
    cot_ref,
    vec_ref,
    cos_ref,
    sin_ref,
    hist_hbm,
    wj_hbm,
    wo_hbm,
    wu_hbm,
    wd_hbm,
    layer_hbm,
    normed_hbm,
    q_hbm,
    k_hbm,
    v_hbm,
    heads_hbm,
    middle_hbm,
    n2_hbm,
    hidden_hbm,
    slope_hbm,
    depth_out,
    wj,
    wo,
    wu,
    wd,
    hist,
    earlier,
    normed,
    q,
    k,
    v,
    heads,
    middle,
    n2,
    hidden,
    slope,
    layer,
    depth_acc,
    load_sem,
    hist_sem,
    save_sem,
):
    loads = [
        pltpu.make_async_copy(src, dst, load_sem.at[i])
        for i, (src, dst) in enumerate(((wj_hbm, wj), (wo_hbm, wo), (wu_hbm, wu), (wd_hbm, wd)))
    ]
    hb = 128

    def hist_copy(step, slot):
        return pltpu.make_async_copy(
            hist_hbm.at[:, 0, pl.ds(step * hb, hb)], hist.at[slot], hist_sem.at[slot]
        )

    hist_copy(0, 0).start()
    hist_copy(1, 1).start()
    for load in loads:
        load.start()
    length = length_ref[0]
    factor = vec_ref[8:9, :D]

    depth_acc[...] = jnp.zeros_like(depth_acc)
    for step in range(SEQ // hb):
        slot = step % 2
        hist_copy(step, slot).wait()

        def part(i, carry, slot=slot, step=step):
            rows = pl.ds(pl.multiple_of(i * 32, 32), 32)
            here = pl.ds(pl.multiple_of(step * hb + i * 32, 32), 32)
            index = lax.broadcasted_iota(jnp.int32, (32, 1), 0) + (step * hb + i * 32)
            seed = jnp.where(index < length, cot_ref[here, :].astype(f32), 0.0)
            total = jnp.zeros((32, D), f32)
            for j in range(HIST):
                part_hist = hist[slot, j, rows, :].astype(f32)
                total = total + depth_ref[j] * part_hist
                depth_acc[j] = depth_acc[j] + fold(seed * part_hist)
            earlier[here, :] = total
            return carry

        lax.fori_loop(0, hb // 32, part, 0)
        if step + 2 < SEQ // hb:
            hist_copy(step + 2, slot).start()

    for i in range(SEQ // 128):
        rows = slice(i * 128, (i + 1) * 128)
        unit, _ = normalize(x_ref[rows, :].astype(f32))
        full = unit * vec_ref[GAIN_1 : GAIN_1 + 1, :D] + vec_ref[SHIFT_1 : SHIFT_1 + 1, :D]
        normed[:, rows] = full.T.astype(bf16)
    saves = []

    def save(src, dst):
        copy = pltpu.make_async_copy(src, dst, save_sem.at[len(saves)])
        copy.start()
        saves.append(copy)

    save(normed, normed_hbm)

    loads[0].wait()
    keys_at = lax.broadcasted_iota(jnp.int32, (1, SEQ), 1)
    key_bias = jnp.where(keys_at < length, 0.0, NEG)
    one = jnp.ones((1, SEQ), f32)
    bias_cols = vec_ref[0:8, : 3 * D].T

    for part, (target, rows) in enumerate(
        ((q, (one,)), (k, (key_bias, one, one, one)), (v, (one, one, one)))
    ):
        extra = tail(rows, SEQ)
        for chunk in range(3):
            first = part * D + chunk * 256
            joined = dot(wj[:, first : first + 256], normed[...], 0, 0)
            joined = joined + bias_cols[first : first + 256, 0:1]
            for h in range(4):
                upper = joined[h * 64 : h * 64 + 32]
                lower = joined[h * 64 + 32 : h * 64 + 64]
                if part < 2:
                    cosine, sine = cos_ref[...], sin_ref[...]
                    upper, lower = upper * cosine - lower * sine, lower * cosine + upper * sine
                both = jnp.concatenate([upper, lower], axis=0).astype(bf16)
                if part == 0:
                    both = both * jnp.asarray(0.125, bf16)
                target[chunk * 4 + h, 0:64, :] = both
                target[chunk * 4 + h, 64:80, :] = extra
    save(k, k_hbm)
    save(v, v_hbm)

    diagonal = lax.broadcasted_iota(jnp.int32, (QB, QB), 0) <= lax.broadcasted_iota(
        jnp.int32, (QB, QB), 1
    )

    def one_head(h, carry):
        keys = k[h].T
        for i in range(SEQ // QB):
            cols = slice(i * QB, (i + 1) * QB)
            seen = (i + 1) * QB
            scores = dot(keys[:seen], q[h, :, cols])
            last = jnp.where(diagonal, scores[seen - QB :], NEG)
            scores = jnp.concatenate([scores[: seen - QB], last], axis=0) if i else last
            top = jnp.max(scores, axis=0, keepdims=True)
            weights = jnp.exp(scores - top).astype(bf16)
            out = dot(v[h, :, :seen], weights)
            total = out[64:65]
            heads[at(h * 64, 64, 64), cols] = (out[:64] / total).astype(bf16)
            log_total = -(top + jnp.log(total))
            q[h, 64:80, cols] = tail((jnp.ones((1, QB), f32), *split_three(log_total)), QB)
        return carry

    lax.fori_loop(0, HEADS, one_head, 0)
    save(q, q_hbm)
    save(heads, heads_hbm)

    loads[1].wait()

    def project(i, carry):
        rows = at(i * 256, 256)
        out = dot(heads[:, rows], wo[...], 0, 0)
        mid = x_ref[rows, :].astype(f32) + (out + vec_ref[OUTPUT_BIAS : OUTPUT_BIAS + 1, :D])
        middle[rows, :] = mid
        unit, _ = normalize(mid)
        n2[rows, :] = (
            unit * vec_ref[GAIN_2 : GAIN_2 + 1, :D] + vec_ref[SHIFT_2 : SHIFT_2 + 1, :D]
        ).astype(bf16)
        return carry

    lax.fori_loop(0, SEQ // 256, project, 0)
    save(middle, middle_hbm)
    save(n2, n2_hbm)

    loads[2].wait()

    def upward(i, carry):
        rows = at((i // 6) * 512, 512)
        cols = at((i % 6) * 512, 512)
        up = dot(n2[rows, :], wu[:, cols]) + vec_ref[UP_BIAS : UP_BIAS + 1, cols]
        square = up * up
        turn = jnp.tanh(up * (C0 + (C0 * C1) * square))
        half = 0.5 + 0.5 * turn
        hidden[rows, cols] = (up * half).astype(bf16)
        bent = (2.0 * up) * (C0 + (3.0 * C0 * C1) * square)
        slope[rows, cols] = (half + bent * (half * (1.0 - half))).astype(bf16)
        return carry

    lax.fori_loop(0, 12, upward, 0)
    save(hidden, hidden_hbm)
    save(slope, slope_hbm)

    loads[3].wait()

    def downward(i, carry):
        rows = at(i * 256, 256)
        out = dot(hidden[rows, :], wd[...])
        block = middle[rows, :] + (out + vec_ref[DOWN_BIAS : DOWN_BIAS + 1, :D])
        layer[rows, :] = (earlier[rows, :] + depth_ref[HIST] * block).astype(bf16)
        index = lax.broadcasted_iota(jnp.int32, (256, 1), 0) + i * 256
        seed = jnp.where(index < length, cot_ref[rows, :].astype(f32), 0.0)
        depth_acc[HIST] = depth_acc[HIST] + fold(seed * block)
        return carry

    lax.fori_loop(0, SEQ // 256, downward, 0)
    save(layer, layer_hbm)
    for j in range(HIST + 1):
        depth_out[j : j + 1, :] = jnp.sum(depth_acc[j], axis=0, keepdims=True) * factor
    for copy in saves:
        copy.wait()


def forward(length, depth, x, cot, vec, cosine, sine, history, wj, wo, wu, wd):
    sds = jax.ShapeDtypeStruct
    saved = [
        sds((SEQ, D), bf16),
        sds((D, SEQ), bf16),
        sds((HEADS, LIFT, SEQ), bf16),
        sds((HEADS, LIFT, SEQ), bf16),
        sds((HEADS, LIFT, SEQ), bf16),
        sds((D, SEQ), bf16),
        sds((SEQ, D), f32),
        sds((SEQ, D), bf16),
        sds((SEQ, FF), bf16),
        sds((SEQ, FF), bf16),
    ]
    return pl.pallas_call(
        forward_kernel,
        name="forward_block",
        out_shape=[*saved, sds((8, D), f32)],
        in_specs=[SM, SM, VM, VM, VM, VM, VM] + [ANY] * 5,
        out_specs=[ANY] * len(saved) + [VM],
        scratch_shapes=[
            pltpu.VMEM((D, 3 * D), bf16),
            pltpu.VMEM((D, D), bf16),
            pltpu.VMEM((D, FF), bf16),
            pltpu.VMEM((FF, D), bf16),
            pltpu.VMEM((2, HIST, 128, D), bf16),
            pltpu.VMEM((SEQ, D), f32),
            *(pltpu.VMEM(s.shape, s.dtype) for s in saved[1:]),
            pltpu.VMEM((SEQ, D), bf16),
            pltpu.VMEM((HIST + 1, 8, D), f32),
            pltpu.SemaphoreType.DMA((4,)),
            pltpu.SemaphoreType.DMA((2,)),
            pltpu.SemaphoreType.DMA((16,)),
        ],
        compiler_params=pltpu.CompilerParams(vmem_limit_bytes=60 << 20),
    )(length, depth, x, cot, vec, cosine, sine, history, wj, wo, wu, wd)


def backward_kernel(
    length_ref,
    depth_ref,
    x_ref,
    cot_ref,
    vec_ref,
    cos_ref,
    sin_ref,
    normed_hbm,
    q_hbm,
    k_hbm,
    v_hbm,
    heads_hbm,
    middle_hbm,
    n2_hbm,
    hidden_hbm,
    slope_hbm,
    wj_hbm,
    wo_hbm,
    wu_hbm,
    wd_hbm,
    input_grad_hbm,
    gj_hbm,
    go_hbm,
    gu_hbm,
    gd_hbm,
    vec_out,
    wj,
    wo,
    wu,
    wd,
    normed,
    q,
    k,
    v,
    heads,
    middle,
    n2,
    hidden,
    slope,
    low,
    joined,
    grad,
    stage,
    load_sem,
    stage_sem,
    save_sem,
):
    names = (hidden, wd, slope, n2, wu, middle, heads, wo, k, q, v, normed, wj)
    sources = (hidden_hbm, wd_hbm, slope_hbm, n2_hbm, wu_hbm, middle_hbm, heads_hbm, wo_hbm)
    sources = sources + (k_hbm, q_hbm, v_hbm, normed_hbm, wj_hbm)
    loads = {
        id(dst): pltpu.make_async_copy(src, dst, load_sem.at[i])
        for i, (src, dst) in enumerate(zip(sources, names))
    }

    def begin(*targets):
        for dst in targets:
            loads[id(dst)].start()

    def ready(*targets):
        for dst in targets:
            loads[id(dst)].wait()

    begin(hidden, wd, slope, n2, wu, middle, heads, wo, k, q, v, normed, wj)
    length = length_ref[0]
    factor = vec_ref[8:9, :D]
    vec_out[...] = jnp.zeros_like(vec_out)

    def seed_of(rows, start, count):
        index = lax.broadcasted_iota(jnp.int32, (count, 1), 0) + start
        return jnp.where(index < length, cot_ref[rows, :].astype(f32), 0.0) * factor

    for i in range(SEQ // 128):
        rows = slice(i * 128, (i + 1) * 128)
        top = (depth_ref[HIST] * seed_of(rows, i * 128, 128)).astype(bf16)
        low[rows, :] = top
        vec_out[DOWN_BIAS : DOWN_BIAS + 1, :D] += jnp.sum(top.astype(f32), axis=0, keepdims=True)

    waiting = {}
    count = [0]

    def put(value, target):
        slot = count[0] % 2
        count[0] += 1
        if slot in waiting:
            waiting.pop(slot).wait()
        stage[slot] = value
        copy = pltpu.make_async_copy(stage.at[slot], target, stage_sem.at[slot])
        copy.start()
        waiting[slot] = copy

    ready(hidden)
    for n in range(4):
        put(dot(hidden[:, n * D : (n + 1) * D], low[...], 0, 0), gd_hbm.at[pl.ds(n * D, D)])

    ready(wd, slope)

    def up_low(i, carry):
        cols = at((i % 6) * 512, 512)
        rows = at((i // 6) * 512, 512)
        back = dot(low[rows, :], wd[cols, :], 1, 1)
        out = (back * slope[rows, cols].astype(f32)).astype(bf16)
        slope[rows, cols] = out
        vec_out[UP_BIAS : UP_BIAS + 1, cols] += jnp.sum(out.astype(f32), axis=0, keepdims=True)
        return carry

    lax.fori_loop(0, 12, up_low, 0)

    ready(n2)
    for n in range(4):
        put(dot(n2[...], slope[:, n * D : (n + 1) * D], 0, 0), gu_hbm.at[:, pl.ds(n * D, D)])

    ready(wu, middle)

    def second_norm(i, carry):
        rows = at(i * 256, 256)
        back = dot(slope[rows, :], wu[...], 1, 1)
        unit, scale = normalize(middle[rows, :])
        vec_out[GAIN_2 : GAIN_2 + 1, :D] += jnp.sum(back * unit, axis=0, keepdims=True)
        vec_out[SHIFT_2 : SHIFT_2 + 1, :D] += jnp.sum(back, axis=0, keepdims=True)
        back = back * vec_ref[GAIN_2 : GAIN_2 + 1, :D]
        along = jnp.mean(back * unit, axis=-1, keepdims=True)
        across = jnp.mean(back, axis=-1, keepdims=True)
        top = depth_ref[HIST] * seed_of(rows, i * 256, 256)
        out = top + scale * (back - across - unit * along)
        middle[rows, :] = out
        out_low = out.astype(bf16)
        low[rows, :] = out_low
        vec_out[OUTPUT_BIAS : OUTPUT_BIAS + 1, :D] += jnp.sum(
            out_low.astype(f32), axis=0, keepdims=True
        )
        return carry

    lax.fori_loop(0, SEQ // 256, second_norm, 0)

    ready(heads, wo)
    put(dot(heads[...], low[...]), go_hbm)

    one = jnp.ones((1, SEQ), f32)

    def heads_back(i, carry):
        rows = at(i * 256, 256)
        back = dot(wo[rows, :], low[...], 1, 1).astype(bf16)
        grad[at(i * 4, 4, 4), 0:64, :] = back.reshape(4, 64, SEQ)
        product = back.astype(f32) * heads[rows, :].astype(f32)
        for h in range(4):
            total = jnp.sum(product[h * 64 : (h + 1) * 64], axis=0, keepdims=True)
            grad[i * 4 + h, 64:80, :] = tail(split_three(-total), SEQ)
        return carry

    lax.fori_loop(0, 3, heads_back, 0)

    ready(k, q, v)
    diagonal = lax.broadcasted_iota(jnp.int32, (QB, QB), 0) <= lax.broadcasted_iota(
        jnp.int32, (QB, QB), 1
    )

    def turn_back(value):
        upper, lower = value[:32], value[32:]
        cosine, sine = cos_ref[...], sin_ref[...]
        return jnp.concatenate(
            [upper * cosine + lower * sine, lower * cosine - upper * sine], axis=0
        ).astype(bf16)

    def one_head(h, carry):
        keys = k[h].T
        values = v[h].T
        rows = at(h * 64, 64, 64)
        query_grad = jnp.zeros((64, SEQ), f32)
        key_grads = []
        for j in range(SEQ // QB):
            here = slice(j * QB, (j + 1) * QB)
            scores = dot(keys[here], q[h, :, j * QB :])
            probs = jnp.exp(scores)
            front = jnp.where(diagonal, probs[:, :QB], 0.0)
            probs = jnp.concatenate([front, probs[:, QB:]], axis=1) if j < 3 else front
            probs_grad = dot(values[here], grad[h, :, j * QB :])
            scores_low = (probs * probs_grad).astype(bf16)
            joined[2, rows, here] = dot(grad[h, 0:64, j * QB :], probs.astype(bf16), 1, 1).astype(
                bf16
            )
            key_grads.append(dot(q[h, 0:64, j * QB :], scores_low, 1, 1))
            step = dot(k[h, 0:64, here], scores_low)
            if j:
                step = jnp.concatenate([jnp.zeros((64, j * QB), f32), step], axis=1)
            query_grad = query_grad + step
        joined[0, rows, :] = turn_back(query_grad * 0.125)
        joined[1, rows, :] = turn_back(jnp.concatenate(key_grads, axis=1))
        return carry

    lax.fori_loop(0, HEADS, one_head, 0)

    ready(normed)
    for part in range(3):
        put(dot(normed[...], joined[part, 0:D, :], 1, 1), gj_hbm.at[:, pl.ds(part * D, D)])
        sums = jnp.sum(joined[part, 0:D, :].astype(f32), axis=1, keepdims=True)
        sums = jnp.broadcast_to(sums, (D, 8)).T
        vec_out[JOINT_BIAS : JOINT_BIAS + 1, part * D : (part + 1) * D] = sums[0:1]

    ready(wj)

    def first_norm(i, carry):
        rows = at(i * 256, 256)
        back = jnp.zeros((256, D), f32)
        for part in range(3):
            flat = joined[part, 0:D, rows].T
            back = back + dot(flat, wj[:, part * D : (part + 1) * D], 1, 1)
        unit, scale = normalize(x_ref[rows, :].astype(f32))
        vec_out[GAIN_1 : GAIN_1 + 1, :D] += jnp.sum(back * unit, axis=0, keepdims=True)
        vec_out[SHIFT_1 : SHIFT_1 + 1, :D] += jnp.sum(back, axis=0, keepdims=True)
        back = back * vec_ref[GAIN_1 : GAIN_1 + 1, :D]
        along = jnp.mean(back * unit, axis=-1, keepdims=True)
        across = jnp.mean(back, axis=-1, keepdims=True)
        middle[rows, :] = middle[rows, :] + scale * (back - across - unit * along)
        return carry

    lax.fori_loop(0, SEQ // 256, first_norm, 0)
    last = pltpu.make_async_copy(middle, input_grad_hbm, save_sem.at[0])
    last.start()
    last.wait()
    for copy in waiting.values():
        copy.wait()


def backward(length, depth, x, cot, vec, cosine, sine, saved, weights):
    sds = jax.ShapeDtypeStruct
    scratch = [(D, 3 * D), (D, D), (D, FF), (FF, D)]
    return pl.pallas_call(
        backward_kernel,
        name="backward_block",
        out_shape=[
            sds((SEQ, D), f32),
            sds((D, 3 * D), f32),
            sds((D, D), f32),
            sds((D, FF), f32),
            sds((FF, D), f32),
            sds((8, FF), f32),
        ],
        in_specs=[SM, SM, VM, VM, VM, VM, VM] + [ANY] * 13,
        out_specs=[ANY] * 5 + [VM],
        scratch_shapes=[
            *(pltpu.VMEM(s, bf16) for s in scratch),
            *(pltpu.VMEM(s.shape, s.dtype) for s in saved),
            pltpu.VMEM((SEQ, D), bf16),
            pltpu.VMEM((3, D, SEQ), bf16),
            pltpu.VMEM((HEADS, LIFT, SEQ), bf16),
            pltpu.VMEM((2, D, D), f32),
            pltpu.SemaphoreType.DMA((13,)),
            pltpu.SemaphoreType.DMA((2,)),
            pltpu.SemaphoreType.DMA((1,)),
        ],
        compiler_params=pltpu.CompilerParams(vmem_limit_bytes=62 << 20),
    )(length, depth, x, cot, vec, cosine, sine, *saved, *weights)


def turning_tables():
    half = HEAD_DIM // 2
    frequency = np.power(10000.0, np.arange(half, dtype=np.float64) * (-2.0 / HEAD_DIM))
    angles = frequency[:, None] * np.arange(SEQ, dtype=np.float64)[None, :]
    return np.cos(angles).astype(np.float32), np.sin(angles).astype(np.float32)


def local(
    inputs,
    history,
    cotangent,
    lengths,
    joint_weight,
    joint_bias,
    output_weight,
    output_bias,
    first_gain,
    first_shift,
    second_gain,
    second_shift,
    upward_weight,
    upward_bias,
    downward_weight,
    downward_bias,
    depth_weights,
):
    devices = lax.axis_size(AXES)
    vectors = (
        joint_bias,
        output_bias,
        first_gain,
        first_shift,
        second_gain,
        second_shift,
        upward_bias,
        downward_bias,
    )
    sizes = [vector.shape[0] for vector in vectors]
    piece = jnp.concatenate([v.astype(f32) for v in (*vectors, lengths)])
    pieces = lax.all_gather(piece, AXES, axis=0, tiled=False).reshape(devices, -1)
    rows, start = [], 0
    for size in sizes:
        row = pieces[:, start : start + size].reshape(1, -1)
        rows.append(jnp.pad(row, ((0, 0), (0, FF - row.shape[1]))))
        start += size
    count = jnp.sum(pieces[:, start:])
    factor = devices * SEQ / count
    vec = jnp.concatenate([*rows, jnp.full((8, FF), factor, f32)])
    shards = (joint_weight, output_weight, upward_weight, downward_weight)
    flat = jnp.concatenate([w.reshape(-1, 768) for w in shards])
    full = lax.all_gather(flat, AXES, axis=0, tiled=False).reshape(devices, -1, 768)
    weights, start = [], 0
    for w in shards:
        size = w.shape[0] * w.shape[1] // 768
        weights.append(full[:, start : start + size].reshape(-1, w.shape[1]))
        start += size
    cosine, sine = turning_tables()
    x, cot = inputs[0], cotangent[0]
    layer, *saved, depth_rows = forward(
        lengths, depth_weights, x, cot, vec, cosine, sine, history, *weights
    )
    input_grad, gj, go, gu, gd, vec_grads = backward(
        lengths, depth_weights, x, cot, vec, cosine, sine, saved, weights
    )
    positions = jnp.arange(SEQ, dtype=jnp.int32)
    seed = jnp.where(positions[:, None] < lengths[0], cot.astype(f32), 0.0) * factor
    history_gradient = depth_weights[:HIST, None, None, None] * seed[None, None]
    depth_terms = jnp.sum(depth_rows[: HIST + 1], axis=1)
    flat = jnp.concatenate(
        [g.astype(bf16).reshape(devices, -1, 768) for g in (gj, go, gu, gd)], axis=1
    )
    summed = lax.psum_scatter(flat, AXES, scatter_dimension=0, tiled=False).astype(f32)
    grads, start = [], 0
    for w in shards:
        size = w.shape[0] * w.shape[1] // 768
        grads.append(summed[start : start + size].reshape(w.shape))
        start += size
    vec_cols = [
        vec_grads[i, : size * devices].reshape(devices, size) for i, size in enumerate(sizes)
    ]
    vec_cols.append(jnp.broadcast_to(depth_terms[None], (devices, HIST + 1)))
    vec_sum = lax.psum_scatter(
        jnp.concatenate(vec_cols, axis=1), AXES, scatter_dimension=0, tiled=False
    )
    outs, start = [], 0
    for size in [*sizes, HIST + 1]:
        outs.append(vec_sum[start : start + size])
        start += size
    return (
        layer[None],
        input_grad[None],
        history_gradient,
        grads[0],
        outs[0],
        grads[1],
        outs[1],
        outs[2],
        outs[3],
        outs[4],
        outs[5],
        grads[2],
        outs[6],
        grads[3],
        outs[7],
        outs[8],
    )


def solution(mesh):
    row, vector = P(AXES, None), P(AXES)
    tokens, levels = P(AXES, None, None), P(None, AXES, None, None)
    return jax.shard_map(
        local,
        mesh=mesh,
        in_specs=(
            *(tokens, levels, tokens, vector),
            *(row, vector, row, vector),
            *(vector, vector, vector, vector),
            *(row, vector, row, vector, P()),
        ),
        out_specs=(
            *(tokens, tokens, levels),
            *(row, vector, row, vector),
            *(vector, vector, vector, vector),
            *(row, vector, row, vector, P()),
        ),
        check_vma=False,
    )
```

```python
import functools
import math
import types

import jax
import jax.numpy as jnp
import numpy as np
from jax import lax
from jax.experimental import pallas as pl
from jax.experimental.pallas import tpu as pltpu
from jax.sharding import PartitionSpec as P

D = 768
HEADS = 12
HEAD_DIM = 64
FF = 3072
SEQ = 1024
HIST = 4
AXES = ("dp", "fsdp")
EPS = 1e-05
NEG = -1e30
LIFT = 80
QB = 256
C0 = math.sqrt(2.0 / math.pi)
C1 = 0.044715

f32 = jnp.float32
bf16 = jnp.bfloat16
ANY = pl.BlockSpec(memory_space=pl.ANY)
VM = pl.BlockSpec(memory_space=pltpu.VMEM)
SM = pl.BlockSpec(memory_space=pltpu.SMEM)

MESH = pl.DeviceIdType.MESH
HALF = D // 2
PACK = D + HALF
PARTS = 8
CHUNKS = 12
SLOTS = 6
NEAR = 4

JOINT_BIAS, OUTPUT_BIAS, GAIN_1, SHIFT_1, GAIN_2, SHIFT_2, UP_BIAS, DOWN_BIAS = range(8)


def dot(left, right, left_dim=1, right_dim=0):
    return lax.dot_general(
        left, right, (((left_dim,), (right_dim,)), ((), ())), preferred_element_type=f32
    )


def at(start, size, unit=128):
    return pl.ds(pl.multiple_of(start, unit), size)


def normalize(values):
    mean = jnp.mean(values, axis=-1, keepdims=True)
    centred = values - mean
    variance = jnp.mean(centred * centred, axis=-1, keepdims=True)
    scale = lax.rsqrt(variance + EPS)
    return centred * scale, scale


def fold(values):
    rows, cols = values.shape
    return jnp.sum(values.reshape(rows // 8, 8, cols), axis=0)


def split_three(row):
    high = row.astype(bf16).astype(f32)
    rest = row - high
    mid = rest.astype(bf16).astype(f32)
    return high, mid, rest - mid


def tail(rows, width):
    index = lax.broadcasted_iota(jnp.int32, (16, width), 0)
    out = jnp.zeros((16, width), f32)
    for place, row in enumerate(rows):
        out = jnp.where(index == place, row, out)
    return out.astype(bf16)


def position():
    dp, fsdp = lax.axis_index("dp"), lax.axis_index("fsdp")
    return dp // 2, dp % 2, fsdp // 2, fsdp % 2


def device(x, c, z, y):
    return (x * 2 + c, z * 2 + y)


class Links:
    def __init__(self, send_sem, recv_sem, *rulers):
        x, c, z, y = position()
        self.send_sem, self.recv_sem = send_sem, recv_sem
        self.rulers = {jnp.dtype(ruler.dtype): ruler for ruler in rulers}
        self.x, self.c, self.z, self.y = x, c, z, y
        self.nx, self.nc, self.ny = 1 - x, 1 - c, 1 - y
        self.zs = (z + 1 - 2 * (z % 2), (z + 2) % 4, 3 - z)
        self.q, self.r = x * 2 + c, (1 - x) * 2 + c
        self.other_x = device(1 - x, c, z, y)
        self.other_y = device(x, c, z, 1 - y)
        self.other_c = device(x, 1 - c, z, y)
        self.along_z = [device(x, c, other, y) for other in self.zs]
        self.sent = {}

    def greet(self):
        barrier = pltpu.get_barrier_semaphore()
        peers = [self.other_x, self.other_y, self.other_c, *self.along_z]
        for peer in peers:
            pl.semaphore_signal(barrier, inc=1, device_id=peer, device_id_type=MESH)
        pl.semaphore_wait(barrier, len(peers))

    def copy(self, source, target, sem, peer):
        return pltpu.make_async_remote_copy(
            src_ref=source,
            dst_ref=target,
            send_sem=self.send_sem.at[sem],
            recv_sem=self.recv_sem.at[sem],
            device_id=peer,
            device_id_type=MESH,
        )

    def send(self, pairs, sem, peer):
        for source, target in pairs():
            self.copy(source, target, sem, peer).start()
        self.sent.setdefault(sem, []).append(pairs)

    def whole(self, refs, sem):
        size = sum(math.prod(ref.shape) for ref in refs)
        ruler = self.rulers[jnp.dtype(refs[0].dtype)]
        rows = 16
        while size % (rows * 128) or size // rows > ruler.shape[1]:
            rows += 16
        part = ruler.at[pl.ds(0, rows), pl.ds(0, size // rows)]
        return self.copy(part, part, sem, self.other_c)

    def arrived(self, targets, sem):
        self.whole(targets, sem).wait_recv()

    def left(self, sem):
        sources = [pair[0] for pairs in self.sent.pop(sem, []) for pair in pairs()]
        if sources:
            self.whole(sources, sem).wait_send()

    def finish(self):
        for sem in list(self.sent):
            self.left(sem)


DOWN = (PARTS, PARTS + 1)
VECTORS = PARTS + 2
WIDE = 512


class Gather:
    def __init__(self, links, parts, rests, down, pieces):
        self.links = links
        self.parts, self.rests, self.down, self.pieces = parts, rests, down, pieces

    def refs(self, item, q, y, z, color):
        if item == VECTORS:
            if color == 1:
                return []
            first = (q * 8 + y * 4 + (0 if z is None else z)) * 16
            return [self.pieces.at[at(first, 64 if z is None else 16, 16)]]
        rows = pl.ds(q * 4, 4) if z is None else q * 4 + z
        if item in DOWN:
            first, last = (0, WIDE) if item == PARTS else (WIDE, D)
            mid = (first + last) // 2
            first, last = {None: (first, last), 0: (first, mid), 1: (mid, last)}[color]
            return [self.down.at[rows, y, :, :, pl.ds(first, last - first)]]
        wide = {None: pl.ds(0, D), 0: pl.ds(0, HALF), 1: pl.ds(HALF, HALF)}[color]
        cut = 2 if item % 2 else 1
        narrow = {None: pl.ds(0, 3), 0: pl.ds(0, cut), 1: pl.ds(cut, 3 - cut)}[color]
        some = pl.ds(0, 4) if z is None else z
        return [
            self.parts.at[item, rows, 2 * y, :, wide],
            self.rests.at[item, q, y, narrow, some],
        ]

    def send(self, item, stage, peer, quads, z=None):
        def pairs():
            refs = []
            for q, y, color in quads:
                refs += self.refs(item, getattr(self.links, q), getattr(self.links, y), z, color)
            return [(ref, ref) for ref in refs]

        self.links.send(pairs, item * 4 + stage, peer)

    def start(self, item):
        links = self.links
        if item in DOWN:
            self.send(item, 0, links.other_x, [("q", "y", 0)], links.z)
            self.send(item, 0, links.other_y, [("q", "y", 1)], links.z)
            return
        for peer in links.along_z:
            self.send(item, 0, peer, [("q", "y", None)], links.z)

    def second(self, item):
        links = self.links
        if item in DOWN:
            refs = self.refs(item, links.r, links.y, links.z, 0)
            links.arrived(refs + self.refs(item, links.q, links.ny, links.z, 1), item * 4)
            quads = [("q", "y", 0), ("r", "y", 0), ("q", "y", 1), ("q", "ny", 1)]
            for peer in links.along_z:
                self.send(item, 1, peer, quads, links.z)
            return
        refs = [self.refs(item, links.q, links.y, z, None) for z in links.zs]
        links.arrived(sum(refs, []), item * 4)
        self.send(item, 1, links.other_x, [("q", "y", 0)])
        self.send(item, 1, links.other_y, [("q", "y", 1)])

    def third(self, item):
        links = self.links
        if item in DOWN:
            quads = [(links.q, links.y, 0), (links.r, links.y, 0)]
            quads += [(links.q, links.y, 1), (links.q, links.ny, 1)]
            refs = [self.refs(item, q, y, z, k) for q, y, k in quads for z in links.zs]
            links.arrived(sum(refs, []), item * 4 + 1)
        else:
            refs = self.refs(item, links.r, links.y, None, 0)
            links.arrived(refs + self.refs(item, links.q, links.ny, None, 1), item * 4 + 1)
        first = [("q", "y", 0), ("r", "y", 0)]
        second = [("q", "y", 1), ("q", "ny", 1)]
        self.send(item, 2, links.other_y, first)
        self.send(item, 2, links.other_x, second)
        self.send(item, 3, links.other_c, first + second)

    def fourth(self, item):
        links = self.links
        quads = [("q", "ny", 0), ("r", "ny", 0), ("r", "y", 1), ("r", "ny", 1)]
        refs = [self.refs(item, getattr(links, q), getattr(links, y), None, k) for q, y, k in quads]
        links.arrived(sum(refs, []), item * 4 + 2)
        self.send(item, 3, links.other_c, quads)

    def ready(self, item):
        links = self.links
        refs = []
        for xx in (0, 1):
            for yy in (0, 1):
                for color in (0, 1):
                    refs += self.refs(item, xx * 2 + links.nc, yy, None, color)
        links.arrived(refs, item * 4 + 3)
        if item < PARTS:

            def merge(p, carry):
                q, z = p // 4, p % 4
                for i in range(3):
                    even = self.rests[item, q, 0, i, z].astype(f32)
                    odd = self.rests[item, q, 1, i, z].astype(f32)
                    for k in (0, 1):
                        first = k * HALF + i * 128
                        half = slice(k * 8, k * 8 + 8)
                        self.parts[item, p, 1, :, first : first + 128] = jnp.concatenate(
                            [even[half], odd[half]], axis=0
                        ).astype(bf16)
                return carry

            lax.fori_loop(0, 16, merge, 0)

    def own(self, item, shard):
        links = self.links
        full = shard.astype(f32)
        even = links.y == 0
        main = jnp.where(even, full[0:16], full[8:24])
        rest = jnp.where(even, full[16:24], full[0:8])
        self.parts[item, links.q * 4 + links.z, 2 * links.y] = main.astype(bf16)
        for i in range(3):
            left, right = rest[:, i * 128 : (i + 1) * 128], rest[:, HALF + i * 128 :][:, :128]
            self.rests[item, links.q, links.y, i, links.z] = jnp.concatenate(
                [left, right], axis=0
            ).astype(bf16)


def block_order():
    index = lax.broadcasted_iota(jnp.int32, (32, 1), 0)
    return (index & 24) + (index & 3) * 2 + ((index >> 2) & 1)


def spread(maps_ref, size):
    row = {24: 0, 72: 2, 96: 4}[size]
    wide = 32 * size
    owner = maps_ref[row : row + 1, :wide] == block_order()
    lane = maps_ref[row + 1 : row + 2, :wide] == lax.broadcasted_iota(jnp.int32, (128, 1), 0)
    return owner, jnp.where(lane, 1.0, 0.0).astype(bf16)


VECTOR_SIZES = (72, 24, 24, 24, 24, 24, 96, 24)


def join_vectors(pieces_ref, maps_ref, vec_ref):
    for size in (24, 72, 96):
        owner, lane = spread(maps_ref, size)
        for row, own in enumerate(VECTOR_SIZES):
            if own == size:
                piece = pieces_ref[pl.ds(row, 32, stride=16), :].astype(bf16)
                full = jnp.where(owner, dot(piece, lane), 0.0)
                vec_ref[row : row + 1, : 32 * size] = jnp.sum(full, axis=0, keepdims=True)
    counts = pieces_ref[pl.ds(8, 32, stride=16), :]
    count = jnp.sum(jnp.sum(counts, axis=0, keepdims=True), axis=1, keepdims=True)
    vec_ref[8:16, :] = jnp.broadcast_to((32 * SEQ) / count, (8, FF))


def cut_vectors(vec_ref, maps_ref, pieces_ref):
    for size in (24, 72, 96):
        owner, lane = spread(maps_ref, size)
        for row, own in enumerate(VECTOR_SIZES):
            if own == size:
                full = jnp.where(owner, vec_ref[row : row + 1, : 32 * size], 0.0)
                high = full.astype(bf16)
                low = (full - high.astype(f32)).astype(bf16)
                pieces_ref[pl.ds(row, 32, stride=16), :] = dot(high, lane, 1, 1) + dot(
                    low, lane, 1, 1
                )


class Scatter:
    def __init__(self, links, base, credit, packed, near, one, two, three):
        self.links, self.base, self.credit = links, base, credit
        self.packed, self.near = packed, near
        self.one, self.two, self.three = one, two, three
        self.wide = packed.shape[3]

    def columns(self, chunk):
        mid = (self.wide + 1 - chunk % 2) // 2
        return pl.ds(0, mid), pl.ds(mid, self.wide - mid)

    def send(self, chunk, stage, peer, pairs, cols=None):
        if cols is None or cols.size:
            self.links.send(pairs, self.base + chunk * 4 + stage, peer)

    def start(self, chunk):
        links = self.links
        if self.credit is not None and chunk >= NEAR:
            pl.semaphore_wait(self.credit, 1)

        def pairs():
            return [
                (
                    self.packed.at[chunk % SLOTS, xx * 2 + links.nc],
                    self.near.at[chunk % NEAR, xx],
                )
                for xx in (0, 1)
            ]

        self.send(chunk, 0, links.other_c, pairs)

    def first(self, chunk):
        links = self.links
        slot, near = chunk % SLOTS, chunk % NEAR
        links.arrived([self.near.at[near, xx] for xx in (0, 1)], self.base + chunk * 4)

        def add(i, carry):
            xx, yy = i // 2, i % 2
            mine = self.packed[slot, xx * 2 + links.c, yy].astype(f32)
            self.packed[slot, xx * 2 + links.c, yy] = (
                mine + self.near[near, xx, yy].astype(f32)
            ).astype(self.packed.dtype)
            return carry

        lax.fori_loop(0, 4, add, 0)
        if self.credit is not None and chunk + NEAR < CHUNKS:
            pl.semaphore_signal(self.credit, inc=1, device_id=links.other_c, device_id_type=MESH)
        here, there = self.columns(chunk)

        def by_y():
            return [
                (self.packed.at[slot, k * 2 + links.c, links.ny, here], self.one.at[chunk, k, here])
                for k in (0, 1)
            ]

        def by_x():
            return [
                (self.packed.at[slot, links.r, k, there], self.one.at[chunk, k, there])
                for k in (0, 1)
            ]

        self.send(chunk, 1, links.other_y, by_y, here)
        self.send(chunk, 1, links.other_x, by_x, there)

    def second(self, chunk):
        links = self.links
        slot = chunk % SLOTS
        links.arrived([self.one.at[chunk, k] for k in (0, 1)], self.base + chunk * 4 + 1)
        here, there = self.columns(chunk)
        for k in (0, 1):
            for cols, q, y in ((here, k * 2 + links.c, links.y), (there, links.q, k)):
                if cols.size:
                    mine = self.packed[slot, q, y, cols].astype(f32)
                    self.one[chunk, k, cols] = (
                        mine + self.one[chunk, k, cols].astype(f32)
                    ).astype(self.one.dtype)
        self.send(
            chunk,
            2,
            links.other_x,
            lambda: [(self.one.at[chunk, links.nx, here], self.two.at[chunk, here])],
            here,
        )
        self.send(
            chunk,
            2,
            links.other_y,
            lambda: [(self.one.at[chunk, links.ny, there], self.two.at[chunk, there])],
            there,
        )

    def third(self, chunk):
        links = self.links
        links.arrived([self.two.at[chunk]], self.base + chunk * 4 + 2)
        for cols, mine in zip(self.columns(chunk), (links.x, links.y)):
            if cols.size:
                self.two[chunk, cols] = (
                    self.one[chunk, mine, cols].astype(f32) + self.two[chunk, cols].astype(f32)
                ).astype(self.two.dtype)
        for k in range(3):

            def pairs(k=k):
                return [(self.two.at[chunk, :, links.zs[k]], self.three.at[chunk, k])]

            self.send(chunk, 3, links.along_z[k], pairs)

    def total(self, chunk):
        links = self.links
        links.arrived([self.three.at[chunk, k] for k in range(3)], self.base + chunk * 4 + 3)
        parts = [self.two[chunk, :, links.z]] + [self.three[chunk, k] for k in range(3)]
        parts = [part.astype(f32) for part in parts]
        return (parts[0] + parts[1]) + (parts[2] + parts[3])

    def free(self, chunk):
        self.links.left(self.base + chunk * 4)
        self.links.left(self.base + chunk * 4 + 1)


def weight(parts_ref, item):
    return parts_ref[item].reshape(D, D)


def masked(cot_ref, rows, start, count, length):
    index = lax.broadcasted_iota(jnp.int32, (count, 1), 0) + start
    return jnp.where(index < length, cot_ref[rows, :].astype(f32), 0.0)


def causal():
    shape = (QB, QB)
    return lax.broadcasted_iota(jnp.int32, shape, 0) <= lax.broadcasted_iota(jnp.int32, shape, 1)


FORWARD_PLAN = {
    (0, 4): ((Gather.second, 10),),
    (0, 7): ((Gather.second, 8), (Gather.second, 9), (Gather.third, 10), (Gather.second, 0), (Gather.fourth, 10), (Gather.second, 1), (Gather.third, 0)),
    (1, 7): ((Gather.second, 2),),
    (2, 0, 0): ((Gather.third, 1), (Gather.second, 3), (Gather.fourth, 0), (Gather.third, 2), (Gather.second, 4)),
    (3, 0): ((Gather.fourth, 1), (Gather.second, 5)),
    (3, 1): ((Gather.third, 3),),
    (3, 2): ((Gather.second, 6), (Gather.fourth, 2)),
    (3, 3): ((Gather.third, 4),),
    (2, 1, 1): ((Gather.second, 7),),
    (2, 1, 2): ((Gather.third, 5),),
    (3, 5): ((Gather.fourth, 3),),
    (3, 6): ((Gather.third, 6),),
    (2, 2, 1): ((Gather.fourth, 4),),
    (3, 8): ((Gather.third, 7),),
    (3, 9): ((Gather.fourth, 5),),
    (3, 11): ((Gather.fourth, 6), (Gather.third, 8)),
    (5, 2): ((Gather.fourth, 7),),
    (6, 3): ((Gather.third, 9),),
    (6, 5): ((Gather.fourth, 8),),
    (6, 7): ((Gather.fourth, 9),),
}


def forward_steps(r, shared):
    length = r.length[0]
    hb = 128

    def hist_copy(step, slot):
        return pltpu.make_async_copy(
            r.history.at[:, 0, pl.ds(step * hb, hb)], r.hist.at[slot], r.hist_sem.at[slot]
        )

    hist_copy(0, 0).start()
    hist_copy(1, 1).start()
    if shared:
        links = Links(r.send_sem, r.recv_sem, r.hidden, r.earlier)
        gather = Gather(links, r.parts, r.rests, r.down, r.pieces)
        links.greet()
        place = (links.q * 8 + links.y * 4 + links.z) * 16
        r.pieces[at(place, 16, 16), :] = r.piece[...]
        gather.start(VECTORS)
        for part in range(3):
            own = [r.wj_in[:, i * D + part * 256 :][:, :256] for i in range(3)]
            gather.own(part, jnp.concatenate(own, axis=1))
            gather.start(part)
        gather.own(3, r.wo_in[...])
        gather.start(3)
        for part in range(4):
            gather.own(4 + part, r.wu_in[:, part * D : (part + 1) * D])
            gather.start(4 + part)
        r.down[links.q * 4 + links.z, links.y] = r.wd_in[...].reshape(6, 16, D)
        for item in DOWN:
            gather.start(item)
        ready = gather.ready
    else:
        plain = [(r.wo_in, 0)] + [(r.wu_in, n * D) for n in range(4)]
        pairs = [
            [
                (r.wj_in.at[:, :, :, pl.ds(i * D + g * 256, 256)], r.parts.at[g, :, :, :, pl.ds(i * 256, 256)])
                for i in range(3)
            ]
            for g in range(3)
        ]
        for n, (source, first) in enumerate(plain):
            pairs.append([(source.at[:, :, :, pl.ds(first, D)], r.parts.at[3 + n])])
        pairs.append([(r.wd_in, r.down)])
        loads, used = [], 0
        for pair in pairs:
            loads.append([])
            for source, target in pair:
                loads[-1].append(pltpu.make_async_copy(source, target, r.load_sem.at[used]))
                loads[-1][-1].start()
                used += 1
        r.vec[...] = r.vec_in[...]

        def ready(item):
            if item != DOWN[1]:
                for load in loads[item]:
                    load.wait()

    def steps(*key):
        if shared:
            for stage, item in FORWARD_PLAN.get(key, ()):
                stage(gather, item)

    def steps_at(now, count, *key):
        for place in range(count if shared else 0):
            if (*key, place) in FORWARD_PLAN:

                @pl.when(now == place)
                def _(place=place):
                    steps(*key, place)

    r.depth_acc[...] = jnp.zeros_like(r.depth_acc)
    for step in range(SEQ // hb):
        slot = step % 2
        hist_copy(step, slot).wait()

        def part(i, carry, slot=slot, step=step):
            rows = pl.ds(pl.multiple_of(i * 32, 32), 32)
            here = pl.ds(pl.multiple_of(step * hb + i * 32, 32), 32)
            seed = masked(r.cot, here, step * hb + i * 32, 32, length)
            total = jnp.zeros((32, D), f32)
            for j in range(HIST):
                part_hist = r.hist[slot, j, rows, :].astype(f32)
                total = total + r.depth[j] * part_hist
                r.depth_acc[j] = r.depth_acc[j] + fold(seed * part_hist)
            r.earlier[here, :] = total
            return carry

        lax.fori_loop(0, hb // 32, part, 0)
        if step + 2 < SEQ // hb:
            hist_copy(step + 2, slot).start()
        steps(0, step)
    if shared:
        ready(VECTORS)
        join_vectors(r.pieces, r.maps, r.vec)
    factor = r.vec[8:9, :D]

    for i in range(SEQ // 128):
        rows = slice(i * 128, (i + 1) * 128)
        unit, _ = normalize(r.x[rows, :].astype(f32))
        full = unit * r.vec[GAIN_1 : GAIN_1 + 1, :D] + r.vec[SHIFT_1 : SHIFT_1 + 1, :D]
        r.normed[:, rows] = full.T.astype(bf16)
        steps(1, i)
    saves = []

    def save(source, target):
        copy = pltpu.make_async_copy(source, target, r.save_sem.at[len(saves)])
        copy.start()
        saves.append(copy)

    save(r.normed, r.normed_out)

    keys_at = lax.broadcasted_iota(jnp.int32, (1, SEQ), 1)
    key_bias = jnp.where(keys_at < length, 0.0, NEG)
    one = jnp.ones((1, SEQ), f32)
    bias_cols = r.vec[0:8, : 3 * D].T
    kinds = ((r.q, (one,)), (r.k, (key_bias, one, one, one)), (r.v, (one, one, one)))
    for target, rows in kinds:
        extra = tail(rows, SEQ)
        for h in range(HEADS):
            target[h, 64:80, :] = extra

    def four_heads(group):
        steps(2, group, 0)
        ready(group)
        for kind, (target, _) in enumerate(kinds):
            cols = slice(kind * 256, (kind + 1) * 256)
            joined = dot(r.parts[group, :, :, :, cols].reshape(D, 256), r.normed[...], 0, 0)
            first = kind * D + group * 256
            joined = joined + bias_cols[first : first + 256, 0:1]
            for h in range(4):
                upper = joined[h * 64 : h * 64 + 32]
                lower = joined[h * 64 + 32 : h * 64 + 64]
                if kind < 2:
                    cosine, sine = r.cos[...], r.sin[...]
                    upper, lower = upper * cosine - lower * sine, lower * cosine + upper * sine
                both = jnp.concatenate([upper, lower], axis=0).astype(bf16)
                if kind == 0:
                    both = both * jnp.asarray(0.125, bf16)
                target[group * 4 + h, 0:64, :] = both
            steps(2, group, kind + 1)

    diagonal = causal()

    def one_head(h, carry):
        for group in range(3):

            @pl.when(h == group * 4)
            def _(group=group):
                four_heads(group)

        keys = r.k[h].T
        for i in range(SEQ // QB):
            cols = slice(i * QB, (i + 1) * QB)
            seen = (i + 1) * QB
            scores = dot(keys[:seen], r.q[h, :, cols])
            last = jnp.where(diagonal, scores[seen - QB :], NEG)
            scores = jnp.concatenate([scores[: seen - QB], last], axis=0) if i else last
            top = jnp.max(scores, axis=0, keepdims=True)
            weights = jnp.exp(scores - top).astype(bf16)
            out = dot(r.v[h, :, :seen], weights)
            total = out[64:65]
            r.heads[at(h * 64, 64, 64), cols] = (out[:64] / total).astype(bf16)
            log_total = -(top + jnp.log(total))
            r.q[h, 64:80, cols] = tail((jnp.ones((1, QB), f32), *split_three(log_total)), QB)
        steps_at(h, HEADS, 3)
        return carry

    lax.fori_loop(0, HEADS, one_head, 0)
    save(r.parts.at[pl.ds(0, 3)], r.parts_out.at[pl.ds(0, 3)])
    save(r.q, r.q_out)
    save(r.k, r.k_out)
    save(r.v, r.v_out)
    save(r.heads, r.heads_out)

    steps(4, 0)
    ready(3)

    def project(i, carry):
        rows = at(i * 256, 256)
        out = dot(r.heads[:, rows], weight(r.parts, 3), 0, 0)
        mid = r.x[rows, :].astype(f32) + (out + r.vec[OUTPUT_BIAS : OUTPUT_BIAS + 1, :D])
        r.middle[rows, :] = mid
        unit, _ = normalize(mid)
        r.n2[rows, :] = (
            unit * r.vec[GAIN_2 : GAIN_2 + 1, :D] + r.vec[SHIFT_2 : SHIFT_2 + 1, :D]
        ).astype(bf16)
        steps_at(i, 4, 5)
        return carry

    lax.fori_loop(0, SEQ // 256, project, 0)
    save(r.middle, r.middle_out)
    save(r.n2, r.n2_out)
    def upward(i, carry):
        steps_at(i, 8, 6)
        for n in range(4):

            @pl.when(i == n)
            def _(n=n):
                ready(4 + n)

        rows = at((i // 4) * 512, 512)
        cols = at((i % 4) * D, D)
        up = dot(r.n2[rows, :], weight(r.parts, 4 + i % 4))
        up = up + r.vec[UP_BIAS : UP_BIAS + 1, cols]
        square = up * up
        turn = jnp.tanh(up * (C0 + (C0 * C1) * square))
        half = 0.5 + 0.5 * turn
        r.hidden[rows, cols] = (up * half).astype(bf16)
        bent = (2.0 * up) * (C0 + (3.0 * C0 * C1) * square)
        r.slope[rows, cols] = (half + bent * (half * (1.0 - half))).astype(bf16)
        return carry

    lax.fori_loop(0, 8, upward, 0)
    save(r.parts.at[pl.ds(3, 5)], r.parts_out.at[pl.ds(3, 5)])
    save(r.slope, r.slope_out)
    for n in range(3):
        save(r.hidden.at[:, pl.ds(n * SEQ, SEQ)], r.hidden_out.at[n])

    def downward(cols, i, carry):
        rows = at(i * 256, 256)
        down = r.down[:, :, :, :, cols].reshape(FF, cols.stop - cols.start)
        out = dot(r.hidden[rows, :], down)
        block = r.middle[rows, cols] + (out + r.vec[DOWN_BIAS : DOWN_BIAS + 1, cols])
        r.layer[rows, cols] = (r.earlier[rows, cols] + r.depth[HIST] * block).astype(bf16)
        index = lax.broadcasted_iota(jnp.int32, (256, 1), 0) + i * 256
        seed = jnp.where(index < length, r.cot[rows, cols].astype(f32), 0.0)
        r.depth_acc[HIST, :, cols] = r.depth_acc[HIST, :, cols] + fold(seed * block)
        steps_at(i, 4, 8, cols.start)
        return carry

    for item in DOWN:
        steps(7, item)
        ready(item)
        cols = slice(0, WIDE) if item == PARTS else slice(WIDE, D)
        lax.fori_loop(0, SEQ // 256, functools.partial(downward, cols), 0)
    save(r.down, r.down_out)
    save(r.layer, r.layer_out)
    r.depth_out[...] = jnp.zeros_like(r.depth_out)
    for j in range(HIST + 1):
        r.depth_out[j : j + 1, :] = jnp.sum(r.depth_acc[j], axis=0, keepdims=True) * factor
    if shared:
        links.finish()
    for copy in saves:
        copy.wait()


def forward_shared(
    length, depth, x, cot, cos, sin, history, maps, piece, wj_in, wo_in, wu_in, wd_in, layer_out, normed_out,
    q_out, k_out, v_out, heads_out, middle_out, n2_out, hidden_out, slope_out, parts_out, down_out, vec,
    depth_out, parts, down, hist, earlier, normed, q, k, v, heads, middle, n2, hidden, slope, layer,
    depth_acc, load_sem, hist_sem, save_sem, rests, pieces, send_sem, recv_sem,
):
    forward_steps(types.SimpleNamespace(**locals()), True)


def forward_alone(
    length, depth, x, cot, cos, sin, history, vec_in, wj_in, wo_in, wu_in, wd_in, layer_out, normed_out,
    q_out, k_out, v_out, heads_out, middle_out, n2_out, hidden_out, slope_out, parts_out, down_out, vec,
    depth_out, parts, down, hist, earlier, normed, q, k, v, heads, middle, n2, hidden, slope, layer,
    depth_acc, load_sem, hist_sem, save_sem,
):
    forward_steps(types.SimpleNamespace(**locals()), False)


def shape(dims, dtype=bf16):
    return jax.ShapeDtypeStruct(dims, dtype)


LIFTED = (HEADS, LIFT, SEQ)
SAVED = (
    shape((D, SEQ)),
    *(shape(LIFTED), shape(LIFTED), shape(LIFTED)),
    shape((D, SEQ)),
    shape((SEQ, D), f32),
    shape((SEQ, D)),
    shape((3, SEQ, SEQ)),
    shape((SEQ, FF)),
    shape((PARTS, 16, 3, 16, D)),
    shape((16, 2, 6, 16, D)),
)


def vmem(dims, dtype=bf16):
    return pltpu.VMEM(dims, dtype)


def forward(common, special, shared):
    dma = pltpu.SemaphoreType.DMA
    scratch = [
        *(vmem(s.shape, s.dtype) for s in SAVED[-2:]),
        vmem((2, HIST, 128, D)),
        vmem((SEQ, D), f32),
        *(vmem(s.shape, s.dtype) for s in SAVED[:7]),
        *(vmem((SEQ, FF)), vmem((SEQ, FF)), vmem((SEQ, D))),
        vmem((HIST + 1, 8, D), f32),
        *(dma((16,)), dma((2,)), dma((20,))),
    ]
    if shared:
        scratch += [vmem((PARTS, 4, 2, 3, 4, 16, 128)), vmem((512, 128), f32)]
        scratch += [dma((44,)), dma((44,))]
    return pl.pallas_call(
        forward_shared if shared else forward_alone,
        name="forward_block",
        out_shape=[shape((SEQ, D)), *SAVED, shape((16, FF), f32), shape((8, D), f32)],
        in_specs=[SM, SM, VM, VM, VM, VM, ANY] + ([VM] * 6 if shared else [VM] + [ANY] * 4),
        out_specs=[ANY] * (1 + len(SAVED)) + [VM, VM],
        scratch_shapes=scratch,
        compiler_params=pltpu.CompilerParams(
            vmem_limit_bytes=62 << 20,
            collective_id=0 if shared else None,
            has_side_effects=shared,
        ),
    )(*common, *special)


BACKWARD_PLAN = {
    (0, 3): ((Scatter.first, 0), (Scatter.first, 1)),
    (0, 4): ((Scatter.first, 2),),
    (0, 5): ((Scatter.first, 3),),
    (0, 7): ((Scatter.second, 0),),
    (1, 1): ((Scatter.second, 1),),
    (1, 2): ((Scatter.first, 4), (Scatter.second, 2)),
    (1, 3): ((Scatter.first, 5),),
    (2, 0): ((Scatter.second, 3), (Scatter.first, 6), (Scatter.third, 0), (Scatter.first, 7), (Scatter.third, 1)),
    (2, 2): ((Scatter.second, 4), (Scatter.third, 2), (None, 0)),
    (3, 0): ((Scatter.second, 5), (None, 1), (Scatter.third, 3)),
    (4, 1): ((None, 2),),
    (5, 0): ((Scatter.first, 8), (Scatter.second, 6), (None, 3), (Scatter.second, 7)),
    (5, 1): ((Scatter.third, 4), (Scatter.third, 5)),
    (5, 2): ((Scatter.second, 8),),
    (8, 9): ((Scatter.third, 6), (None, 4), (Scatter.third, 7)),
    (5, 3): ((Scatter.third, 8), (None, 5)),
    (5, 4): ((None, 6), (Scatter.first, 9)),
    (5, 5): ((None, 7),),
    (5, 6): ((Scatter.second, 9), (None, 8)),
    (5, 7): ((Scatter.third, 9),),
    (5, 9): ((Scatter.first, 10), (None, 9)),
    (8, 11): ((Scatter.second, 10),),
    (6, 1): ((Scatter.third, 10), (Scatter.first, 11)),
    (7, 0): ((None, 10), (Scatter.second, 11), (Scatter.first, 12), (Scatter.third, 11), (Scatter.second, 12), (Scatter.third, 12), (None, 11)),
}


def backward_steps(r, shared):
    length = r.length[0]
    factor = r.vec[8:9, :D]
    loads = {}

    def load(name, source, target):
        loads[name] = pltpu.make_async_copy(source, target, r.load_sem.at[len(loads)])
        loads[name].start()

    def ready(*keys):
        for key in keys:
            loads[key].wait()

    load("hidden", r.hidden_in, r.hidden)
    load("lower", r.down_in, r.lower)
    load("slope", r.slope_in, r.slope)
    load("n2", r.n2_in, r.n2)
    load("upper", r.parts_in.at[pl.ds(4, 4)], r.upper)
    load("middle", r.middle_in, r.middle)
    load("heads", r.heads_in, r.heads)
    load("k", r.k_in, r.k)
    load("q", r.q_in, r.q)
    load("v", r.v_in, r.v)
    load("normed", r.normed_in, r.normed)
    r.vec_grad[...] = jnp.zeros_like(r.vec_grad)

    if shared:
        links = Links(r.send_sem, r.recv_sem, r.slope, r.middle)
        links.greet()
        scatter = Scatter(links, 0, r.credit, r.packed, r.near, r.one, r.two, r.three)
        small = Scatter(
            links,
            CHUNKS * 4,
            None,
            *(r.vec_packed, r.vec_near, r.vec_one, r.vec_two, r.vec_three),
        )
    waiting = {}
    count = [0]

    def put_out(value, target):
        slot = count[0] % 2
        count[0] += 1
        if slot in waiting:
            waiting.pop(slot).wait()
        rows, cols = value.shape
        r.stage[slot, :rows, :cols] = value
        source = r.stage.at[slot, pl.ds(0, rows), pl.ds(0, cols)]
        copy = pltpu.make_async_copy(source, target, r.stage_sem.at[slot])
        copy.start()
        waiting[slot] = copy

    def place(chunk, half, value):
        slot = chunk % SLOTS
        for i in range(8):
            p = half * 8 + i
            block = value[i * 48 : (i + 1) * 48]
            for y in (0, 1):
                main = block[32 * y : 32 * y + 16].astype(bf16)
                rest = block[16 + 8 * y : 24 + 8 * y]
                rest = jnp.concatenate([rest[:, :HALF], rest[:, HALF:]], axis=0).astype(bf16)
                whole = jnp.concatenate([main, rest], axis=1)
                for n in range(PACK // 128):
                    r.packed[slot, p // 4, y, n, p % 4] = whole[:, n * 128 : (n + 1) * 128]

    def place_down(tile, value):
        for i in range(value.shape[0] // 16):
            owner, t = divmod(tile + i, 6)
            q, z, y = owner // 8, owner % 8 // 2, owner % 2
            block = value[i * 16 : (i + 1) * 16].astype(bf16)
            for n in range(6):
                chunk, col = divmod(t * 6 + n, PACK // 128)
                r.packed[chunk, q, y, col, z] = block[:, n * 128 : (n + 1) * 128]

    def put_part(chunk, make, targets):
        if not shared:
            for half in (0, 1):
                value = make(half)
                for n, target in enumerate(targets):
                    wide = D // len(targets)
                    rows = pl.ds(half * 384, 384)
                    put_out(value[:, n * wide : (n + 1) * wide], target.at[rows])
            return
        steps(8, chunk)
        if chunk >= SLOTS:
            scatter.free(chunk - SLOTS)
        for half in (0, 1):
            place(chunk, half, make(half))
        scatter.start(chunk)

    def finish(chunk):
        total = scatter.total(chunk)
        if chunk < 4:
            for n in range(PACK // 128):
                t, col = divmod(chunk * (PACK // 128) + n, 6)
                r.gd[t * 16 : (t + 1) * 16, col * 128 : (col + 1) * 128] = total[n]
            return
        even = links.y == 0
        for n in range(6):
            rest = total[6 + n % 3][n // 3 * 8 : n // 3 * 8 + 8]
            upper, lower = total[n][0:8], total[n][8:16]
            if chunk < 8:
                target, first = r.gu, (chunk - 4) * D + n * 128
            elif chunk == 8:
                target, first = r.go, n * 128
            else:
                target, first = r.gj, n // 2 * D + (chunk - 9) * 256 + n % 2 * 128
            cols = slice(first, first + 128)
            target[0:8, cols] = jnp.where(even, upper, rest)
            target[8:16, cols] = jnp.where(even, lower, upper)
            target[16:24, cols] = jnp.where(even, rest, lower)

    def steps(*key):
        if shared:
            for stage, chunk in BACKWARD_PLAN.get(key, ()):
                if stage is None:
                    finish(chunk)
                elif chunk < CHUNKS:
                    stage(scatter, chunk)
                else:
                    stage(small, 0)

    def steps_at(now, count, *key):
        for place in range(count if shared else 0):
            if (*key, place) in BACKWARD_PLAN:

                @pl.when(now == place)
                def _(place=place):
                    steps(*key, place)

    def add_row(row, cols, value):
        r.vec_grad[row : row + 1, cols] += jnp.sum(value, axis=0, keepdims=True)

    for i in range(SEQ // 128):
        rows = slice(i * 128, (i + 1) * 128)
        seed = masked(r.cot, rows, i * 128, 128, length) * factor
        top = (r.depth[HIST] * seed).astype(bf16)
        r.low[rows, :] = top
        add_row(DOWN_BIAS, slice(0, D), top.astype(f32))

    ready("hidden")
    for n in range(6):
        value = dot(r.hidden[n // 2, :, n % 2 * 512 : n % 2 * 512 + 512], r.low[...], 0, 0)
        if shared:
            place_down(n * 32, value)
        else:
            put_out(value, r.gd.at[pl.ds(n * 512, 512)])
    for chunk in range(4 if shared else 0):
        scatter.start(chunk)

    ready("lower", "slope")

    def up_low(i, carry):
        cols = at((i % 4) * D, D)
        rows = at((i // 4) * 512, 512)
        back = dot(r.low[rows, :], r.lower[pl.ds((i % 4) * 4, 4)].reshape(D, D), 1, 1)
        out = (back * r.slope[rows, cols].astype(f32)).astype(bf16)
        r.slope[rows, cols] = out
        add_row(UP_BIAS, cols, out.astype(f32))
        steps_at(i, 8, 0)
        return carry

    lax.fori_loop(0, 8, up_low, 0)
    load("joint", r.parts_in.at[pl.ds(0, 4)], r.lower.reshape(4, 16, 3, 16, D))

    ready("n2")
    for n in range(4):
        put_part(
            4 + n,
            lambda half, n=n: dot(
                r.n2[:, half * 384 : half * 384 + 384], r.slope[:, n * D : (n + 1) * D], 0, 0
            ),
            None if shared else [r.gu.at[:, pl.ds(n * D, D)]],
        )
        steps(1, n)

    ready("upper", "middle")
    def second_norm(i, carry):
        rows = at(i * 256, 256)
        back = jnp.zeros((256, D), f32)
        for n in range(4):
            back = back + dot(r.slope[rows, n * D : (n + 1) * D], weight(r.upper, n), 1, 1)
        unit, scale = normalize(r.middle[rows, :])
        add_row(GAIN_2, slice(0, D), back * unit)
        add_row(SHIFT_2, slice(0, D), back)
        back = back * r.vec[GAIN_2 : GAIN_2 + 1, :D]
        along = jnp.mean(back * unit, axis=-1, keepdims=True)
        across = jnp.mean(back, axis=-1, keepdims=True)
        seed = masked(r.cot, rows, i * 256, 256, length) * factor
        out = r.depth[HIST] * seed + scale * (back - across - unit * along)
        r.middle[rows, :] = out
        out_low = out.astype(bf16)
        r.low[rows, :] = out_low
        add_row(OUTPUT_BIAS, slice(0, D), out_low.astype(f32))
        steps_at(i, 4, 2)
        return carry

    lax.fori_loop(0, SEQ // 256, second_norm, 0)

    ready("heads", "joint")
    put_part(
        8,
        lambda half: dot(r.heads[half * 384 : half * 384 + 384, :], r.low[...]),
        None if shared else [r.go],
    )
    steps(3, 0)

    def heads_back(i, carry):
        rows = at(i * 256, 256)
        flat = r.lower.reshape(3072 // 16, 16, D)[pl.ds(144 + i * 16, 16)].reshape(256, D)
        back = dot(flat, r.low[...], 1, 1).astype(bf16)
        r.grad[at(i * 4, 4, 4), 0:64, :] = back.reshape(4, 64, SEQ)
        product = back.astype(f32) * r.heads[rows, :].astype(f32)
        for h in range(4):
            total = jnp.sum(product[h * 64 : (h + 1) * 64], axis=0, keepdims=True)
            r.grad[i * 4 + h, 64:80, :] = tail(split_three(-total), SEQ)
        steps_at(i, 3, 4)
        return carry

    lax.fori_loop(0, 3, heads_back, 0)

    ready("k", "q", "v", "normed")
    load("x", r.x_in, r.n2)
    diagonal = causal()

    def turn_back(value):
        upper, lower = value[:32], value[32:]
        cosine, sine = r.cos[...], r.sin[...]
        return jnp.concatenate(
            [upper * cosine + lower * sine, lower * cosine - upper * sine], axis=0
        ).astype(bf16)

    def joint_part(part):
        put_part(
            9 + part,
            lambda half: dot(
                r.normed[half * 384 : half * 384 + 384, :], r.hidden[part, 0:D, :], 1, 1
            ),
            None if shared else [r.gj.at[:, pl.ds(n * D + part * 256, 256)] for n in range(3)],
        )
        sums = jnp.sum(r.hidden[part, 0:D, :].astype(f32), axis=1, keepdims=True)
        sums = jnp.broadcast_to(sums, (D, 8)).T
        for n in range(3):
            first = n * D + part * 256
            r.vec_grad[JOINT_BIAS : JOINT_BIAS + 1, first : first + 256] = sums[
                0:1, n * 256 : (n + 1) * 256
            ]

    def one_head(h, carry):
        keys = r.k[h].T
        values = r.v[h].T
        group = h // 4
        query_rows, key_rows, value_rows = (at(n * 256 + h % 4 * 64, 64, 64) for n in range(3))
        query_grad = jnp.zeros((64, SEQ), f32)
        key_grads = []
        for j in range(SEQ // QB):
            here = slice(j * QB, (j + 1) * QB)
            scores = dot(keys[here], r.q[h, :, j * QB :])
            probs = jnp.exp(scores)
            front = jnp.where(diagonal, probs[:, :QB], 0.0)
            probs = jnp.concatenate([front, probs[:, QB:]], axis=1) if j < 3 else front
            probs_grad = dot(values[here], r.grad[h, :, j * QB :])
            scores_low = (probs * probs_grad).astype(bf16)
            value_grad = dot(r.grad[h, 0:64, j * QB :], probs.astype(bf16), 1, 1)
            r.hidden[group, value_rows, here] = value_grad.astype(bf16)
            key_grads.append(dot(r.q[h, 0:64, j * QB :], scores_low, 1, 1))
            step = dot(r.k[h, 0:64, here], scores_low)
            if j:
                step = jnp.concatenate([jnp.zeros((64, j * QB), f32), step], axis=1)
            query_grad = query_grad + step
        r.hidden[group, query_rows, :] = turn_back(query_grad * 0.125)
        r.hidden[group, key_rows, :] = turn_back(jnp.concatenate(key_grads, axis=1))
        if shared:
            for n in range(3):

                @pl.when(h == n * 4 + 3)
                def _(n=n):
                    joint_part(n)

        steps_at(h, HEADS, 5)
        return carry

    lax.fori_loop(0, HEADS, one_head, 0)
    if not shared:
        for part in range(3):
            joint_part(part)

    ready("x")

    def first_norm(i, carry):
        rows = at(i * 256, 256)
        back = jnp.zeros((256, D), f32)
        for part in range(3):
            flat = r.hidden[part, 0:D, rows].T
            joint = r.lower.reshape(4, 16, 3, 16, D)[part].reshape(D, D)
            back = back + dot(flat, joint, 1, 1)
        unit, scale = normalize(r.n2[rows, :].astype(f32))
        add_row(GAIN_1, slice(0, D), back * unit)
        add_row(SHIFT_1, slice(0, D), back)
        back = back * r.vec[GAIN_1 : GAIN_1 + 1, :D]
        along = jnp.mean(back * unit, axis=-1, keepdims=True)
        across = jnp.mean(back, axis=-1, keepdims=True)
        r.middle[rows, :] = r.middle[rows, :] + scale * (back - across - unit * along)
        steps_at(i, 4, 6)
        return carry

    lax.fori_loop(0, SEQ // 256, first_norm, 0)
    last = pltpu.make_async_copy(r.middle, r.input_grad, r.save_sem.at[0])
    last.start()
    if shared:
        cut_vectors(r.vec_grad, r.maps, r.pieces)
        lane = lax.broadcasted_iota(jnp.int32, (1, 128), 1)
        row = jnp.zeros((1, 128), f32)
        for j in range(HIST + 1):
            total = jnp.sum(r.depth_rows[j : j + 1, :], axis=1, keepdims=True)
            row = jnp.where(lane == j, total, row)
        r.pieces[pl.ds(8, 32, stride=16), :] = jnp.broadcast_to(row, (32, 128))
        for i in range(7):
            r.pieces[pl.ds(9 + i, 32, stride=16), :] = jnp.zeros((32, 128), f32)
        r.vec_packed[0] = r.pieces[...].reshape(4, 2, 1, 4, 16, 128)
        small.start(0)
        steps(7, 0)
        r.pieces_out[...] = small.total(0)[0]
        links.finish()
    for copy in waiting.values():
        copy.wait()
    last.wait()


def backward_shared(
    length, depth, x_in, cot, cos, sin, vec, depth_rows, maps, normed_in, q_in, k_in, v_in, heads_in,
    middle_in, n2_in, hidden_in, slope_in, parts_in, down_in, input_grad, gj, go, gu, gd, pieces_out, upper,
    lower, normed, q, k, v, heads, middle, n2, hidden, slope, low, grad, load_sem, save_sem, packed, near,
    one, two, three, pieces, vec_packed, vec_near, vec_one, vec_two, vec_three, vec_grad, send_sem, recv_sem,
    credit,
):
    backward_steps(types.SimpleNamespace(**locals()), True)


def backward_alone(
    length, depth, x_in, cot, cos, sin, vec, depth_rows, maps, normed_in, q_in, k_in, v_in, heads_in,
    middle_in, n2_in, hidden_in, slope_in, parts_in, down_in, input_grad, gj, go, gu, gd, vec_grad, upper,
    lower, normed, q, k, v, heads, middle, n2, hidden, slope, low, grad, load_sem, save_sem, stage, stage_sem,
):
    backward_steps(types.SimpleNamespace(**locals()), False)


def backward(common, saved, shared):
    dma = pltpu.SemaphoreType.DMA
    local_sizes = SAVED[:9]
    scratch = [
        vmem((4, 16, 3, 16, D)),
        vmem((16, 2, 6, 16, D)),
        *(vmem(s.shape, s.dtype) for s in local_sizes),
        vmem((SEQ, D)),
        vmem(LIFTED),
        *(dma((16,)), dma((1,))),
    ]
    if shared:
        outs = [(24, 3 * D), (24, D), (24, FF), (96, D), (16, 128)]
        scratch += [
            vmem((SLOTS, 4, 2, PACK // 128, 4, 16, 128)),
            vmem((NEAR, 2, 2, PACK // 128, 4, 16, 128)),
            vmem((CHUNKS, 2, PACK // 128, 4, 16, 128)),
            vmem((CHUNKS, PACK // 128, 4, 16, 128)),
            vmem((CHUNKS, 3, PACK // 128, 16, 128)),
            vmem((512, 128), f32),
            vmem((1, 4, 2, 1, 4, 16, 128), f32),
            vmem((1, 2, 2, 1, 4, 16, 128), f32),
            vmem((1, 2, 1, 4, 16, 128), f32),
            vmem((1, 1, 4, 16, 128), f32),
            vmem((1, 3, 1, 16, 128), f32),
            vmem((8, FF), f32),
            *(dma((CHUNKS * 4 + 4,)), dma((CHUNKS * 4 + 4,))),
            pltpu.SemaphoreType.REGULAR,
        ]
    else:
        outs = [(D, 3 * D), (D, D), (D, FF), (FF, D), (8, FF)]
        scratch += [vmem((2, 512, D), f32), dma((2,))]
    return pl.pallas_call(
        backward_shared if shared else backward_alone,
        name="backward_block",
        out_shape=[shape((SEQ, D), f32), *(shape(dims, f32) for dims in outs)],
        in_specs=[SM, SM, ANY] + [VM] * 6 + [ANY] * len(SAVED),
        out_specs=[ANY] + ([VM] * 5 if shared else [ANY] * 4 + [VM]),
        scratch_shapes=scratch,
        compiler_params=pltpu.CompilerParams(
            vmem_limit_bytes=63 << 20,
            collective_id=1 if shared else None,
            has_side_effects=shared,
        ),
    )(*common, *saved)


def results(length, depth, vec, cot, pieces, *refs):
    sources, targets, history_grad, rest = refs[:6], refs[6:12], refs[12], refs[13:]
    vectors, held, (stage, in_sem, out_sem, stage_sem) = rest[:-10], rest[-10:-4], rest[-4:]
    inward = [
        pltpu.make_async_copy(source, place, in_sem.at[i])
        for i, (source, place) in enumerate(zip(sources, held))
    ]
    outward = [
        pltpu.make_async_copy(place, target, out_sem.at[i])
        for i, (place, target) in enumerate(zip(held, targets))
    ]
    for copy in inward:
        copy.start()
    for i, vector in enumerate(vectors):
        vector[...] = pieces[i : i + 1, : vector.shape[1]]
    factor = vec[8:9, :D]
    waiting = {}
    for i in range(SEQ // 128):
        slot = i % 2
        if slot in waiting:
            waiting.pop(slot).wait()
        seed = masked(cot, slice(i * 128, (i + 1) * 128), i * 128, 128, length[0]) * factor
        for j in range(HIST):
            stage[slot, j] = depth[j] * seed
        target = history_grad.at[:, pl.ds(i * 128, 128)]
        waiting[slot] = pltpu.make_async_copy(stage.at[slot], target, stage_sem.at[slot])
        waiting[slot].start()
        if i == 3:
            for copy, onward in zip(inward, outward):
                copy.wait()
                onward.start()
    for copy in [*waiting.values(), *outward]:
        copy.wait()


def write_results(length, depth, vec, cot, pieces, arrays, sizes):
    dma = pltpu.SemaphoreType.DMA
    outs = [shape(a.shape, a.dtype) for a in arrays]
    return pl.pallas_call(
        results,
        out_shape=[
            *(*outs, shape((HIST, SEQ, D), f32)),
            *(shape((1, size), f32) for size in sizes),
        ],
        in_specs=[SM, SM, VM, VM, VM] + [ANY] * 6,
        out_specs=[ANY] * 7 + [VM] * len(sizes),
        scratch_shapes=[
            *(vmem(s.shape, s.dtype) for s in outs),
            *(vmem((2, HIST, 128, D), f32), dma((6,)), dma((6,)), dma((2,))),
        ],
        compiler_params=pltpu.CompilerParams(vmem_limit_bytes=62 << 20),
    )(length, depth, vec, cot, pieces, *arrays)


def turning_tables():
    half = HEAD_DIM // 2
    frequency = np.power(10000.0, np.arange(half, dtype=np.float64) * (-2.0 / HEAD_DIM))
    angles = frequency[:, None] * np.arange(SEQ, dtype=np.float64)[None, :]
    return np.cos(angles).astype(np.float32), np.sin(angles).astype(np.float32)


def lane_maps():
    maps = np.full((8, FF), -1, np.int32)
    for row, size in ((0, 24), (2, 72), (4, 96)):
        lanes = np.arange(32 * size)
        maps[row, : 32 * size] = lanes // size
        maps[row + 1, : 32 * size] = lanes % size
    return maps


def local(
    inputs,
    history,
    cotangent,
    lengths,
    joint_weight,
    joint_bias,
    output_weight,
    output_bias,
    first_gain,
    first_shift,
    second_gain,
    second_shift,
    upward_weight,
    upward_bias,
    downward_weight,
    downward_bias,
    depth_weights,
):
    devices = lax.axis_size(AXES)
    shared = (lax.axis_size("dp"), lax.axis_size("fsdp")) == (4, 8)
    vectors = (
        joint_bias,
        output_bias,
        first_gain,
        first_shift,
        second_gain,
        second_shift,
        upward_bias,
        downward_bias,
    )
    sizes = [vector.shape[0] for vector in vectors]
    shards = (joint_weight, output_weight, upward_weight, downward_weight)
    x, cot = inputs[0], cotangent[0]
    cosine, sine = turning_tables()
    maps = lane_maps()
    common = (lengths, depth_weights, x, cot, cosine, sine)
    if shared:
        piece = jnp.zeros(16 * 128, f32)
        for i, v in enumerate((*vectors, lengths)):
            after = (15 - i) * 128 + 128 - v.shape[0]
            piece = piece + lax.pad(v.astype(f32), jnp.float32(0), [(i * 128, after, 0)])
        piece = piece.reshape(16, 128)
        special = (maps, piece, *shards)
    else:
        piece = jnp.concatenate([v.astype(f32) for v in (*vectors, lengths)])
        pieces = lax.all_gather(piece, AXES, axis=0, tiled=False).reshape(devices, -1)
        rows, start = [], 0
        for size in sizes:
            row = pieces[:, start : start + size].reshape(1, -1)
            rows.append(jnp.pad(row, ((0, 0), (0, FF - row.shape[1]))))
            start += size
        count = jnp.sum(pieces[:, start:])
        vec = jnp.concatenate([*rows, jnp.full((8, FF), devices * SEQ / count, f32)])
        full = [lax.all_gather(w, AXES, axis=0, tiled=True) for w in shards]
        special = (
            vec,
            *(w.reshape(16, 3, 16, -1) for w in full[:3]),
            full[3].reshape(16, 2, 6, 16, D),
        )
    layer, *saved, vec, depth_rows = forward((*common, history), special, shared)
    input_grad, *grads, vec_grads = backward(
        (*common, vec, depth_rows, maps), saved, shared
    )
    if shared:
        arrays = (layer, input_grad, *grads)
        written = write_results(
            lengths, depth_weights, vec, cot, vec_grads, arrays, [*sizes, HIST + 1]
        )
        layer, input_grad, *grads, history_grad = written[:7]
        outs = [row[0] for row in written[7:]]
        return (
            *(layer[None], input_grad[None], history_grad[:, None]),
            *(grads[0], outs[0], grads[1]),
            *(*outs[1:6], grads[2], outs[6], grads[3], outs[7], outs[8]),
        )
    factor = vec[8, 0]
    positions = jnp.arange(SEQ, dtype=jnp.int32)
    seed = jnp.where(positions[:, None] < lengths[0], cot.astype(f32), 0.0) * factor
    history_gradient = depth_weights[:HIST, None, None, None] * seed[None, None]
    depth_terms = jnp.sum(depth_rows[: HIST + 1], axis=1)
    grads = [lax.psum_scatter(g, AXES, scatter_dimension=0, tiled=True) for g in grads]
    cols = [vec_grads[i, : size * devices].reshape(devices, size) for i, size in enumerate(sizes)]
    cols.append(jnp.broadcast_to(depth_terms[None], (devices, HIST + 1)))
    total = lax.psum_scatter(
        jnp.concatenate(cols, axis=1), AXES, scatter_dimension=0, tiled=False
    )
    outs, start = [], 0
    for size in [*sizes, HIST + 1]:
        outs.append(total[start : start + size])
        start += size
    return (
        layer[None],
        input_grad[None],
        history_gradient,
        grads[0],
        outs[0],
        grads[1],
        *outs[1:6],
        grads[2],
        outs[6],
        grads[3],
        outs[7],
        outs[8],
    )


def solution(mesh):
    row, vector = P(AXES, None), P(AXES)
    tokens, levels = P(AXES, None, None), P(None, AXES, None, None)
    return jax.shard_map(
        local,
        mesh=mesh,
        in_specs=(
            *(tokens, levels, tokens, vector),
            *(row, vector, row, vector),
            *(vector, vector, vector, vector),
            *(row, vector, row, vector, P()),
        ),
        out_specs=(
            *(tokens, tokens, levels),
            *(row, vector, row, vector),
            *(vector, vector, vector, vector),
            *(row, vector, row, vector, P()),
        ),
        check_vma=False,
    )
```

```python
import functools
import math
import types

import jax
import jax.numpy as jnp
import numpy as np
from jax import lax
from jax.experimental import pallas as pl
from jax.experimental.pallas import tpu as pltpu
from jax.sharding import PartitionSpec as P

D = 768
HEADS = 12
HEAD_DIM = 64
FF = 3072
SEQ = 1024
HIST = 4
AXES = ("dp", "fsdp")
EPS = 1e-05
NEG = -1e30
LIFT = 80
QB = 256
C0 = math.sqrt(2.0 / math.pi)
C1 = 0.044715

f32 = jnp.float32
bf16 = jnp.bfloat16
ANY = pl.BlockSpec(memory_space=pl.ANY)
VM = pl.BlockSpec(memory_space=pltpu.VMEM)
SM = pl.BlockSpec(memory_space=pltpu.SMEM)

MESH = pl.DeviceIdType.MESH
HALF = D // 2
PACK = D + HALF
PARTS = 8
CHUNKS = 12
SLOTS = 8
NEAR = 4

JOINT_BIAS, OUTPUT_BIAS, GAIN_1, SHIFT_1, GAIN_2, SHIFT_2, UP_BIAS, DOWN_BIAS = range(8)


def dot(left, right, left_dim=1, right_dim=0):
    return lax.dot_general(
        left, right, (((left_dim,), (right_dim,)), ((), ())), preferred_element_type=f32
    )


def at(start, size, unit=128):
    return pl.ds(pl.multiple_of(start, unit), size)


def normalize(values):
    mean = jnp.mean(values, axis=-1, keepdims=True)
    centred = values - mean
    variance = jnp.mean(centred * centred, axis=-1, keepdims=True)
    scale = lax.rsqrt(variance + EPS)
    return centred * scale, scale


def fold(values):
    rows, cols = values.shape
    return jnp.sum(values.reshape(rows // 8, 8, cols), axis=0)


def split_three(row):
    high = row.astype(bf16).astype(f32)
    rest = row - high
    mid = rest.astype(bf16).astype(f32)
    return high, mid, rest - mid


def tail(rows, width):
    index = lax.broadcasted_iota(jnp.int32, (16, width), 0)
    out = jnp.zeros((16, width), f32)
    for place, row in enumerate(rows):
        out = jnp.where(index == place, row, out)
    return out.astype(bf16)


def position():
    dp, fsdp = lax.axis_index("dp"), lax.axis_index("fsdp")
    return dp // 2, dp % 2, fsdp // 2, fsdp % 2


def device(x, c, z, y):
    return (x * 2 + c, z * 2 + y)


class Links:
    def __init__(self, send_sem, recv_sem, *rulers):
        x, c, z, y = position()
        self.send_sem, self.recv_sem = send_sem, recv_sem
        self.rulers = {jnp.dtype(ruler.dtype): ruler for ruler in rulers}
        self.x, self.c, self.z, self.y = x, c, z, y
        self.nx, self.nc, self.ny = 1 - x, 1 - c, 1 - y
        self.zs = (z + 1 - 2 * (z % 2), (z + 2) % 4, 3 - z)
        self.q, self.r = x * 2 + c, (1 - x) * 2 + c
        self.other_x = device(1 - x, c, z, y)
        self.other_y = device(x, c, z, 1 - y)
        self.other_c = device(x, 1 - c, z, y)
        self.along_z = [device(x, c, other, y) for other in self.zs]
        self.sent = {}

    def greet(self):
        barrier = pltpu.get_barrier_semaphore()
        peers = [self.other_x, self.other_y, self.other_c, *self.along_z]
        for peer in peers:
            pl.semaphore_signal(barrier, inc=1, device_id=peer, device_id_type=MESH)
        pl.semaphore_wait(barrier, len(peers))

    def copy(self, source, target, sem, peer):
        return pltpu.make_async_remote_copy(
            src_ref=source,
            dst_ref=target,
            send_sem=self.send_sem.at[sem],
            recv_sem=self.recv_sem.at[sem],
            device_id=peer,
            device_id_type=MESH,
        )

    def send(self, pairs, sem, peer):
        for source, target in pairs():
            self.copy(source, target, sem, peer).start()
        self.sent.setdefault(sem, []).append(pairs)

    def whole(self, refs, sem):
        size = sum(math.prod(ref.shape) for ref in refs)
        ruler = self.rulers[jnp.dtype(refs[0].dtype)]
        rows = 16
        while size % (rows * 128) or size // rows > ruler.shape[1]:
            rows += 16
        part = ruler.at[pl.ds(0, rows), pl.ds(0, size // rows)]
        return self.copy(part, part, sem, self.other_c)

    def arrived(self, targets, sem):
        self.whole(targets, sem).wait_recv()

    def left(self, sem):
        sources = [pair[0] for pairs in self.sent.pop(sem, []) for pair in pairs()]
        if sources:
            self.whole(sources, sem).wait_send()

    def finish(self):
        for sem in list(self.sent):
            self.left(sem)


DOWN = (PARTS, PARTS + 1)
VECTORS = PARTS + 2
WIDE = 512


class Gather:
    def __init__(self, links, parts, rests, down, pieces):
        self.links = links
        self.parts, self.rests, self.down, self.pieces = parts, rests, down, pieces

    def refs(self, item, q, y, z, color):
        if item == VECTORS:
            if color == 1:
                return []
            first = (q * 8 + y * 4 + (0 if z is None else z)) * 16
            return [self.pieces.at[at(first, 64 if z is None else 16, 16)]]
        rows = pl.ds(q * 4, 4) if z is None else q * 4 + z
        if item in DOWN:
            first, last = (0, 4) if item == PARTS else (4, 6)
            mid = (first + last) // 2
            first, last = {None: (first, last), 0: (first, mid), 1: (mid, last)}[color]
            return [self.down.at[rows, y, pl.ds(first, last - first)]]
        wide = {None: pl.ds(0, D), 0: pl.ds(0, HALF), 1: pl.ds(HALF, HALF)}[color]
        cut = 2 if item % 2 else 1
        narrow = {None: pl.ds(0, 3), 0: pl.ds(0, cut), 1: pl.ds(cut, 3 - cut)}[color]
        some = pl.ds(0, 4) if z is None else z
        return [
            self.parts.at[item, rows, 2 * y, :, wide],
            self.rests.at[item, q, y, narrow, some],
        ]

    def send(self, item, stage, peer, quads, z=None):
        def pairs():
            refs = []
            for q, y, color in quads:
                refs += self.refs(item, getattr(self.links, q), getattr(self.links, y), z, color)
            return [(ref, ref) for ref in refs]

        self.links.send(pairs, item * 4 + stage, peer)

    def start(self, item):
        links = self.links
        if item in DOWN:
            self.send(item, 0, links.other_x, [("q", "y", 0)], links.z)
            self.send(item, 0, links.other_y, [("q", "y", 1)], links.z)
            return
        for peer in links.along_z:
            self.send(item, 0, peer, [("q", "y", None)], links.z)

    def second(self, item):
        links = self.links
        if item in DOWN:
            refs = self.refs(item, links.r, links.y, links.z, 0)
            links.arrived(refs + self.refs(item, links.q, links.ny, links.z, 1), item * 4)
            quads = [("q", "y", 0), ("r", "y", 0), ("q", "y", 1), ("q", "ny", 1)]
            for peer in links.along_z:
                self.send(item, 1, peer, quads, links.z)
            return
        refs = [self.refs(item, links.q, links.y, z, None) for z in links.zs]
        links.arrived(sum(refs, []), item * 4)
        self.send(item, 1, links.other_x, [("q", "y", 0)])
        self.send(item, 1, links.other_y, [("q", "y", 1)])

    def third(self, item):
        links = self.links
        if item in DOWN:
            quads = [(links.q, links.y, 0), (links.r, links.y, 0)]
            quads += [(links.q, links.y, 1), (links.q, links.ny, 1)]
            refs = [self.refs(item, q, y, z, k) for q, y, k in quads for z in links.zs]
            links.arrived(sum(refs, []), item * 4 + 1)
        else:
            refs = self.refs(item, links.r, links.y, None, 0)
            links.arrived(refs + self.refs(item, links.q, links.ny, None, 1), item * 4 + 1)
        first = [("q", "y", 0), ("r", "y", 0)]
        second = [("q", "y", 1), ("q", "ny", 1)]
        self.send(item, 2, links.other_y, first)
        self.send(item, 2, links.other_x, second)
        self.send(item, 3, links.other_c, first + second)

    def fourth(self, item):
        links = self.links
        quads = [("q", "ny", 0), ("r", "ny", 0), ("r", "y", 1), ("r", "ny", 1)]
        refs = [self.refs(item, getattr(links, q), getattr(links, y), None, k) for q, y, k in quads]
        links.arrived(sum(refs, []), item * 4 + 2)
        self.send(item, 3, links.other_c, quads)

    def ready(self, item):
        links = self.links
        refs = []
        for xx in (0, 1):
            for yy in (0, 1):
                for color in (0, 1):
                    refs += self.refs(item, xx * 2 + links.nc, yy, None, color)
        links.arrived(refs, item * 4 + 3)
        if item < PARTS:

            def merge(p, carry):
                q, z = p // 4, p % 4
                for i in range(3):
                    even = self.rests[item, q, 0, i, z].astype(f32)
                    odd = self.rests[item, q, 1, i, z].astype(f32)
                    for k in (0, 1):
                        first = k * HALF + i * 128
                        half = slice(k * 8, k * 8 + 8)
                        self.parts[item, p, 1, :, first : first + 128] = jnp.concatenate(
                            [even[half], odd[half]], axis=0
                        ).astype(bf16)
                return carry

            lax.fori_loop(0, 16, merge, 0)

    def own(self, item, shard):
        links = self.links
        full = shard.astype(f32)
        even = links.y == 0
        main = jnp.where(even, full[0:16], full[8:24])
        rest = jnp.where(even, full[16:24], full[0:8])
        self.parts[item, links.q * 4 + links.z, 2 * links.y] = main.astype(bf16)
        for i in range(3):
            left, right = rest[:, i * 128 : (i + 1) * 128], rest[:, HALF + i * 128 :][:, :128]
            self.rests[item, links.q, links.y, i, links.z] = jnp.concatenate(
                [left, right], axis=0
            ).astype(bf16)


def block_order():
    index = lax.broadcasted_iota(jnp.int32, (32, 1), 0)
    return (index & 24) + (index & 3) * 2 + ((index >> 2) & 1)


def spread(maps_ref, size):
    row = {24: 0, 72: 2, 96: 4}[size]
    wide = 32 * size
    owner = maps_ref[row : row + 1, :wide] == block_order()
    lane = maps_ref[row + 1 : row + 2, :wide] == lax.broadcasted_iota(jnp.int32, (128, 1), 0)
    return owner, jnp.where(lane, 1.0, 0.0).astype(bf16)


VECTOR_SIZES = (72, 24, 24, 24, 24, 24, 96, 24)


def join_vectors(pieces_ref, maps_ref, vec_ref):
    for size in (24, 72, 96):
        owner, lane = spread(maps_ref, size)
        for row, own in enumerate(VECTOR_SIZES):
            if own == size:
                piece = pieces_ref[pl.ds(row, 32, stride=16), :].astype(bf16)
                full = jnp.where(owner, dot(piece, lane), 0.0)
                vec_ref[row : row + 1, : 32 * size] = jnp.sum(full, axis=0, keepdims=True)
    counts = pieces_ref[pl.ds(8, 32, stride=16), :]
    count = jnp.sum(jnp.sum(counts, axis=0, keepdims=True), axis=1, keepdims=True)
    vec_ref[8:16, :] = jnp.broadcast_to((32 * SEQ) / count, (8, FF))


def cut_vectors(vec_ref, maps_ref, pieces_ref):
    for size in (24, 72, 96):
        owner, lane = spread(maps_ref, size)
        for row, own in enumerate(VECTOR_SIZES):
            if own == size:
                full = jnp.where(owner, vec_ref[row : row + 1, : 32 * size], 0.0)
                high = full.astype(bf16)
                low = (full - high.astype(f32)).astype(bf16)
                pieces_ref[pl.ds(row, 32, stride=16), :] = dot(high, lane, 1, 1) + dot(
                    low, lane, 1, 1
                )


class Scatter:
    def __init__(self, links, base, credit, packed, near, one, two, three):
        self.links, self.base, self.credit = links, base, credit
        self.packed, self.near = packed, near
        self.one, self.two, self.three = one, two, three
        self.wide = packed.shape[3]

    def columns(self, chunk):
        mid = (self.wide + 1 - chunk % 2) // 2
        return pl.ds(0, mid), pl.ds(mid, self.wide - mid)

    def send(self, chunk, stage, peer, pairs, cols=None):
        if cols is None or cols.size:
            self.links.send(pairs, self.base + chunk * 4 + stage, peer)

    def start(self, chunk):
        links = self.links
        if self.credit is not None and chunk >= NEAR:
            pl.semaphore_wait(self.credit, 1)

        def pairs():
            return [
                (
                    self.packed.at[chunk % SLOTS, xx * 2 + links.nc],
                    self.near.at[chunk % NEAR, xx],
                )
                for xx in (0, 1)
            ]

        self.send(chunk, 0, links.other_c, pairs)

    def first(self, chunk):
        links = self.links
        slot, near = chunk % SLOTS, chunk % NEAR
        links.arrived([self.near.at[near, xx] for xx in (0, 1)], self.base + chunk * 4)

        def add(i, carry):
            xx, yy = i // 2, i % 2
            mine = self.packed[slot, xx * 2 + links.c, yy]
            self.packed[slot, xx * 2 + links.c, yy] = mine + self.near[near, xx, yy]
            return carry

        lax.fori_loop(0, 4, add, 0)
        if self.credit is not None and chunk + NEAR < CHUNKS:
            pl.semaphore_signal(self.credit, inc=1, device_id=links.other_c, device_id_type=MESH)
        here, there = self.columns(chunk)

        def by_y():
            return [
                (self.packed.at[slot, k * 2 + links.c, links.ny, here], self.one.at[chunk, k, here])
                for k in (0, 1)
            ]

        def by_x():
            return [
                (self.packed.at[slot, links.r, k, there], self.one.at[chunk, k, there])
                for k in (0, 1)
            ]

        self.send(chunk, 1, links.other_y, by_y, here)
        self.send(chunk, 1, links.other_x, by_x, there)

    def second(self, chunk):
        links = self.links
        slot = chunk % SLOTS
        links.arrived([self.one.at[chunk, k] for k in (0, 1)], self.base + chunk * 4 + 1)
        here, there = self.columns(chunk)
        for k in (0, 1):
            for cols, q, y in ((here, k * 2 + links.c, links.y), (there, links.q, k)):
                if cols.size:
                    mine = self.packed[slot, q, y, cols]
                    self.one[chunk, k, cols] = mine + self.one[chunk, k, cols]
        self.send(
            chunk,
            2,
            links.other_x,
            lambda: [(self.one.at[chunk, links.nx, here], self.two.at[chunk, here])],
            here,
        )
        self.send(
            chunk,
            2,
            links.other_y,
            lambda: [(self.one.at[chunk, links.ny, there], self.two.at[chunk, there])],
            there,
        )

    def third(self, chunk):
        links = self.links
        links.arrived([self.two.at[chunk]], self.base + chunk * 4 + 2)
        for cols, mine in zip(self.columns(chunk), (links.x, links.y)):
            if cols.size:
                self.two[chunk, cols] = self.one[chunk, mine, cols] + self.two[chunk, cols]
        for k in range(3):

            def pairs(k=k):
                return [(self.two.at[chunk, :, links.zs[k]], self.three.at[chunk, k])]

            self.send(chunk, 3, links.along_z[k], pairs)

    def total(self, chunk):
        links = self.links
        links.arrived([self.three.at[chunk, k] for k in range(3)], self.base + chunk * 4 + 3)
        parts = [self.two[chunk, :, links.z]] + [self.three[chunk, k] for k in range(3)]
        parts = [part.astype(f32) for part in parts]
        return (parts[0] + parts[1]) + (parts[2] + parts[3])

    def free(self, chunk):
        self.links.left(self.base + chunk * 4)
        self.links.left(self.base + chunk * 4 + 1)


def weight(parts_ref, item):
    return parts_ref[item].reshape(D, D)


def masked(cot_ref, rows, start, count, length):
    index = lax.broadcasted_iota(jnp.int32, (count, 1), 0) + start
    return jnp.where(index < length, cot_ref[rows, :].astype(f32), 0.0)


def causal():
    shape = (QB, QB)
    return lax.broadcasted_iota(jnp.int32, shape, 0) <= lax.broadcasted_iota(jnp.int32, shape, 1)


FORWARD_PLAN = {
    (0, 7): ((Gather.second, 10), (Gather.second, 8), (Gather.second, 9), (Gather.second, 0), (Gather.third, 10), (Gather.second, 1), (Gather.third, 0), (Gather.fourth, 10), (Gather.second, 2)),
    (1, 7): ((Gather.third, 1),),
    (2, 0, 0): ((Gather.second, 3), (Gather.fourth, 0), (Gather.third, 2), (Gather.second, 4)),
    (3, 1): ((Gather.fourth, 1), (Gather.second, 5)),
    (3, 2): ((Gather.third, 3),),
    (3, 3): ((Gather.second, 6), (Gather.fourth, 2)),
    (2, 1, 3): ((Gather.third, 4),),
    (3, 4): ((Gather.second, 7), (Gather.third, 5)),
    (3, 6): ((Gather.fourth, 3),),
    (3, 7): ((Gather.third, 6),),
    (3, 8): ((Gather.fourth, 4),),
    (3, 9): ((Gather.third, 7),),
    (3, 10): ((Gather.fourth, 5),),
    (5, 1): ((Gather.fourth, 6), (Gather.third, 8)),
    (6, 1): ((Gather.fourth, 7),),
    (6, 4): ((Gather.third, 9),),
    (6, 7): ((Gather.fourth, 8),),
    (7, 8): ((Gather.fourth, 9),),
}


def forward_steps(r, shared):
    length = r.length[0]
    hb = 128

    def hist_copy(step, slot):
        return pltpu.make_async_copy(
            r.history.at[:, 0, pl.ds(step * hb, hb)], r.hist.at[slot], r.hist_sem.at[slot]
        )

    first_loads = [
        pltpu.make_async_copy(r.cot_in, r.cot, r.load_sem.at[22]),
        pltpu.make_async_copy(r.x_in, r.x, r.load_sem.at[23]),
    ]
    first_loads[0].start()
    hist_copy(0, 0).start()
    hist_copy(1, 1).start()
    first_loads[1].start()
    if shared:
        links = Links(r.send_sem, r.recv_sem, r.hidden, r.earlier)
        gather = Gather(links, r.parts, r.rests, r.down, r.pieces)
        links.greet()
        place = (links.q * 8 + links.y * 4 + links.z) * 16
        r.pieces[at(place, 16, 16), :] = r.piece[...]
        gather.start(VECTORS)
        for part in range(3):
            own = [r.wj_in[:, i * D + part * 256 :][:, :256] for i in range(3)]
            gather.own(part, jnp.concatenate(own, axis=1))
            gather.start(part)
        gather.own(3, r.wo_in[...])
        gather.start(3)
        for part in range(4):
            gather.own(4 + part, r.wu_in[:, part * D : (part + 1) * D])
            gather.start(4 + part)
        for i in range(6):
            r.down[links.q * 4 + links.z, links.y, i] = r.wd_in[:, i * 128 : (i + 1) * 128]
        for item in DOWN:
            gather.start(item)
        ready = gather.ready
    else:
        plain = [(r.wo_in, 0)] + [(r.wu_in, n * D) for n in range(4)]
        pairs = [
            [
                (r.wj_in.at[:, :, :, pl.ds(i * D + g * 256, 256)], r.parts.at[g, :, :, :, pl.ds(i * 256, 256)])
                for i in range(3)
            ]
            for g in range(3)
        ]
        for n, (source, first) in enumerate(plain):
            pairs.append([(source.at[:, :, :, pl.ds(first, D)], r.parts.at[3 + n])])
        pairs.append(
            [(r.wd_in.at[:, :, :, pl.ds(i * 128, 128)], r.down.at[:, :, i]) for i in range(6)]
        )
        loads, used = [], 0
        for pair in pairs:
            loads.append([])
            for source, target in pair:
                loads[-1].append(pltpu.make_async_copy(source, target, r.load_sem.at[used]))
                loads[-1][-1].start()
                used += 1
        r.vec[...] = r.vec_in[...]

        def ready(item):
            if item != DOWN[1]:
                for load in loads[item]:
                    load.wait()

    def steps(*key):
        if shared:
            for stage, item in FORWARD_PLAN.get(key, ()):
                stage(gather, item)

    def steps_at(now, count, *key):
        for place in range(count if shared else 0):
            if (*key, place) in FORWARD_PLAN:

                @pl.when(now == place)
                def _(place=place):
                    steps(*key, place)

    r.depth_acc[...] = jnp.zeros_like(r.depth_acc)
    first_loads[0].wait()
    for step in range(SEQ // hb):
        slot = step % 2
        hist_copy(step, slot).wait()

        def part(i, carry, slot=slot, step=step):
            rows = pl.ds(pl.multiple_of(i * 32, 32), 32)
            here = pl.ds(pl.multiple_of(step * hb + i * 32, 32), 32)
            seed = masked(r.cot, here, step * hb + i * 32, 32, length)
            total = jnp.zeros((32, D), f32)
            for j in range(HIST):
                part_hist = r.hist[slot, j, rows, :].astype(f32)
                total = total + r.depth[j] * part_hist
                r.depth_acc[j] = r.depth_acc[j] + fold(seed * part_hist)
            r.earlier[here, :] = total
            return carry

        lax.fori_loop(0, hb // 32, part, 0)
        if step + 2 < SEQ // hb:
            hist_copy(step + 2, slot).start()
        steps(0, step)
    if shared:
        ready(VECTORS)
        join_vectors(r.pieces, r.maps, r.vec)
    factor = r.vec[8:9, :D]

    first_loads[1].wait()
    for i in range(SEQ // 128):
        rows = slice(i * 128, (i + 1) * 128)
        unit, _ = normalize(r.x[rows, :].astype(f32))
        full = unit * r.vec[GAIN_1 : GAIN_1 + 1, :D] + r.vec[SHIFT_1 : SHIFT_1 + 1, :D]
        r.normed[:, rows] = full.T.astype(bf16)
        steps(1, i)
    saves = []

    def save(source, target):
        copy = pltpu.make_async_copy(source, target, r.save_sem.at[len(saves)])
        copy.start()
        saves.append(copy)

    save(r.normed, r.normed_out)

    keys_at = lax.broadcasted_iota(jnp.int32, (1, SEQ), 1)
    key_bias = jnp.where(keys_at < length, 0.0, NEG)
    one = jnp.ones((1, SEQ), f32)
    bias_cols = r.vec[0:8, : 3 * D].T
    kinds = ((r.q, (one,)), (r.k, (key_bias, one, one, one)), (r.v, (one, one, one)))
    for target, rows in kinds:
        extra = tail(rows, SEQ)
        for h in range(HEADS):
            target[h, 64:80, :] = extra

    def four_heads(group):
        steps(2, group, 0)
        ready(group)
        for kind, (target, _) in enumerate(kinds):
            cols = slice(kind * 256, (kind + 1) * 256)
            joined = dot(r.parts[group, :, :, :, cols].reshape(D, 256), r.normed[...], 0, 0)
            first = kind * D + group * 256
            joined = joined + bias_cols[first : first + 256, 0:1]
            for h in range(4):
                upper = joined[h * 64 : h * 64 + 32]
                lower = joined[h * 64 + 32 : h * 64 + 64]
                if kind < 2:
                    cosine, sine = r.cos[...], r.sin[...]
                    upper, lower = upper * cosine - lower * sine, lower * cosine + upper * sine
                both = jnp.concatenate([upper, lower], axis=0).astype(bf16)
                if kind == 0:
                    both = both * jnp.asarray(0.125, bf16)
                target[group * 4 + h, 0:64, :] = both
            steps(2, group, kind + 1)

    diagonal = causal()

    def one_head(h, carry):
        for group in range(3):

            @pl.when(h == group * 4)
            def _(group=group):
                four_heads(group)

        keys = r.k[h].T
        for i in range(SEQ // QB):
            cols = slice(i * QB, (i + 1) * QB)
            seen = (i + 1) * QB
            scores = dot(keys[:seen], r.q[h, :, cols])
            last = jnp.where(diagonal, scores[seen - QB :], NEG)
            scores = jnp.concatenate([scores[: seen - QB], last], axis=0) if i else last
            top = jnp.max(scores, axis=0, keepdims=True)
            weights = jnp.exp(scores - top).astype(bf16)
            out = dot(r.v[h, :, :seen], weights)
            total = out[64:65]
            r.heads[at(h * 64, 64, 64), cols] = (out[:64] / total).astype(bf16)
            log_total = -(top + jnp.log(total))
            r.q[h, 64:80, cols] = tail((jnp.ones((1, QB), f32), *split_three(log_total)), QB)
        steps_at(h, HEADS, 3)
        return carry

    lax.fori_loop(0, HEADS, one_head, 0)
    save(r.parts.at[pl.ds(0, 3)], r.parts_out.at[pl.ds(0, 3)])
    save(r.q, r.q_out)
    save(r.k, r.k_out)
    save(r.v, r.v_out)
    save(r.heads, r.heads_out)

    steps(4, 0)
    ready(3)

    def project(i, carry):
        rows = at(i * 256, 256)
        out = dot(r.heads[:, rows], weight(r.parts, 3), 0, 0)
        mid = r.x[rows, :].astype(f32) + (out + r.vec[OUTPUT_BIAS : OUTPUT_BIAS + 1, :D])
        r.middle[rows, :] = mid
        unit, _ = normalize(mid)
        r.n2[rows, :] = (
            unit * r.vec[GAIN_2 : GAIN_2 + 1, :D] + r.vec[SHIFT_2 : SHIFT_2 + 1, :D]
        ).astype(bf16)
        steps_at(i, 4, 5)
        return carry

    lax.fori_loop(0, SEQ // 256, project, 0)
    save(r.middle, r.middle_out)
    save(r.n2, r.n2_out)
    def upward(i, carry):
        steps_at(i, 8, 6)
        for n in range(4):

            @pl.when(i == n)
            def _(n=n):
                ready(4 + n)

        rows = at((i // 4) * 512, 512)
        cols = at((i % 4) * D, D)
        up = dot(r.n2[rows, :], weight(r.parts, 4 + i % 4))
        up = up + r.vec[UP_BIAS : UP_BIAS + 1, cols]
        square = up * up
        turn = jnp.tanh(up * (C0 + (C0 * C1) * square))
        half = 0.5 + 0.5 * turn
        r.hidden[rows, cols] = (up * half).astype(bf16)
        bent = (2.0 * up) * (C0 + (3.0 * C0 * C1) * square)
        r.slope[rows, cols] = (half + bent * (half * (1.0 - half))).astype(bf16)
        return carry

    lax.fori_loop(0, 8, upward, 0)
    save(r.parts.at[pl.ds(3, 5)], r.parts_out.at[pl.ds(3, 5)])
    save(r.slope, r.slope_out)
    for n in range(3):
        save(r.hidden.at[:, pl.ds(n * SEQ, SEQ)], r.hidden_out.at[n])

    def downward(cols, i, carry):
        rows = at(i * 256, 256)
        blocks = range(cols.start // 128, cols.stop // 128)
        down = [r.down[:, :, n].reshape(FF, 128) for n in blocks]
        out = dot(r.hidden[rows, :], jnp.concatenate(down, axis=1))
        block = r.middle[rows, cols] + (out + r.vec[DOWN_BIAS : DOWN_BIAS + 1, cols])
        r.layer[rows, cols] = (r.earlier[rows, cols] + r.depth[HIST] * block).astype(bf16)
        index = lax.broadcasted_iota(jnp.int32, (256, 1), 0) + i * 256
        seed = jnp.where(index < length, r.cot[rows, cols].astype(f32), 0.0)
        r.depth_acc[HIST, :, cols] = r.depth_acc[HIST, :, cols] + fold(seed * block)
        steps_at(i, 4, 8, cols.start)
        return carry

    for item in DOWN:
        steps(7, item)
        ready(item)
        cols = slice(0, WIDE) if item == PARTS else slice(WIDE, D)
        blocks = pl.ds(cols.start // 128, (cols.stop - cols.start) // 128)
        save(r.down.at[:, :, blocks], r.down_out.at[:, :, blocks])
        lax.fori_loop(0, SEQ // 256, functools.partial(downward, cols), 0)
    save(r.layer, r.layer_out)
    r.depth_out[...] = jnp.zeros_like(r.depth_out)
    for j in range(HIST + 1):
        r.depth_out[j : j + 1, :] = jnp.sum(r.depth_acc[j], axis=0, keepdims=True) * factor
    if shared:
        links.finish()
    for copy in saves:
        copy.wait()


def forward_shared(
    length, depth, x_in, cot_in, cos, sin, history, maps, piece, wj_in, wo_in, wu_in, wd_in, layer_out, normed_out,
    q_out, k_out, v_out, heads_out, middle_out, n2_out, hidden_out, slope_out, parts_out, down_out, vec,
    depth_out, x, cot, parts, down, hist, earlier, normed, q, k, v, heads, middle, n2, hidden, slope, layer,
    depth_acc, load_sem, hist_sem, save_sem, rests, pieces, send_sem, recv_sem,
):
    forward_steps(types.SimpleNamespace(**locals()), True)


def forward_alone(
    length, depth, x_in, cot_in, cos, sin, history, vec_in, wj_in, wo_in, wu_in, wd_in, layer_out, normed_out,
    q_out, k_out, v_out, heads_out, middle_out, n2_out, hidden_out, slope_out, parts_out, down_out, vec,
    depth_out, x, cot, parts, down, hist, earlier, normed, q, k, v, heads, middle, n2, hidden, slope, layer,
    depth_acc, load_sem, hist_sem, save_sem,
):
    forward_steps(types.SimpleNamespace(**locals()), False)


def shape(dims, dtype=bf16):
    return jax.ShapeDtypeStruct(dims, dtype)


LIFTED = (HEADS, LIFT, SEQ)
SAVED = (
    shape((D, SEQ)),
    *(shape(LIFTED), shape(LIFTED), shape(LIFTED)),
    shape((D, SEQ)),
    shape((SEQ, D), f32),
    shape((SEQ, D)),
    shape((3, SEQ, SEQ)),
    shape((SEQ, FF)),
    shape((PARTS, 16, 3, 16, D)),
    shape((16, 2, 6, 96, 128)),
)


def vmem(dims, dtype=bf16):
    return pltpu.VMEM(dims, dtype)


def forward(common, special, shared):
    dma = pltpu.SemaphoreType.DMA
    scratch = [
        *(vmem((SEQ, D)), vmem((SEQ, D))),
        *(vmem(s.shape, s.dtype) for s in SAVED[-2:]),
        vmem((2, HIST, 128, D)),
        vmem((SEQ, D), f32),
        *(vmem(s.shape, s.dtype) for s in SAVED[:7]),
        *(vmem((SEQ, FF)), vmem((SEQ, FF)), vmem((SEQ, D))),
        vmem((HIST + 1, 8, D), f32),
        *(dma((24,)), dma((2,)), dma((24,))),
    ]
    if shared:
        scratch += [vmem((PARTS, 4, 2, 3, 4, 16, 128)), vmem((512, 128), f32)]
        scratch += [dma((44,)), dma((44,))]
    return pl.pallas_call(
        forward_shared if shared else forward_alone,
        name="forward_block",
        out_shape=[shape((SEQ, D)), *SAVED, shape((16, FF), f32), shape((8, D), f32)],
        in_specs=[SM, SM, ANY, ANY, VM, VM, ANY] + ([VM] * 6 if shared else [VM] + [ANY] * 4),
        out_specs=[ANY] * (1 + len(SAVED)) + [VM, VM],
        scratch_shapes=scratch,
        compiler_params=pltpu.CompilerParams(
            vmem_limit_bytes=62 << 20,
            collective_id=0 if shared else None,
            has_side_effects=shared,
        ),
    )(*common, *special)


BACKWARD_PLAN = {
    (9, 2): ((Scatter.first, 0),),
    (9, 3): ((Scatter.first, 1), (Scatter.first, 2)),
    (9, 4): ((Scatter.first, 3),),
    (2, 1): ((Scatter.second, 0),),
    (2, 3): ((Scatter.first, 4), (Scatter.second, 1), (Scatter.first, 5), (Scatter.first, 6)),
    (3, 0): ((Scatter.second, 2), (Scatter.first, 7)),
    (4, 2): ((Scatter.second, 3),),
    (5, 0): ((Scatter.third, 0),),
    (5, 1): ((Scatter.first, 8), (Scatter.second, 4)),
    (5, 2): ((Scatter.third, 1),),
    (5, 3): ((Scatter.second, 5), (None, 0)),
    (5, 4): ((Scatter.second, 6),),
    (5, 5): ((Scatter.third, 2), (None, 1)),
    (5, 6): ((Scatter.second, 7), (Scatter.first, 9)),
    (8, 10): ((Scatter.third, 3),),
    (5, 7): ((Scatter.second, 8),),
    (5, 8): ((Scatter.third, 4), (None, 2)),
    (5, 9): ((Scatter.third, 5), (Scatter.third, 6)),
    (5, 10): ((Scatter.third, 7), (Scatter.first, 10), (None, 3)),
    (8, 11): ((Scatter.second, 9),),
    (5, 11): ((Scatter.third, 8), (None, 4)),
    (6, 1): ((None, 5),),
    (6, 2): ((Scatter.second, 10),),
    (6, 3): ((None, 6), (Scatter.third, 9), (Scatter.first, 11)),
    (7, 0): ((None, 7), (None, 8), (Scatter.third, 10), (Scatter.first, 12), (None, 9), (Scatter.second, 11), (Scatter.second, 12), (None, 10), (Scatter.third, 11), (Scatter.third, 12), (None, 11)),
}


def backward_steps(r, shared):
    length = r.length[0]
    factor = r.vec[8:9, :D]
    loads = {}

    def load(name, source, target):
        loads[name] = pltpu.make_async_copy(source, target, r.load_sem.at[len(loads)])
        loads[name].start()

    def ready(*keys):
        for key in keys:
            loads[key].wait()

    for i in range(6):
        load(i, r.down_in.at[:, :, i], r.lower.at[:, :, :, pl.ds(i * 128, 128)])
    load("slope", r.slope_in, r.slope)
    load("n2", r.n2_in, r.n2)
    load("hidden", r.hidden_in, r.hidden)
    load("upper", r.parts_in.at[pl.ds(4, 4)], r.upper)
    load("middle", r.middle_in, r.middle)
    load("heads", r.heads_in, r.heads)
    load("k", r.k_in, r.k)
    load("q", r.q_in, r.q)
    load("v", r.v_in, r.v)
    load("normed", r.normed_in, r.normed)
    r.vec_grad[...] = jnp.zeros_like(r.vec_grad)

    if shared:
        links = Links(r.send_sem, r.recv_sem, r.slope, r.middle)
        links.greet()
        scatter = Scatter(links, 0, r.credit, r.packed, r.near, r.one, r.two, r.three)
        small = Scatter(
            links,
            CHUNKS * 4,
            None,
            *(r.vec_packed, r.vec_near, r.vec_one, r.vec_two, r.vec_three),
        )
    waiting = {}
    count = [0]

    def put_out(value, target):
        slot = count[0] % 2
        count[0] += 1
        if slot in waiting:
            waiting.pop(slot).wait()
        rows, cols = value.shape
        r.stage[slot, :rows, :cols] = value
        source = r.stage.at[slot, pl.ds(0, rows), pl.ds(0, cols)]
        copy = pltpu.make_async_copy(source, target, r.stage_sem.at[slot])
        copy.start()
        waiting[slot] = copy

    def place(chunk, half, value):
        slot = chunk % SLOTS
        for i in range(8):
            p = half * 8 + i
            block = value[i * 48 : (i + 1) * 48]
            for y in (0, 1):
                main = block[32 * y : 32 * y + 16].astype(bf16)
                rest = block[16 + 8 * y : 24 + 8 * y]
                rest = jnp.concatenate([rest[:, :HALF], rest[:, HALF:]], axis=0).astype(bf16)
                whole = jnp.concatenate([main, rest], axis=1)
                for n in range(PACK // 128):
                    r.packed[slot, p // 4, y, n, p % 4] = whole[:, n * 128 : (n + 1) * 128]

    def place_down(tile, value):
        for i in range(value.shape[0] // 16):
            owner, t = divmod(tile + i, 6)
            q, z, y = owner // 8, owner % 8 // 2, owner % 2
            block = value[i * 16 : (i + 1) * 16].astype(bf16)
            for n in range(6):
                chunk, col = divmod(t * 6 + n, PACK // 128)
                r.packed[4 + chunk, q, y, col, z] = block[:, n * 128 : (n + 1) * 128]

    def put_part(chunk, make, targets):
        if not shared:
            for half in (0, 1):
                value = make(half)
                for n, target in enumerate(targets):
                    wide = D // len(targets)
                    rows = pl.ds(half * 384, 384)
                    put_out(value[:, n * wide : (n + 1) * wide], target.at[rows])
            return
        steps(8, chunk)
        if chunk >= SLOTS:
            scatter.free(chunk - SLOTS)
        for half in (0, 1):
            place(chunk, half, make(half))
        scatter.start(chunk)

    def finish(chunk):
        total = scatter.total(chunk)
        if 4 <= chunk < 8:
            for n in range(PACK // 128):
                t, col = divmod((chunk - 4) * (PACK // 128) + n, 6)
                r.gd[t * 16 : (t + 1) * 16, col * 128 : (col + 1) * 128] = total[n]
            return
        even = links.y == 0
        for n in range(6):
            rest = total[6 + n % 3][n // 3 * 8 : n // 3 * 8 + 8]
            upper, lower = total[n][0:8], total[n][8:16]
            if chunk < 4:
                target, first = r.gu, chunk * D + n * 128
            elif chunk == 8:
                target, first = r.go, n * 128
            else:
                target, first = r.gj, n // 2 * D + (chunk - 9) * 256 + n % 2 * 128
            cols = slice(first, first + 128)
            target[0:8, cols] = jnp.where(even, upper, rest)
            target[8:16, cols] = jnp.where(even, lower, upper)
            target[16:24, cols] = jnp.where(even, rest, lower)

    def steps(*key):
        if shared:
            for stage, chunk in BACKWARD_PLAN.get(key, ()):
                if stage is None:
                    finish(chunk)
                elif chunk < CHUNKS:
                    stage(scatter, chunk)
                else:
                    stage(small, 0)

    def steps_at(now, count, *key):
        for place in range(count if shared else 0):
            if (*key, place) in BACKWARD_PLAN:

                @pl.when(now == place)
                def _(place=place):
                    steps(*key, place)

    def add_row(row, cols, value):
        r.vec_grad[row : row + 1, cols] += jnp.sum(value, axis=0, keepdims=True)

    for i in range(SEQ // 128):
        rows = slice(i * 128, (i + 1) * 128)
        seed = masked(r.cot, rows, i * 128, 128, length) * factor
        top = (r.depth[HIST] * seed).astype(bf16)
        r.low[rows, :] = top
        add_row(DOWN_BIAS, slice(0, D), top.astype(f32))

    ready("slope", *range(6))

    def up_low(i, carry):
        cols = at((i % 4) * D, D)
        rows = at((i // 4) * 512, 512)
        back = dot(r.low[rows, :], r.lower[pl.ds((i % 4) * 4, 4)].reshape(D, D), 1, 1)
        out = (back * r.slope[rows, cols].astype(f32)).astype(bf16)
        r.slope[rows, cols] = out
        add_row(UP_BIAS, cols, out.astype(f32))
        steps_at(i, 8, 0)
        return carry

    lax.fori_loop(0, 8, up_low, 0)
    load("joint", r.parts_in.at[pl.ds(0, 4)], r.lower.reshape(4, 16, 3, 16, D))

    ready("n2")
    for n in range(4):
        put_part(
            n,
            lambda half, n=n: dot(
                r.n2[:, half * 384 : half * 384 + 384], r.slope[:, n * D : (n + 1) * D], 0, 0
            ),
            None if shared else [r.gu.at[:, pl.ds(n * D, D)]],
        )
        steps(1, n)

    ready("hidden")
    for n in range(6):
        value = dot(r.hidden[n // 2, :, n % 2 * 512 : n % 2 * 512 + 512], r.low[...], 0, 0)
        if shared:
            place_down(n * 32, value)
        else:
            put_out(value, r.gd.at[pl.ds(n * 512, 512)])
        steps(9, n)
    for chunk in range(4, 8 if shared else 4):
        scatter.start(chunk)

    ready("upper", "middle")
    def second_norm(i, carry):
        rows = at(i * 256, 256)
        back = jnp.zeros((256, D), f32)
        for n in range(4):
            back = back + dot(r.slope[rows, n * D : (n + 1) * D], weight(r.upper, n), 1, 1)
        unit, scale = normalize(r.middle[rows, :])
        add_row(GAIN_2, slice(0, D), back * unit)
        add_row(SHIFT_2, slice(0, D), back)
        back = back * r.vec[GAIN_2 : GAIN_2 + 1, :D]
        along = jnp.mean(back * unit, axis=-1, keepdims=True)
        across = jnp.mean(back, axis=-1, keepdims=True)
        seed = masked(r.cot, rows, i * 256, 256, length) * factor
        out = r.depth[HIST] * seed + scale * (back - across - unit * along)
        r.middle[rows, :] = out
        out_low = out.astype(bf16)
        r.low[rows, :] = out_low
        add_row(OUTPUT_BIAS, slice(0, D), out_low.astype(f32))
        steps_at(i, 4, 2)
        return carry

    lax.fori_loop(0, SEQ // 256, second_norm, 0)

    ready("heads", "joint")
    put_part(
        8,
        lambda half: dot(r.heads[half * 384 : half * 384 + 384, :], r.low[...]),
        None if shared else [r.go],
    )
    steps(3, 0)

    def heads_back(i, carry):
        rows = at(i * 256, 256)
        flat = r.lower.reshape(3072 // 16, 16, D)[pl.ds(144 + i * 16, 16)].reshape(256, D)
        back = dot(flat, r.low[...], 1, 1).astype(bf16)
        r.grad[at(i * 4, 4, 4), 0:64, :] = back.reshape(4, 64, SEQ)
        product = back.astype(f32) * r.heads[rows, :].astype(f32)
        for h in range(4):
            total = jnp.sum(product[h * 64 : (h + 1) * 64], axis=0, keepdims=True)
            r.grad[i * 4 + h, 64:80, :] = tail(split_three(-total), SEQ)
        steps_at(i, 3, 4)
        return carry

    lax.fori_loop(0, 3, heads_back, 0)

    ready("k", "q", "v", "normed")
    load("x", r.x_in, r.n2)
    diagonal = causal()

    def turn_back(value):
        upper, lower = value[:32], value[32:]
        cosine, sine = r.cos[...], r.sin[...]
        return jnp.concatenate(
            [upper * cosine + lower * sine, lower * cosine - upper * sine], axis=0
        ).astype(bf16)

    def joint_part(part):
        put_part(
            9 + part,
            lambda half: dot(
                r.normed[half * 384 : half * 384 + 384, :], r.hidden[part, 0:D, :], 1, 1
            ),
            None if shared else [r.gj.at[:, pl.ds(n * D + part * 256, 256)] for n in range(3)],
        )
        sums = jnp.sum(r.hidden[part, 0:D, :].astype(f32), axis=1, keepdims=True)
        sums = jnp.broadcast_to(sums, (D, 8)).T
        for n in range(3):
            first = n * D + part * 256
            r.vec_grad[JOINT_BIAS : JOINT_BIAS + 1, first : first + 256] = sums[
                0:1, n * 256 : (n + 1) * 256
            ]

    def one_head(h, carry):
        keys = r.k[h].T
        values = r.v[h].T
        group = h // 4
        query_rows, key_rows, value_rows = (at(n * 256 + h % 4 * 64, 64, 64) for n in range(3))
        query_grad = jnp.zeros((64, SEQ), f32)
        key_grads = []
        for j in range(SEQ // QB):
            here = slice(j * QB, (j + 1) * QB)
            scores = dot(keys[here], r.q[h, :, j * QB :])
            probs = jnp.exp(scores)
            front = jnp.where(diagonal, probs[:, :QB], 0.0)
            probs = jnp.concatenate([front, probs[:, QB:]], axis=1) if j < 3 else front
            probs_grad = dot(values[here], r.grad[h, :, j * QB :])
            scores_low = (probs * probs_grad).astype(bf16)
            value_grad = dot(r.grad[h, 0:64, j * QB :], probs.astype(bf16), 1, 1)
            r.hidden[group, value_rows, here] = value_grad.astype(bf16)
            key_grads.append(dot(r.q[h, 0:64, j * QB :], scores_low, 1, 1))
            step = dot(r.k[h, 0:64, here], scores_low)
            if j:
                step = jnp.concatenate([jnp.zeros((64, j * QB), f32), step], axis=1)
            query_grad = query_grad + step
        r.hidden[group, query_rows, :] = turn_back(query_grad * 0.125)
        r.hidden[group, key_rows, :] = turn_back(jnp.concatenate(key_grads, axis=1))
        if shared:
            for n in range(3):

                @pl.when(h == n * 4 + 3)
                def _(n=n):
                    joint_part(n)

        steps_at(h, HEADS, 5)
        return carry

    lax.fori_loop(0, HEADS, one_head, 0)
    if not shared:
        for part in range(3):
            joint_part(part)

    ready("x")

    def first_norm(i, carry):
        rows = at(i * 256, 256)
        back = jnp.zeros((256, D), f32)
        for part in range(3):
            flat = r.hidden[part, 0:D, rows].T
            joint = r.lower.reshape(4, 16, 3, 16, D)[part].reshape(D, D)
            back = back + dot(flat, joint, 1, 1)
        unit, scale = normalize(r.n2[rows, :].astype(f32))
        add_row(GAIN_1, slice(0, D), back * unit)
        add_row(SHIFT_1, slice(0, D), back)
        back = back * r.vec[GAIN_1 : GAIN_1 + 1, :D]
        along = jnp.mean(back * unit, axis=-1, keepdims=True)
        across = jnp.mean(back, axis=-1, keepdims=True)
        r.middle[rows, :] = r.middle[rows, :] + scale * (back - across - unit * along)
        steps_at(i, 4, 6)
        return carry

    lax.fori_loop(0, SEQ // 256, first_norm, 0)
    last = pltpu.make_async_copy(r.middle, r.input_grad, r.save_sem.at[0])
    last.start()
    if shared:
        cut_vectors(r.vec_grad, r.maps, r.pieces)
        lane = lax.broadcasted_iota(jnp.int32, (1, 128), 1)
        row = jnp.zeros((1, 128), f32)
        for j in range(HIST + 1):
            total = jnp.sum(r.depth_rows[j : j + 1, :], axis=1, keepdims=True)
            row = jnp.where(lane == j, total, row)
        r.pieces[pl.ds(8, 32, stride=16), :] = jnp.broadcast_to(row, (32, 128))
        for i in range(7):
            r.pieces[pl.ds(9 + i, 32, stride=16), :] = jnp.zeros((32, 128), f32)
        r.vec_packed[0] = r.pieces[...].reshape(4, 2, 1, 4, 16, 128)
        small.start(0)
        steps(7, 0)
        r.pieces_out[...] = small.total(0)[0]
        links.finish()
    for copy in waiting.values():
        copy.wait()
    last.wait()


def backward_shared(
    length, depth, x_in, cot, cos, sin, vec, depth_rows, maps, normed_in, q_in, k_in, v_in, heads_in,
    middle_in, n2_in, hidden_in, slope_in, parts_in, down_in, input_grad, gj, go, gu, gd, pieces_out, upper,
    lower, normed, q, k, v, heads, middle, n2, hidden, slope, low, grad, load_sem, save_sem, packed, near,
    one, two, three, pieces, vec_packed, vec_near, vec_one, vec_two, vec_three, vec_grad, send_sem, recv_sem,
    credit,
):
    backward_steps(types.SimpleNamespace(**locals()), True)


def backward_alone(
    length, depth, x_in, cot, cos, sin, vec, depth_rows, maps, normed_in, q_in, k_in, v_in, heads_in,
    middle_in, n2_in, hidden_in, slope_in, parts_in, down_in, input_grad, gj, go, gu, gd, vec_grad, upper,
    lower, normed, q, k, v, heads, middle, n2, hidden, slope, low, grad, load_sem, save_sem, stage, stage_sem,
):
    backward_steps(types.SimpleNamespace(**locals()), False)


def backward(common, saved, shared):
    dma = pltpu.SemaphoreType.DMA
    local_sizes = SAVED[:9]
    scratch = [
        vmem((4, 16, 3, 16, D)),
        vmem((16, 2, 96, D)),
        *(vmem(s.shape, s.dtype) for s in local_sizes),
        vmem((SEQ, D)),
        vmem(LIFTED),
        *(dma((20,)), dma((1,))),
    ]
    if shared:
        outs = [(24, 3 * D), (24, D), (24, FF), (96, D), (16, 128)]
        scratch += [
            vmem((SLOTS, 4, 2, PACK // 128, 4, 16, 128)),
            vmem((NEAR, 2, 2, PACK // 128, 4, 16, 128)),
            vmem((CHUNKS, 2, PACK // 128, 4, 16, 128)),
            vmem((CHUNKS, PACK // 128, 4, 16, 128)),
            vmem((CHUNKS, 3, PACK // 128, 16, 128)),
            vmem((512, 128), f32),
            vmem((1, 4, 2, 1, 4, 16, 128), f32),
            vmem((1, 2, 2, 1, 4, 16, 128), f32),
            vmem((1, 2, 1, 4, 16, 128), f32),
            vmem((1, 1, 4, 16, 128), f32),
            vmem((1, 3, 1, 16, 128), f32),
            vmem((8, FF), f32),
            *(dma((CHUNKS * 4 + 4,)), dma((CHUNKS * 4 + 4,))),
            pltpu.SemaphoreType.REGULAR,
        ]
    else:
        outs = [(D, 3 * D), (D, D), (D, FF), (FF, D), (8, FF)]
        scratch += [vmem((2, 512, D), f32), dma((2,))]
    return pl.pallas_call(
        backward_shared if shared else backward_alone,
        name="backward_block",
        out_shape=[shape((SEQ, D), f32), *(shape(dims, f32) for dims in outs)],
        in_specs=[SM, SM, ANY] + [VM] * 6 + [ANY] * len(SAVED),
        out_specs=[ANY] + ([VM] * 5 if shared else [ANY] * 4 + [VM]),
        scratch_shapes=scratch,
        compiler_params=pltpu.CompilerParams(
            vmem_limit_bytes=64 << 20,
            collective_id=1 if shared else None,
            has_side_effects=shared,
        ),
    )(*common, *saved)


def results(length, depth, vec, cot, pieces, *refs):
    sources, targets, history_grad, rest = refs[:6], refs[6:12], refs[12], refs[13:]
    vectors, held, (stage, in_sem, out_sem, stage_sem) = rest[:-10], rest[-10:-4], rest[-4:]
    inward = [
        pltpu.make_async_copy(source, place, in_sem.at[i])
        for i, (source, place) in enumerate(zip(sources, held))
    ]
    outward = [
        pltpu.make_async_copy(place, target, out_sem.at[i])
        for i, (place, target) in enumerate(zip(held, targets))
    ]
    for copy in inward:
        copy.start()
    for i, vector in enumerate(vectors):
        vector[...] = pieces[i : i + 1, : vector.shape[1]]
    factor = vec[8:9, :D]
    waiting = {}
    for i in range(SEQ // 128):
        slot = i % 2
        if slot in waiting:
            waiting.pop(slot).wait()
        seed = masked(cot, slice(i * 128, (i + 1) * 128), i * 128, 128, length[0]) * factor
        for j in range(HIST):
            stage[slot, j] = depth[j] * seed
        target = history_grad.at[:, pl.ds(i * 128, 128)]
        waiting[slot] = pltpu.make_async_copy(stage.at[slot], target, stage_sem.at[slot])
        waiting[slot].start()
        if i == 3:
            for copy, onward in zip(inward, outward):
                copy.wait()
                onward.start()
    for copy in [*waiting.values(), *outward]:
        copy.wait()


def write_results(length, depth, vec, cot, pieces, arrays, sizes):
    dma = pltpu.SemaphoreType.DMA
    outs = [shape(a.shape, a.dtype) for a in arrays]
    return pl.pallas_call(
        results,
        out_shape=[
            *(*outs, shape((HIST, SEQ, D), f32)),
            *(shape((1, size), f32) for size in sizes),
        ],
        in_specs=[SM, SM, VM, VM, VM] + [ANY] * 6,
        out_specs=[ANY] * 7 + [VM] * len(sizes),
        scratch_shapes=[
            *(vmem(s.shape, s.dtype) for s in outs),
            *(vmem((2, HIST, 128, D), f32), dma((6,)), dma((6,)), dma((2,))),
        ],
        compiler_params=pltpu.CompilerParams(vmem_limit_bytes=62 << 20),
    )(length, depth, vec, cot, pieces, *arrays)


def turning_tables():
    half = HEAD_DIM // 2
    frequency = np.power(10000.0, np.arange(half, dtype=np.float64) * (-2.0 / HEAD_DIM))
    angles = frequency[:, None] * np.arange(SEQ, dtype=np.float64)[None, :]
    return np.cos(angles).astype(np.float32), np.sin(angles).astype(np.float32)


def lane_maps():
    maps = np.full((8, FF), -1, np.int32)
    for row, size in ((0, 24), (2, 72), (4, 96)):
        lanes = np.arange(32 * size)
        maps[row, : 32 * size] = lanes // size
        maps[row + 1, : 32 * size] = lanes % size
    return maps


def local(
    inputs,
    history,
    cotangent,
    lengths,
    joint_weight,
    joint_bias,
    output_weight,
    output_bias,
    first_gain,
    first_shift,
    second_gain,
    second_shift,
    upward_weight,
    upward_bias,
    downward_weight,
    downward_bias,
    depth_weights,
):
    devices = lax.axis_size(AXES)
    shared = (lax.axis_size("dp"), lax.axis_size("fsdp")) == (4, 8)
    vectors = (
        joint_bias,
        output_bias,
        first_gain,
        first_shift,
        second_gain,
        second_shift,
        upward_bias,
        downward_bias,
    )
    sizes = [vector.shape[0] for vector in vectors]
    shards = (joint_weight, output_weight, upward_weight, downward_weight)
    x, cot = inputs[0], cotangent[0]
    cosine, sine = turning_tables()
    maps = lane_maps()
    common = (lengths, depth_weights, x, cot, cosine, sine)
    if shared:
        piece = jnp.zeros(16 * 128, f32)
        for i, v in enumerate((*vectors, lengths)):
            after = (15 - i) * 128 + 128 - v.shape[0]
            piece = piece + lax.pad(v.astype(f32), jnp.float32(0), [(i * 128, after, 0)])
        piece = piece.reshape(16, 128)
        special = (maps, piece, *shards)
    else:
        piece = jnp.concatenate([v.astype(f32) for v in (*vectors, lengths)])
        pieces = lax.all_gather(piece, AXES, axis=0, tiled=False).reshape(devices, -1)
        rows, start = [], 0
        for size in sizes:
            row = pieces[:, start : start + size].reshape(1, -1)
            rows.append(jnp.pad(row, ((0, 0), (0, FF - row.shape[1]))))
            start += size
        count = jnp.sum(pieces[:, start:])
        vec = jnp.concatenate([*rows, jnp.full((8, FF), devices * SEQ / count, f32)])
        full = [lax.all_gather(w, AXES, axis=0, tiled=True) for w in shards]
        special = (
            vec,
            *(w.reshape(16, 3, 16, -1) for w in full[:3]),
            full[3].reshape(16, 2, 96, D),
        )
    layer, *saved, vec, depth_rows = forward((*common, history), special, shared)
    input_grad, *grads, vec_grads = backward(
        (*common, vec, depth_rows, maps), saved, shared
    )
    if shared:
        arrays = (layer, input_grad, *grads)
        written = write_results(
            lengths, depth_weights, vec, cot, vec_grads, arrays, [*sizes, HIST + 1]
        )
        layer, input_grad, *grads, history_grad = written[:7]
        outs = [row[0] for row in written[7:]]
        return (
            *(layer[None], input_grad[None], history_grad[:, None]),
            *(grads[0], outs[0], grads[1]),
            *(*outs[1:6], grads[2], outs[6], grads[3], outs[7], outs[8]),
        )
    factor = vec[8, 0]
    positions = jnp.arange(SEQ, dtype=jnp.int32)
    seed = jnp.where(positions[:, None] < lengths[0], cot.astype(f32), 0.0) * factor
    history_gradient = depth_weights[:HIST, None, None, None] * seed[None, None]
    depth_terms = jnp.sum(depth_rows[: HIST + 1], axis=1)
    grads = [lax.psum_scatter(g, AXES, scatter_dimension=0, tiled=True) for g in grads]
    cols = [vec_grads[i, : size * devices].reshape(devices, size) for i, size in enumerate(sizes)]
    cols.append(jnp.broadcast_to(depth_terms[None], (devices, HIST + 1)))
    total = lax.psum_scatter(
        jnp.concatenate(cols, axis=1), AXES, scatter_dimension=0, tiled=False
    )
    outs, start = [], 0
    for size in [*sizes, HIST + 1]:
        outs.append(total[start : start + size])
        start += size
    return (
        layer[None],
        input_grad[None],
        history_gradient,
        grads[0],
        outs[0],
        grads[1],
        *outs[1:6],
        grads[2],
        outs[6],
        grads[3],
        outs[7],
        outs[8],
    )


def solution(mesh):
    row, vector = P(AXES, None), P(AXES)
    tokens, levels = P(AXES, None, None), P(None, AXES, None, None)
    return jax.shard_map(
        local,
        mesh=mesh,
        in_specs=(
            *(tokens, levels, tokens, vector),
            *(row, vector, row, vector),
            *(vector, vector, vector, vector),
            *(row, vector, row, vector, P()),
        ),
        out_specs=(
            *(tokens, tokens, levels),
            *(row, vector, row, vector),
            *(vector, vector, vector, vector),
            *(row, vector, row, vector, P()),
        ),
        check_vma=False,
    )
```

```python
import functools
import math
import types

import jax
import jax.numpy as jnp
import numpy as np
from jax import lax
from jax.experimental import pallas as pl
from jax.experimental.pallas import tpu as pltpu
from jax.sharding import PartitionSpec as P

D = 768
HEADS = 12
HEAD_DIM = 64
FF = 3072
SEQ = 1024
HIST = 4
AXES = ("dp", "fsdp")
EPS = 1e-05
NEG = -1e30
LIFT = 80
QB = 256
C0 = math.sqrt(2.0 / math.pi)
C1 = 0.044715

f32 = jnp.float32
bf16 = jnp.bfloat16
ANY = pl.BlockSpec(memory_space=pl.ANY)
VM = pl.BlockSpec(memory_space=pltpu.VMEM)
SM = pl.BlockSpec(memory_space=pltpu.SMEM)

MESH = pl.DeviceIdType.MESH
HALF = D // 2
PACK = D + HALF
PARTS = 8
CHUNKS = 12
SLOTS = 8
NEAR = 4

JOINT_BIAS, OUTPUT_BIAS, GAIN_1, SHIFT_1, GAIN_2, SHIFT_2, UP_BIAS, DOWN_BIAS = range(8)


def dot(left, right, left_dim=1, right_dim=0):
    return lax.dot_general(
        left, right, (((left_dim,), (right_dim,)), ((), ())), preferred_element_type=f32
    )


def at(start, size, unit=128):
    return pl.ds(pl.multiple_of(start, unit), size)


def normalize(values):
    mean = jnp.mean(values, axis=-1, keepdims=True)
    centred = values - mean
    variance = jnp.mean(centred * centred, axis=-1, keepdims=True)
    scale = lax.rsqrt(variance + EPS)
    return centred * scale, scale


def fold(values):
    rows, cols = values.shape
    return jnp.sum(values.reshape(rows // 8, 8, cols), axis=0)


def split_three(row):
    high = row.astype(bf16).astype(f32)
    rest = row - high
    mid = rest.astype(bf16).astype(f32)
    return high, mid, rest - mid


def tail(rows, width):
    index = lax.broadcasted_iota(jnp.int32, (16, width), 0)
    out = jnp.zeros((16, width), f32)
    for place, row in enumerate(rows):
        out = jnp.where(index == place, row, out)
    return out.astype(bf16)


def position():
    dp, fsdp = lax.axis_index("dp"), lax.axis_index("fsdp")
    return dp // 2, dp % 2, fsdp // 2, fsdp % 2


def device(x, c, z, y):
    return (x * 2 + c, z * 2 + y)


class Links:
    def __init__(self, send_sem, recv_sem, *rulers):
        x, c, z, y = position()
        self.send_sem, self.recv_sem = send_sem, recv_sem
        self.rulers = {jnp.dtype(ruler.dtype): ruler for ruler in rulers}
        self.x, self.c, self.z, self.y = x, c, z, y
        self.nx, self.nc, self.ny = 1 - x, 1 - c, 1 - y
        self.zs = (z + 1 - 2 * (z % 2), (z + 2) % 4, 3 - z)
        self.q, self.r = x * 2 + c, (1 - x) * 2 + c
        self.other_x = device(1 - x, c, z, y)
        self.other_y = device(x, c, z, 1 - y)
        self.other_c = device(x, 1 - c, z, y)
        self.along_z = [device(x, c, other, y) for other in self.zs]
        self.sent = {}

    def greet(self):
        barrier = pltpu.get_barrier_semaphore()
        peers = [self.other_x, self.other_y, self.other_c, *self.along_z]
        for peer in peers:
            pl.semaphore_signal(barrier, inc=1, device_id=peer, device_id_type=MESH)
        pl.semaphore_wait(barrier, len(peers))

    def copy(self, source, target, sem, peer):
        return pltpu.make_async_remote_copy(
            src_ref=source,
            dst_ref=target,
            send_sem=self.send_sem.at[sem],
            recv_sem=self.recv_sem.at[sem],
            device_id=peer,
            device_id_type=MESH,
        )

    def send(self, pairs, sem, peer):
        for source, target in pairs():
            self.copy(source, target, sem, peer).start()
        self.sent.setdefault(sem, []).append(pairs)

    def whole(self, refs, sem):
        size = sum(math.prod(ref.shape) for ref in refs)
        ruler = self.rulers[jnp.dtype(refs[0].dtype)]
        rows = 16
        while size % (rows * 128) or size // rows > ruler.shape[1]:
            rows += 16
        part = ruler.at[pl.ds(0, rows), pl.ds(0, size // rows)]
        return self.copy(part, part, sem, self.other_c)

    def arrived(self, targets, sem):
        self.whole(targets, sem).wait_recv()

    def left(self, sem):
        sources = [pair[0] for pairs in self.sent.pop(sem, []) for pair in pairs()]
        if sources:
            self.whole(sources, sem).wait_send()

    def finish(self):
        for sem in list(self.sent):
            self.left(sem)


DOWN = (PARTS, PARTS + 1)
VECTORS = PARTS + 2
WIDE = 512


class Gather:
    def __init__(self, links, parts, rests, down, pieces):
        self.links = links
        self.parts, self.rests, self.down, self.pieces = parts, rests, down, pieces

    def refs(self, item, q, y, z, color):
        if item == VECTORS:
            if color == 1:
                return []
            first = (q * 8 + y * 4 + (0 if z is None else z)) * 16
            return [self.pieces.at[at(first, 64 if z is None else 16, 16)]]
        rows = pl.ds(q * 4, 4) if z is None else q * 4 + z
        if item in DOWN:
            first, last = (0, 4) if item == PARTS else (4, 6)
            mid = (first + last) // 2
            first, last = {None: (first, last), 0: (first, mid), 1: (mid, last)}[color]
            return [self.down.at[rows, y, pl.ds(first, last - first)]]
        wide = {None: pl.ds(0, D), 0: pl.ds(0, HALF), 1: pl.ds(HALF, HALF)}[color]
        cut = 2 if item % 2 else 1
        narrow = {None: pl.ds(0, 3), 0: pl.ds(0, cut), 1: pl.ds(cut, 3 - cut)}[color]
        some = pl.ds(0, 4) if z is None else z
        return [
            self.parts.at[item, rows, 2 * y, :, wide],
            self.rests.at[item, q, y, narrow, some],
        ]

    def send(self, item, stage, peer, quads, z=None):
        def pairs():
            refs = []
            for q, y, color in quads:
                refs += self.refs(item, getattr(self.links, q), getattr(self.links, y), z, color)
            return [(ref, ref) for ref in refs]

        self.links.send(pairs, item * 4 + stage, peer)

    def start(self, item):
        links = self.links
        if item in DOWN:
            self.send(item, 0, links.other_x, [("q", "y", 0)], links.z)
            self.send(item, 0, links.other_y, [("q", "y", 1)], links.z)
            return
        for peer in links.along_z:
            self.send(item, 0, peer, [("q", "y", None)], links.z)

    def second(self, item):
        links = self.links
        if item in DOWN:
            refs = self.refs(item, links.r, links.y, links.z, 0)
            links.arrived(refs + self.refs(item, links.q, links.ny, links.z, 1), item * 4)
            quads = [("q", "y", 0), ("r", "y", 0), ("q", "y", 1), ("q", "ny", 1)]
            for peer in links.along_z:
                self.send(item, 1, peer, quads, links.z)
            return
        refs = [self.refs(item, links.q, links.y, z, None) for z in links.zs]
        links.arrived(sum(refs, []), item * 4)
        self.send(item, 1, links.other_x, [("q", "y", 0)])
        self.send(item, 1, links.other_y, [("q", "y", 1)])

    def third(self, item):
        links = self.links
        if item in DOWN:
            quads = [(links.q, links.y, 0), (links.r, links.y, 0)]
            quads += [(links.q, links.y, 1), (links.q, links.ny, 1)]
            refs = [self.refs(item, q, y, z, k) for q, y, k in quads for z in links.zs]
            links.arrived(sum(refs, []), item * 4 + 1)
        else:
            refs = self.refs(item, links.r, links.y, None, 0)
            links.arrived(refs + self.refs(item, links.q, links.ny, None, 1), item * 4 + 1)
        first = [("q", "y", 0), ("r", "y", 0)]
        second = [("q", "y", 1), ("q", "ny", 1)]
        self.send(item, 2, links.other_y, first)
        self.send(item, 2, links.other_x, second)
        self.send(item, 3, links.other_c, first + second)

    def fourth(self, item):
        links = self.links
        quads = [("q", "ny", 0), ("r", "ny", 0), ("r", "y", 1), ("r", "ny", 1)]
        refs = [self.refs(item, getattr(links, q), getattr(links, y), None, k) for q, y, k in quads]
        links.arrived(sum(refs, []), item * 4 + 2)
        self.send(item, 3, links.other_c, quads)

    def ready(self, item):
        links = self.links
        refs = []
        for xx in (0, 1):
            for yy in (0, 1):
                for color in (0, 1):
                    refs += self.refs(item, xx * 2 + links.nc, yy, None, color)
        links.arrived(refs, item * 4 + 3)
        if item < PARTS:

            def merge(p, carry):
                q, z = p // 4, p % 4
                for i in range(3):
                    even = self.rests[item, q, 0, i, z].astype(f32)
                    odd = self.rests[item, q, 1, i, z].astype(f32)
                    for k in (0, 1):
                        first = k * HALF + i * 128
                        half = slice(k * 8, k * 8 + 8)
                        self.parts[item, p, 1, :, first : first + 128] = jnp.concatenate(
                            [even[half], odd[half]], axis=0
                        ).astype(bf16)
                return carry

            lax.fori_loop(0, 16, merge, 0)

    def own(self, item, shard):
        links = self.links
        full = shard.astype(f32)
        even = links.y == 0
        main = jnp.where(even, full[0:16], full[8:24])
        rest = jnp.where(even, full[16:24], full[0:8])
        self.parts[item, links.q * 4 + links.z, 2 * links.y] = main.astype(bf16)
        for i in range(3):
            left, right = rest[:, i * 128 : (i + 1) * 128], rest[:, HALF + i * 128 :][:, :128]
            self.rests[item, links.q, links.y, i, links.z] = jnp.concatenate(
                [left, right], axis=0
            ).astype(bf16)


def block_order():
    index = lax.broadcasted_iota(jnp.int32, (32, 1), 0)
    return (index & 24) + (index & 3) * 2 + ((index >> 2) & 1)


def spread(maps_ref, size):
    row = {24: 0, 72: 2, 96: 4}[size]
    wide = 32 * size
    owner = maps_ref[row : row + 1, :wide] == block_order()
    lane = maps_ref[row + 1 : row + 2, :wide] == lax.broadcasted_iota(jnp.int32, (128, 1), 0)
    return owner, jnp.where(lane, 1.0, 0.0).astype(bf16)


VECTOR_SIZES = (72, 24, 24, 24, 24, 24, 96, 24)


def join_vectors(pieces_ref, maps_ref, vec_ref):
    for size in (24, 72, 96):
        owner, lane = spread(maps_ref, size)
        for row, own in enumerate(VECTOR_SIZES):
            if own == size:
                piece = pieces_ref[pl.ds(row, 32, stride=16), :].astype(bf16)
                full = jnp.where(owner, dot(piece, lane), 0.0)
                vec_ref[row : row + 1, : 32 * size] = jnp.sum(full, axis=0, keepdims=True)
    counts = pieces_ref[pl.ds(8, 32, stride=16), :]
    count = jnp.sum(jnp.sum(counts, axis=0, keepdims=True), axis=1, keepdims=True)
    vec_ref[8:16, :] = jnp.broadcast_to((32 * SEQ) / count, (8, FF))


def cut_vectors(vec_ref, maps_ref, pieces_ref):
    for size in (24, 72, 96):
        owner, lane = spread(maps_ref, size)
        for row, own in enumerate(VECTOR_SIZES):
            if own == size:
                full = jnp.where(owner, vec_ref[row : row + 1, : 32 * size], 0.0)
                high = full.astype(bf16)
                low = (full - high.astype(f32)).astype(bf16)
                pieces_ref[pl.ds(row, 32, stride=16), :] = dot(high, lane, 1, 1) + dot(
                    low, lane, 1, 1
                )


class Scatter:
    def __init__(self, links, base, credit, packed, near, one, two, three):
        self.links, self.base, self.credit = links, base, credit
        self.packed, self.near = packed, near
        self.one, self.two, self.three = one, two, three
        self.wide = packed.shape[3]

    def columns(self, chunk):
        mid = (self.wide + 1 - chunk % 2) // 2
        return pl.ds(0, mid), pl.ds(mid, self.wide - mid)

    def send(self, chunk, stage, peer, pairs, cols=None):
        if cols is None or cols.size:
            self.links.send(pairs, self.base + chunk * 4 + stage, peer)

    def start(self, chunk):
        links = self.links
        if self.credit is not None and chunk >= NEAR:
            pl.semaphore_wait(self.credit, 1)

        def pairs():
            return [
                (
                    self.packed.at[chunk % SLOTS, xx * 2 + links.nc],
                    self.near.at[chunk % NEAR, xx],
                )
                for xx in (0, 1)
            ]

        self.send(chunk, 0, links.other_c, pairs)

    def first(self, chunk):
        links = self.links
        slot, near = chunk % SLOTS, chunk % NEAR
        links.arrived([self.near.at[near, xx] for xx in (0, 1)], self.base + chunk * 4)

        def add(i, carry):
            xx, yy = i // 2, i % 2
            mine = self.packed[slot, xx * 2 + links.c, yy]
            self.packed[slot, xx * 2 + links.c, yy] = mine + self.near[near, xx, yy]
            return carry

        lax.fori_loop(0, 4, add, 0)
        if self.credit is not None and chunk + NEAR < CHUNKS:
            pl.semaphore_signal(self.credit, inc=1, device_id=links.other_c, device_id_type=MESH)
        here, there = self.columns(chunk)

        def by_y():
            return [
                (self.packed.at[slot, k * 2 + links.c, links.ny, here], self.one.at[chunk, k, here])
                for k in (0, 1)
            ]

        def by_x():
            return [
                (self.packed.at[slot, links.r, k, there], self.one.at[chunk, k, there])
                for k in (0, 1)
            ]

        self.send(chunk, 1, links.other_y, by_y, here)
        self.send(chunk, 1, links.other_x, by_x, there)

    def second(self, chunk):
        links = self.links
        slot = chunk % SLOTS
        links.arrived([self.one.at[chunk, k] for k in (0, 1)], self.base + chunk * 4 + 1)
        here, there = self.columns(chunk)
        for k in (0, 1):
            for cols, q, y in ((here, k * 2 + links.c, links.y), (there, links.q, k)):
                if cols.size:
                    mine = self.packed[slot, q, y, cols]
                    self.one[chunk, k, cols] = mine + self.one[chunk, k, cols]
        self.send(
            chunk,
            2,
            links.other_x,
            lambda: [(self.one.at[chunk, links.nx, here], self.two.at[chunk, here])],
            here,
        )
        self.send(
            chunk,
            2,
            links.other_y,
            lambda: [(self.one.at[chunk, links.ny, there], self.two.at[chunk, there])],
            there,
        )

    def third(self, chunk):
        links = self.links
        links.arrived([self.two.at[chunk]], self.base + chunk * 4 + 2)
        for cols, mine in zip(self.columns(chunk), (links.x, links.y)):
            if cols.size:
                self.two[chunk, cols] = self.one[chunk, mine, cols] + self.two[chunk, cols]
        for k in range(3):

            def pairs(k=k):
                return [(self.two.at[chunk, :, links.zs[k]], self.three.at[chunk, k])]

            self.send(chunk, 3, links.along_z[k], pairs)

    def total(self, chunk):
        links = self.links
        links.arrived([self.three.at[chunk, k] for k in range(3)], self.base + chunk * 4 + 3)
        parts = [self.two[chunk, :, links.z]] + [self.three[chunk, k] for k in range(3)]
        parts = [part.astype(f32) for part in parts]
        return (parts[0] + parts[1]) + (parts[2] + parts[3])

    def free(self, chunk):
        self.links.left(self.base + chunk * 4)
        self.links.left(self.base + chunk * 4 + 1)


def weight(parts_ref, item):
    return parts_ref[item].reshape(D, D)


def masked(cot_ref, rows, start, count, length):
    index = lax.broadcasted_iota(jnp.int32, (count, 1), 0) + start
    return jnp.where(index < length, cot_ref[rows, :].astype(f32), 0.0)


def causal():
    shape = (QB, QB)
    return lax.broadcasted_iota(jnp.int32, shape, 0) <= lax.broadcasted_iota(jnp.int32, shape, 1)


FORWARD_PLAN = {
    (0, 7): ((Gather.second, 10), (Gather.second, 8), (Gather.second, 9), (Gather.second, 0), (Gather.third, 10), (Gather.second, 1), (Gather.third, 0), (Gather.fourth, 10), (Gather.second, 2)),
    (1, 7): ((Gather.third, 1),),
    (2, 0, 0): ((Gather.second, 3), (Gather.fourth, 0), (Gather.third, 2), (Gather.second, 4)),
    (3, 1): ((Gather.fourth, 1), (Gather.second, 5)),
    (3, 2): ((Gather.third, 3),),
    (3, 3): ((Gather.second, 6), (Gather.fourth, 2)),
    (2, 1, 3): ((Gather.third, 4),),
    (3, 4): ((Gather.second, 7), (Gather.third, 5)),
    (3, 6): ((Gather.fourth, 3),),
    (3, 7): ((Gather.third, 6),),
    (3, 8): ((Gather.fourth, 4),),
    (3, 9): ((Gather.third, 7),),
    (3, 10): ((Gather.fourth, 5),),
    (5, 1): ((Gather.fourth, 6), (Gather.third, 8)),
    (6, 1): ((Gather.fourth, 7),),
    (6, 4): ((Gather.third, 9),),
    (6, 7): ((Gather.fourth, 8),),
    (7, 8): ((Gather.fourth, 9),),
}


def forward_steps(r, shared):
    length = r.length[0]
    hb = 128

    def hist_copy(step, slot):
        return pltpu.make_async_copy(
            r.history.at[:, 0, pl.ds(step * hb, hb)], r.hist.at[slot], r.hist_sem.at[slot]
        )

    first_loads = [
        pltpu.make_async_copy(r.cot_in, r.cot, r.load_sem.at[22]),
        pltpu.make_async_copy(r.x_in, r.x, r.load_sem.at[23]),
    ]
    first_loads[0].start()
    hist_copy(0, 0).start()
    hist_copy(1, 1).start()
    first_loads[1].start()
    if shared:
        links = Links(r.send_sem, r.recv_sem, r.hidden, r.earlier)
        gather = Gather(links, r.parts, r.rests, r.down, r.pieces)
        links.greet()
        place = (links.q * 8 + links.y * 4 + links.z) * 16
        r.pieces[at(place, 16, 16), :] = r.piece[...]
        gather.start(VECTORS)
        for part in range(3):
            own = [r.wj_in[:, i * D + part * 256 :][:, :256] for i in range(3)]
            gather.own(part, jnp.concatenate(own, axis=1))
            gather.start(part)
        gather.own(3, r.wo_in[...])
        gather.start(3)
        for part in range(4):
            gather.own(4 + part, r.wu_in[:, part * D : (part + 1) * D])
            gather.start(4 + part)
        for i in range(6):
            r.down[links.q * 4 + links.z, links.y, i] = r.wd_in[:, i * 128 : (i + 1) * 128]
        for item in DOWN:
            gather.start(item)
        ready = gather.ready
    else:
        plain = [(r.wo_in, 0)] + [(r.wu_in, n * D) for n in range(4)]
        pairs = [
            [
                (r.wj_in.at[:, :, :, pl.ds(i * D + g * 256, 256)], r.parts.at[g, :, :, :, pl.ds(i * 256, 256)])
                for i in range(3)
            ]
            for g in range(3)
        ]
        for n, (source, first) in enumerate(plain):
            pairs.append([(source.at[:, :, :, pl.ds(first, D)], r.parts.at[3 + n])])
        pairs.append(
            [(r.wd_in.at[:, :, :, pl.ds(i * 128, 128)], r.down.at[:, :, i]) for i in range(6)]
        )
        loads, used = [], 0
        for pair in pairs:
            loads.append([])
            for source, target in pair:
                loads[-1].append(pltpu.make_async_copy(source, target, r.load_sem.at[used]))
                loads[-1][-1].start()
                used += 1
        r.vec[...] = r.vec_in[...]

        def ready(item):
            if item != DOWN[1]:
                for load in loads[item]:
                    load.wait()

    def steps(*key):
        if shared:
            for stage, item in FORWARD_PLAN.get(key, ()):
                stage(gather, item)

    def steps_at(now, count, *key):
        for place in range(count if shared else 0):
            if (*key, place) in FORWARD_PLAN:

                @pl.when(now == place)
                def _(place=place):
                    steps(*key, place)

    r.depth_acc[...] = jnp.zeros_like(r.depth_acc)
    first_loads[0].wait()
    for step in range(SEQ // hb):
        slot = step % 2
        hist_copy(step, slot).wait()

        def part(i, carry, slot=slot, step=step):
            rows = pl.ds(pl.multiple_of(i * 32, 32), 32)
            here = pl.ds(pl.multiple_of(step * hb + i * 32, 32), 32)
            seed = masked(r.cot, here, step * hb + i * 32, 32, length)
            total = jnp.zeros((32, D), f32)
            for j in range(HIST):
                part_hist = r.hist[slot, j, rows, :].astype(f32)
                total = total + r.depth[j] * part_hist
                r.depth_acc[j] = r.depth_acc[j] + fold(seed * part_hist)
            r.earlier[here, :] = total
            return carry

        lax.fori_loop(0, hb // 32, part, 0)
        if step + 2 < SEQ // hb:
            hist_copy(step + 2, slot).start()
        steps(0, step)
    if shared:
        ready(VECTORS)
        join_vectors(r.pieces, r.maps, r.vec)
    factor = r.vec[8:9, :D]

    first_loads[1].wait()
    for i in range(SEQ // 128):
        rows = slice(i * 128, (i + 1) * 128)
        unit, _ = normalize(r.x[rows, :].astype(f32))
        full = unit * r.vec[GAIN_1 : GAIN_1 + 1, :D] + r.vec[SHIFT_1 : SHIFT_1 + 1, :D]
        r.normed[:, rows] = full.T.astype(bf16)
        steps(1, i)
    saves = []

    def save(source, target):
        copy = pltpu.make_async_copy(source, target, r.save_sem.at[len(saves)])
        copy.start()
        saves.append(copy)

    save(r.normed, r.normed_out)

    keys_at = lax.broadcasted_iota(jnp.int32, (1, SEQ), 1)
    key_bias = jnp.where(keys_at < length, 0.0, NEG)
    one = jnp.ones((1, SEQ), f32)
    bias_cols = r.vec[0:8, : 3 * D].T
    kinds = ((r.q, (one,)), (r.k, (key_bias, one, one, one)), (r.v, (one, one, one)))
    for target, rows in kinds:
        extra = tail(rows, SEQ)
        for h in range(HEADS):
            target[h, 64:80, :] = extra

    def four_heads(group):
        steps(2, group, 0)
        ready(group)
        for kind, (target, _) in enumerate(kinds):
            cols = slice(kind * 256, (kind + 1) * 256)
            joined = dot(r.parts[group, :, :, :, cols].reshape(D, 256), r.normed[...], 0, 0)
            first = kind * D + group * 256
            joined = joined + bias_cols[first : first + 256, 0:1]
            for h in range(4):
                upper = joined[h * 64 : h * 64 + 32]
                lower = joined[h * 64 + 32 : h * 64 + 64]
                if kind < 2:
                    cosine, sine = r.cos[...], r.sin[...]
                    upper, lower = upper * cosine - lower * sine, lower * cosine + upper * sine
                both = jnp.concatenate([upper, lower], axis=0).astype(bf16)
                if kind == 0:
                    both = both * jnp.asarray(0.125, bf16)
                target[group * 4 + h, 0:64, :] = both
            steps(2, group, kind + 1)

    diagonal = causal()

    def one_head(h, carry):
        for group in range(3):

            @pl.when(h == group * 4)
            def _(group=group):
                four_heads(group)

        keys, queries, values = r.k[h].T, r.q[h], r.v[h]
        outs, tails = [], []
        for i in range(SEQ // QB):
            cols = slice(i * QB, (i + 1) * QB)
            seen = (i + 1) * QB
            scores = dot(keys[:seen], queries[:, cols])
            last = jnp.where(diagonal, scores[seen - QB :], NEG)
            scores = jnp.concatenate([scores[: seen - QB], last], axis=0) if i else last
            top = jnp.max(scores, axis=0, keepdims=True)
            weights = jnp.exp(scores - top).astype(bf16)
            out = dot(values[:, :seen], weights)
            total = out[64:65]
            outs.append((out[:64] / total).astype(bf16))
            log_total = -(top + jnp.log(total))
            tails.append(tail((jnp.ones((1, QB), f32), *split_three(log_total)), QB))
        r.heads[at(h * 64, 64, 64), :] = jnp.concatenate(outs, axis=1)
        r.q[h, 64:80, :] = jnp.concatenate(tails, axis=1)
        steps_at(h, HEADS, 3)
        return carry

    lax.fori_loop(0, HEADS, one_head, 0)
    save(r.parts.at[pl.ds(0, 3)], r.parts_out.at[pl.ds(0, 3)])
    save(r.q, r.q_out)
    save(r.k, r.k_out)
    save(r.v, r.v_out)
    save(r.heads, r.heads_out)

    steps(4, 0)
    ready(3)

    def project(i, carry):
        rows = at(i * 256, 256)
        out = dot(r.heads[:, rows], weight(r.parts, 3), 0, 0)
        mid = r.x[rows, :].astype(f32) + (out + r.vec[OUTPUT_BIAS : OUTPUT_BIAS + 1, :D])
        r.middle[rows, :] = mid
        unit, _ = normalize(mid)
        r.n2[rows, :] = (
            unit * r.vec[GAIN_2 : GAIN_2 + 1, :D] + r.vec[SHIFT_2 : SHIFT_2 + 1, :D]
        ).astype(bf16)
        steps_at(i, 4, 5)
        return carry

    lax.fori_loop(0, SEQ // 256, project, 0)
    save(r.middle, r.middle_out)
    save(r.n2, r.n2_out)
    def upward(i, carry):
        steps_at(i, 8, 6)
        for n in range(4):

            @pl.when(i == n)
            def _(n=n):
                ready(4 + n)

        rows = at((i // 4) * 512, 512)
        cols = at((i % 4) * D, D)
        up = dot(r.n2[rows, :], weight(r.parts, 4 + i % 4))
        up = up + r.vec[UP_BIAS : UP_BIAS + 1, cols]
        square = up * up
        turn = jnp.tanh(up * (C0 + (C0 * C1) * square))
        half = 0.5 + 0.5 * turn
        r.hidden[rows, cols] = (up * half).astype(bf16)
        bent = (2.0 * up) * (C0 + (3.0 * C0 * C1) * square)
        r.slope[rows, cols] = (half + bent * (half * (1.0 - half))).astype(bf16)
        return carry

    lax.fori_loop(0, 8, upward, 0)
    save(r.parts.at[pl.ds(3, 5)], r.parts_out.at[pl.ds(3, 5)])
    save(r.slope, r.slope_out)
    for n in range(3):
        save(r.hidden.at[:, pl.ds(n * SEQ, SEQ)], r.hidden_out.at[n])

    def downward(cols, i, carry):
        rows = at(i * 256, 256)
        blocks = range(cols.start // 128, cols.stop // 128)
        down = [r.down[:, :, n].reshape(FF, 128) for n in blocks]
        out = dot(r.hidden[rows, :], jnp.concatenate(down, axis=1))
        block = r.middle[rows, cols] + (out + r.vec[DOWN_BIAS : DOWN_BIAS + 1, cols])
        r.layer[rows, cols] = (r.earlier[rows, cols] + r.depth[HIST] * block).astype(bf16)
        index = lax.broadcasted_iota(jnp.int32, (256, 1), 0) + i * 256
        seed = jnp.where(index < length, r.cot[rows, cols].astype(f32), 0.0)
        r.depth_acc[HIST, :, cols] = r.depth_acc[HIST, :, cols] + fold(seed * block)
        steps_at(i, 4, 8, cols.start)
        return carry

    for item in DOWN:
        steps(7, item)
        ready(item)
        cols = slice(0, WIDE) if item == PARTS else slice(WIDE, D)
        blocks = pl.ds(cols.start // 128, (cols.stop - cols.start) // 128)
        save(r.down.at[:, :, blocks], r.down_out.at[:, :, blocks])
        lax.fori_loop(0, SEQ // 256, functools.partial(downward, cols), 0)
    save(r.layer, r.layer_out)
    r.depth_out[...] = jnp.zeros_like(r.depth_out)
    for j in range(HIST + 1):
        r.depth_out[j : j + 1, :] = jnp.sum(r.depth_acc[j], axis=0, keepdims=True) * factor
    if shared:
        links.finish()
    for copy in saves:
        copy.wait()


def forward_shared(
    length, depth, x_in, cot_in, cos, sin, history, maps, piece, wj_in, wo_in, wu_in, wd_in, layer_out, normed_out,
    q_out, k_out, v_out, heads_out, middle_out, n2_out, hidden_out, slope_out, parts_out, down_out, vec,
    depth_out, x, cot, parts, down, hist, earlier, normed, q, k, v, heads, middle, n2, hidden, slope, layer,
    depth_acc, load_sem, hist_sem, save_sem, rests, pieces, send_sem, recv_sem,
):
    forward_steps(types.SimpleNamespace(**locals()), True)


def forward_alone(
    length, depth, x_in, cot_in, cos, sin, history, vec_in, wj_in, wo_in, wu_in, wd_in, layer_out, normed_out,
    q_out, k_out, v_out, heads_out, middle_out, n2_out, hidden_out, slope_out, parts_out, down_out, vec,
    depth_out, x, cot, parts, down, hist, earlier, normed, q, k, v, heads, middle, n2, hidden, slope, layer,
    depth_acc, load_sem, hist_sem, save_sem,
):
    forward_steps(types.SimpleNamespace(**locals()), False)


def shape(dims, dtype=bf16):
    return jax.ShapeDtypeStruct(dims, dtype)


LIFTED = (HEADS, LIFT, SEQ)
SAVED = (
    shape((D, SEQ)),
    *(shape(LIFTED), shape(LIFTED), shape(LIFTED)),
    shape((D, SEQ)),
    shape((SEQ, D), f32),
    shape((SEQ, D)),
    shape((3, SEQ, SEQ)),
    shape((SEQ, FF)),
    shape((PARTS, 16, 3, 16, D)),
    shape((16, 2, 6, 96, 128)),
)


def vmem(dims, dtype=bf16):
    return pltpu.VMEM(dims, dtype)


def forward(common, special, shared):
    dma = pltpu.SemaphoreType.DMA
    scratch = [
        *(vmem((SEQ, D)), vmem((SEQ, D))),
        *(vmem(s.shape, s.dtype) for s in SAVED[-2:]),
        vmem((2, HIST, 128, D)),
        vmem((SEQ, D), f32),
        *(vmem(s.shape, s.dtype) for s in SAVED[:7]),
        *(vmem((SEQ, FF)), vmem((SEQ, FF)), vmem((SEQ, D))),
        vmem((HIST + 1, 8, D), f32),
        *(dma((24,)), dma((2,)), dma((24,))),
    ]
    if shared:
        scratch += [vmem((PARTS, 4, 2, 3, 4, 16, 128)), vmem((512, 128), f32)]
        scratch += [dma((44,)), dma((44,))]
    return pl.pallas_call(
        forward_shared if shared else forward_alone,
        name="forward_block",
        out_shape=[shape((SEQ, D)), *SAVED, shape((16, FF), f32), shape((8, D), f32)],
        in_specs=[SM, SM, ANY, ANY, VM, VM, ANY] + ([VM] * 6 if shared else [VM] + [ANY] * 4),
        out_specs=[ANY] * (1 + len(SAVED)) + [VM, VM],
        scratch_shapes=scratch,
        compiler_params=pltpu.CompilerParams(
            vmem_limit_bytes=62 << 20,
            collective_id=0 if shared else None,
            has_side_effects=shared,
        ),
    )(*common, *special)


BACKWARD_PLAN = {
    (9, 0): ((Scatter.first, 0),),
    (9, 1): ((Scatter.first, 1),),
    (9, 2): ((Scatter.first, 2),),
    (9, 3): ((Scatter.first, 3),),
    (2, 0): ((Scatter.second, 0),),
    (2, 1): ((Scatter.second, 1),),
    (2, 2): ((Scatter.first, 4), (Scatter.first, 5), (Scatter.second, 2), (Scatter.first, 6)),
    (2, 3): ((Scatter.first, 7), (Scatter.second, 3)),
    (3, 0): ((Scatter.third, 0),),
    (4, 0): ((Scatter.third, 1),),
    (5, 0): ((Scatter.second, 4),),
    (5, 1): ((Scatter.first, 8),),
    (5, 2): ((Scatter.second, 5), (None, 0), (Scatter.third, 2)),
    (8, 9): ((None, 1),),
    (5, 3): ((Scatter.second, 6),),
    (5, 4): ((Scatter.second, 7),),
    (5, 5): ((None, 2), (Scatter.third, 3)),
    (5, 6): ((Scatter.first, 9), (Scatter.third, 4)),
    (8, 10): ((Scatter.second, 8),),
    (5, 7): ((Scatter.third, 5), (Scatter.third, 6)),
    (5, 8): ((None, 3), (Scatter.third, 7)),
    (5, 9): ((None, 4), (Scatter.second, 9), (Scatter.first, 10)),
    (5, 10): ((Scatter.third, 8), (None, 5)),
    (5, 11): ((None, 6), (Scatter.third, 9)),
    (6, 1): ((None, 7), (Scatter.second, 10)),
    (6, 2): ((Scatter.first, 11), (None, 8)),
    (7, 0): ((None, 9), (Scatter.third, 10), (Scatter.first, 12), (Scatter.second, 11), (Scatter.second, 12), (None, 10), (Scatter.third, 11), (Scatter.third, 12), (None, 11)),
}


def backward_steps(r, shared):
    length = r.length[0]
    factor = r.vec[8:9, :D]
    loads = {}

    def load(name, source, target):
        loads[name] = pltpu.make_async_copy(source, target, r.load_sem.at[len(loads)])
        loads[name].start()

    def ready(*keys):
        for key in keys:
            loads[key].wait()

    for i in range(6):
        load(i, r.down_in.at[:, :, i], r.lower.at[:, :, :, pl.ds(i * 128, 128)])
    load("slope", r.slope_in, r.slope)
    load("n2", r.n2_in, r.n2)
    load("hidden", r.hidden_in, r.hidden)
    load("upper", r.parts_in.at[pl.ds(4, 4)], r.upper)
    load("middle", r.middle_in, r.middle)
    load("heads", r.heads_in, r.heads)
    load("k", r.k_in, r.k)
    load("q", r.q_in, r.q)
    load("v", r.v_in, r.v)
    load("normed", r.normed_in, r.normed)
    r.vec_grad[...] = jnp.zeros_like(r.vec_grad)

    if shared:
        links = Links(r.send_sem, r.recv_sem, r.slope, r.middle)
        links.greet()
        scatter = Scatter(links, 0, r.credit, r.packed, r.near, r.one, r.two, r.three)
        small = Scatter(
            links,
            CHUNKS * 4,
            None,
            *(r.vec_packed, r.vec_near, r.vec_one, r.vec_two, r.vec_three),
        )
    waiting = {}
    count = [0]

    def put_out(value, target):
        slot = count[0] % 2
        count[0] += 1
        if slot in waiting:
            waiting.pop(slot).wait()
        rows, cols = value.shape
        r.stage[slot, :rows, :cols] = value
        source = r.stage.at[slot, pl.ds(0, rows), pl.ds(0, cols)]
        copy = pltpu.make_async_copy(source, target, r.stage_sem.at[slot])
        copy.start()
        waiting[slot] = copy

    def place(chunk, half, value):
        slot = chunk % SLOTS
        for i in range(8):
            p = half * 8 + i
            block = value[i * 48 : (i + 1) * 48]
            for y in (0, 1):
                main = block[32 * y : 32 * y + 16].astype(bf16)
                rest = block[16 + 8 * y : 24 + 8 * y]
                rest = jnp.concatenate([rest[:, :HALF], rest[:, HALF:]], axis=0).astype(bf16)
                whole = jnp.concatenate([main, rest], axis=1)
                for n in range(PACK // 128):
                    r.packed[slot, p // 4, y, n, p % 4] = whole[:, n * 128 : (n + 1) * 128]

    def place_down(tile, value):
        for i in range(value.shape[0] // 16):
            owner, t = divmod(tile + i, 6)
            q, z, y = owner // 8, owner % 8 // 2, owner % 2
            block = value[i * 16 : (i + 1) * 16].astype(bf16)
            for n in range(6):
                chunk, col = divmod(t * 6 + n, PACK // 128)
                r.packed[4 + chunk, q, y, col, z] = block[:, n * 128 : (n + 1) * 128]

    def put_part(chunk, make, targets):
        if not shared:
            for half in (0, 1):
                value = make(half)
                for n, target in enumerate(targets):
                    wide = D // len(targets)
                    rows = pl.ds(half * 384, 384)
                    put_out(value[:, n * wide : (n + 1) * wide], target.at[rows])
            return
        steps(8, chunk)
        if chunk >= SLOTS:
            scatter.free(chunk - SLOTS)
        for half in (0, 1):
            place(chunk, half, make(half))
        scatter.start(chunk)

    def finish(chunk):
        total = scatter.total(chunk)
        if 4 <= chunk < 8:
            for n in range(PACK // 128):
                t, col = divmod((chunk - 4) * (PACK // 128) + n, 6)
                r.gd[t * 16 : (t + 1) * 16, col * 128 : (col + 1) * 128] = total[n]
            return
        even = links.y == 0
        for n in range(6):
            rest = total[6 + n % 3][n // 3 * 8 : n // 3 * 8 + 8]
            upper, lower = total[n][0:8], total[n][8:16]
            if chunk < 4:
                target, first = r.gu, chunk * D + n * 128
            elif chunk == 8:
                target, first = r.go, n * 128
            else:
                target, first = r.gj, n // 2 * D + (chunk - 9) * 256 + n % 2 * 128
            cols = slice(first, first + 128)
            target[0:8, cols] = jnp.where(even, upper, rest)
            target[8:16, cols] = jnp.where(even, lower, upper)
            target[16:24, cols] = jnp.where(even, rest, lower)

    def steps(*key):
        if shared:
            for stage, chunk in BACKWARD_PLAN.get(key, ()):
                if stage is None:
                    finish(chunk)
                elif chunk < CHUNKS:
                    stage(scatter, chunk)
                else:
                    stage(small, 0)

    def steps_at(now, count, *key):
        for place in range(count if shared else 0):
            if (*key, place) in BACKWARD_PLAN:

                @pl.when(now == place)
                def _(place=place):
                    steps(*key, place)

    def add_row(row, cols, value):
        r.vec_grad[row : row + 1, cols] += jnp.sum(value, axis=0, keepdims=True)

    for i in range(SEQ // 128):
        rows = slice(i * 128, (i + 1) * 128)
        seed = masked(r.cot, rows, i * 128, 128, length) * factor
        top = (r.depth[HIST] * seed).astype(bf16)
        r.low[rows, :] = top
        add_row(DOWN_BIAS, slice(0, D), top.astype(f32))

    ready("slope", *range(6))

    def up_low(i, carry):
        cols = at((i % 4) * D, D)
        rows = at((i // 4) * 512, 512)
        back = dot(r.low[rows, :], r.lower[pl.ds((i % 4) * 4, 4)].reshape(D, D), 1, 1)
        out = (back * r.slope[rows, cols].astype(f32)).astype(bf16)
        r.slope[rows, cols] = out
        add_row(UP_BIAS, cols, out.astype(f32))
        steps_at(i, 8, 0)
        return carry

    lax.fori_loop(0, 8, up_low, 0)
    load("joint", r.parts_in.at[pl.ds(0, 4)], r.lower.reshape(4, 16, 3, 16, D))

    ready("n2")
    for n in range(4):
        put_part(
            n,
            lambda half, n=n: dot(
                r.n2[:, half * 384 : half * 384 + 384], r.slope[:, n * D : (n + 1) * D], 0, 0
            ),
            None if shared else [r.gu.at[:, pl.ds(n * D, D)]],
        )
        steps(1, n)

    ready("hidden")
    for n in range(6):
        value = dot(r.hidden[n // 2, :, n % 2 * 512 : n % 2 * 512 + 512], r.low[...], 0, 0)
        if shared:
            place_down(n * 32, value)
        else:
            put_out(value, r.gd.at[pl.ds(n * 512, 512)])
        steps(9, n)
    for chunk in range(4, 8 if shared else 4):
        scatter.start(chunk)

    ready("upper", "middle")
    def second_norm(i, carry):
        rows = at(i * 256, 256)
        back = jnp.zeros((256, D), f32)
        for n in range(4):
            back = back + dot(r.slope[rows, n * D : (n + 1) * D], weight(r.upper, n), 1, 1)
        unit, scale = normalize(r.middle[rows, :])
        add_row(GAIN_2, slice(0, D), back * unit)
        add_row(SHIFT_2, slice(0, D), back)
        back = back * r.vec[GAIN_2 : GAIN_2 + 1, :D]
        along = jnp.mean(back * unit, axis=-1, keepdims=True)
        across = jnp.mean(back, axis=-1, keepdims=True)
        seed = masked(r.cot, rows, i * 256, 256, length) * factor
        out = r.depth[HIST] * seed + scale * (back - across - unit * along)
        r.middle[rows, :] = out
        out_low = out.astype(bf16)
        r.low[rows, :] = out_low
        add_row(OUTPUT_BIAS, slice(0, D), out_low.astype(f32))
        steps_at(i, 4, 2)
        return carry

    lax.fori_loop(0, SEQ // 256, second_norm, 0)

    ready("heads", "joint")
    put_part(
        8,
        lambda half: dot(r.heads[half * 384 : half * 384 + 384, :], r.low[...]),
        None if shared else [r.go],
    )
    steps(3, 0)

    def heads_back(i, carry):
        rows = at(i * 256, 256)
        flat = r.lower.reshape(3072 // 16, 16, D)[pl.ds(144 + i * 16, 16)].reshape(256, D)
        back = dot(flat, r.low[...], 1, 1).astype(bf16)
        r.grad[at(i * 4, 4, 4), 0:64, :] = back.reshape(4, 64, SEQ)
        product = back.astype(f32) * r.heads[rows, :].astype(f32)
        for h in range(4):
            total = jnp.sum(product[h * 64 : (h + 1) * 64], axis=0, keepdims=True)
            r.grad[i * 4 + h, 64:80, :] = tail(split_three(-total), SEQ)
        steps_at(i, 3, 4)
        return carry

    lax.fori_loop(0, 3, heads_back, 0)

    ready("k", "q", "v", "normed")
    load("x", r.x_in, r.n2)
    diagonal = causal()

    def turn_back(value):
        upper, lower = value[:32], value[32:]
        cosine, sine = r.cos[...], r.sin[...]
        return jnp.concatenate(
            [upper * cosine + lower * sine, lower * cosine - upper * sine], axis=0
        ).astype(bf16)

    def joint_part(part):
        put_part(
            9 + part,
            lambda half: dot(
                r.normed[half * 384 : half * 384 + 384, :], r.hidden[part, 0:D, :], 1, 1
            ),
            None if shared else [r.gj.at[:, pl.ds(n * D + part * 256, 256)] for n in range(3)],
        )
        sums = jnp.sum(r.hidden[part, 0:D, :].astype(f32), axis=1, keepdims=True)
        sums = jnp.broadcast_to(sums, (D, 8)).T
        for n in range(3):
            first = n * D + part * 256
            r.vec_grad[JOINT_BIAS : JOINT_BIAS + 1, first : first + 256] = sums[
                0:1, n * 256 : (n + 1) * 256
            ]

    def one_head(h, carry):
        keys = r.k[h].T
        values = r.v[h].T
        group = h // 4
        query_rows, key_rows, value_rows = (at(n * 256 + h % 4 * 64, 64, 64) for n in range(3))
        query_grad = jnp.zeros((64, SEQ), f32)
        key_grads = []
        for j in range(SEQ // QB):
            here = slice(j * QB, (j + 1) * QB)
            scores = dot(keys[here], r.q[h, :, j * QB :])
            probs = jnp.exp(scores)
            front = jnp.where(diagonal, probs[:, :QB], 0.0)
            probs = jnp.concatenate([front, probs[:, QB:]], axis=1) if j < 3 else front
            probs_grad = dot(values[here], r.grad[h, :, j * QB :])
            scores_low = (probs * probs_grad).astype(bf16)
            value_grad = dot(r.grad[h, 0:64, j * QB :], probs.astype(bf16), 1, 1)
            r.hidden[group, value_rows, here] = value_grad.astype(bf16)
            key_grads.append(dot(r.q[h, 0:64, j * QB :], scores_low, 1, 1))
            step = dot(r.k[h, 0:64, here], scores_low)
            if j:
                step = jnp.concatenate([jnp.zeros((64, j * QB), f32), step], axis=1)
            query_grad = query_grad + step
        r.hidden[group, query_rows, :] = turn_back(query_grad * 0.125)
        r.hidden[group, key_rows, :] = turn_back(jnp.concatenate(key_grads, axis=1))
        if shared:
            for n in range(3):

                @pl.when(h == n * 4 + 3)
                def _(n=n):
                    joint_part(n)

        steps_at(h, HEADS, 5)
        return carry

    lax.fori_loop(0, HEADS, one_head, 0)
    if not shared:
        for part in range(3):
            joint_part(part)

    ready("x")

    def first_norm(i, carry):
        rows = at(i * 256, 256)
        back = jnp.zeros((256, D), f32)
        for part in range(3):
            flat = r.hidden[part, 0:D, rows].T
            joint = r.lower.reshape(4, 16, 3, 16, D)[part].reshape(D, D)
            back = back + dot(flat, joint, 1, 1)
        unit, scale = normalize(r.n2[rows, :].astype(f32))
        add_row(GAIN_1, slice(0, D), back * unit)
        add_row(SHIFT_1, slice(0, D), back)
        back = back * r.vec[GAIN_1 : GAIN_1 + 1, :D]
        along = jnp.mean(back * unit, axis=-1, keepdims=True)
        across = jnp.mean(back, axis=-1, keepdims=True)
        r.middle[rows, :] = r.middle[rows, :] + scale * (back - across - unit * along)
        steps_at(i, 4, 6)
        return carry

    lax.fori_loop(0, SEQ // 256, first_norm, 0)
    last = pltpu.make_async_copy(r.middle, r.input_grad, r.save_sem.at[0])
    last.start()
    if shared:
        cut_vectors(r.vec_grad, r.maps, r.pieces)
        lane = lax.broadcasted_iota(jnp.int32, (1, 128), 1)
        row = jnp.zeros((1, 128), f32)
        for j in range(HIST + 1):
            total = jnp.sum(r.depth_rows[j : j + 1, :], axis=1, keepdims=True)
            row = jnp.where(lane == j, total, row)
        r.pieces[pl.ds(8, 32, stride=16), :] = jnp.broadcast_to(row, (32, 128))
        for i in range(7):
            r.pieces[pl.ds(9 + i, 32, stride=16), :] = jnp.zeros((32, 128), f32)
        r.vec_packed[0] = r.pieces[...].reshape(4, 2, 1, 4, 16, 128)
        small.start(0)
        steps(7, 0)
        r.pieces_out[...] = small.total(0)[0]
        links.finish()
    for copy in waiting.values():
        copy.wait()
    last.wait()


def backward_shared(
    length, depth, x_in, cot, cos, sin, vec, depth_rows, maps, normed_in, q_in, k_in, v_in, heads_in,
    middle_in, n2_in, hidden_in, slope_in, parts_in, down_in, input_grad, gj, go, gu, gd, pieces_out, upper,
    lower, normed, q, k, v, heads, middle, n2, hidden, slope, low, grad, load_sem, save_sem, packed, near,
    one, two, three, pieces, vec_packed, vec_near, vec_one, vec_two, vec_three, vec_grad, send_sem, recv_sem,
    credit,
):
    backward_steps(types.SimpleNamespace(**locals()), True)


def backward_alone(
    length, depth, x_in, cot, cos, sin, vec, depth_rows, maps, normed_in, q_in, k_in, v_in, heads_in,
    middle_in, n2_in, hidden_in, slope_in, parts_in, down_in, input_grad, gj, go, gu, gd, vec_grad, upper,
    lower, normed, q, k, v, heads, middle, n2, hidden, slope, low, grad, load_sem, save_sem, stage, stage_sem,
):
    backward_steps(types.SimpleNamespace(**locals()), False)


def backward(common, saved, shared):
    dma = pltpu.SemaphoreType.DMA
    local_sizes = SAVED[:9]
    scratch = [
        vmem((4, 16, 3, 16, D)),
        vmem((16, 2, 96, D)),
        *(vmem(s.shape, s.dtype) for s in local_sizes),
        vmem((SEQ, D)),
        vmem(LIFTED),
        *(dma((20,)), dma((1,))),
    ]
    if shared:
        outs = [(24, 3 * D), (24, D), (24, FF), (96, D), (16, 128)]
        scratch += [
            vmem((SLOTS, 4, 2, PACK // 128, 4, 16, 128)),
            vmem((NEAR, 2, 2, PACK // 128, 4, 16, 128)),
            vmem((CHUNKS, 2, PACK // 128, 4, 16, 128)),
            vmem((CHUNKS, PACK // 128, 4, 16, 128)),
            vmem((CHUNKS, 3, PACK // 128, 16, 128)),
            vmem((512, 128), f32),
            vmem((1, 4, 2, 1, 4, 16, 128), f32),
            vmem((1, 2, 2, 1, 4, 16, 128), f32),
            vmem((1, 2, 1, 4, 16, 128), f32),
            vmem((1, 1, 4, 16, 128), f32),
            vmem((1, 3, 1, 16, 128), f32),
            vmem((8, FF), f32),
            *(dma((CHUNKS * 4 + 4,)), dma((CHUNKS * 4 + 4,))),
            pltpu.SemaphoreType.REGULAR,
        ]
    else:
        outs = [(D, 3 * D), (D, D), (D, FF), (FF, D), (8, FF)]
        scratch += [vmem((2, 512, D), f32), dma((2,))]
    return pl.pallas_call(
        backward_shared if shared else backward_alone,
        name="backward_block",
        out_shape=[shape((SEQ, D), f32), *(shape(dims, f32) for dims in outs)],
        in_specs=[SM, SM, ANY] + [VM] * 6 + [ANY] * len(SAVED),
        out_specs=[ANY] + ([VM] * 5 if shared else [ANY] * 4 + [VM]),
        scratch_shapes=scratch,
        compiler_params=pltpu.CompilerParams(
            vmem_limit_bytes=64 << 20,
            collective_id=1 if shared else None,
            has_side_effects=shared,
        ),
    )(*common, *saved)


def results(length, depth, vec, cot_in, pieces, *refs):
    sources, targets, history_grad, rest = refs[:6], refs[6:12], refs[12], refs[13:]
    vectors, held, rest = rest[:-12], rest[-12:-6], rest[-6:]
    cot, stage, cot_sem, in_sem, out_sem, stage_sem = rest
    quarters = [
        pltpu.make_async_copy(
            cot_in.at[pl.ds(i * 256, 256)], cot.at[pl.ds(i * 256, 256)], cot_sem.at[i]
        )
        for i in range(4)
    ]
    for copy in quarters:
        copy.start()
    inward = [
        pltpu.make_async_copy(source, place, in_sem.at[i])
        for i, (source, place) in enumerate(zip(sources, held))
    ]
    outward = [
        pltpu.make_async_copy(place, target, out_sem.at[i])
        for i, (place, target) in enumerate(zip(held, targets))
    ]
    for copy in inward:
        copy.start()
    for i, vector in enumerate(vectors):
        vector[...] = pieces[i : i + 1, : vector.shape[1]]
    factor = vec[8:9, :D]
    waiting = {}
    for i in range(SEQ // 128):
        slot = i % 3
        if i % 2 == 0:
            quarters[i // 2].wait()
        if slot in waiting:
            waiting.pop(slot).wait()
        seed = masked(cot, slice(i * 128, (i + 1) * 128), i * 128, 128, length[0]) * factor
        for j in range(HIST):
            stage[slot, j] = depth[j] * seed
        target = history_grad.at[:, pl.ds(i * 128, 128)]
        waiting[slot] = pltpu.make_async_copy(stage.at[slot], target, stage_sem.at[slot])
        waiting[slot].start()
        if i == 2:
            for copy, onward in zip(inward, outward):
                copy.wait()
                onward.start()
    for copy in [*waiting.values(), *outward]:
        copy.wait()


def write_results(length, depth, vec, cot, pieces, arrays, sizes):
    dma = pltpu.SemaphoreType.DMA
    outs = [shape(a.shape, a.dtype) for a in arrays]
    return pl.pallas_call(
        results,
        out_shape=[
            *(*outs, shape((HIST, SEQ, D), f32)),
            *(shape((1, size), f32) for size in sizes),
        ],
        in_specs=[SM, SM, VM, ANY, VM] + [ANY] * 6,
        out_specs=[ANY] * 7 + [VM] * len(sizes),
        scratch_shapes=[
            *(vmem(s.shape, s.dtype) for s in outs),
            *(vmem((SEQ, D)), vmem((3, HIST, 128, D), f32)),
            *(dma((4,)), dma((6,)), dma((6,)), dma((3,))),
        ],
        compiler_params=pltpu.CompilerParams(vmem_limit_bytes=62 << 20),
    )(length, depth, vec, cot, pieces, *arrays)


def turning_tables():
    half = HEAD_DIM // 2
    frequency = np.power(10000.0, np.arange(half, dtype=np.float64) * (-2.0 / HEAD_DIM))
    angles = frequency[:, None] * np.arange(SEQ, dtype=np.float64)[None, :]
    return np.cos(angles).astype(np.float32), np.sin(angles).astype(np.float32)


def lane_maps():
    maps = np.full((8, FF), -1, np.int32)
    for row, size in ((0, 24), (2, 72), (4, 96)):
        lanes = np.arange(32 * size)
        maps[row, : 32 * size] = lanes // size
        maps[row + 1, : 32 * size] = lanes % size
    return maps


def local(
    inputs,
    history,
    cotangent,
    lengths,
    joint_weight,
    joint_bias,
    output_weight,
    output_bias,
    first_gain,
    first_shift,
    second_gain,
    second_shift,
    upward_weight,
    upward_bias,
    downward_weight,
    downward_bias,
    depth_weights,
):
    devices = lax.axis_size(AXES)
    shared = (lax.axis_size("dp"), lax.axis_size("fsdp")) == (4, 8)
    vectors = (
        joint_bias,
        output_bias,
        first_gain,
        first_shift,
        second_gain,
        second_shift,
        upward_bias,
        downward_bias,
    )
    sizes = [vector.shape[0] for vector in vectors]
    shards = (joint_weight, output_weight, upward_weight, downward_weight)
    x, cot = inputs[0], cotangent[0]
    cosine, sine = turning_tables()
    maps = lane_maps()
    common = (lengths, depth_weights, x, cot, cosine, sine)
    if shared:
        piece = jnp.zeros(16 * 128, f32)
        for i, v in enumerate((*vectors, lengths)):
            after = (15 - i) * 128 + 128 - v.shape[0]
            piece = piece + lax.pad(v.astype(f32), jnp.float32(0), [(i * 128, after, 0)])
        piece = piece.reshape(16, 128)
        special = (maps, piece, *shards)
    else:
        piece = jnp.concatenate([v.astype(f32) for v in (*vectors, lengths)])
        pieces = lax.all_gather(piece, AXES, axis=0, tiled=False).reshape(devices, -1)
        rows, start = [], 0
        for size in sizes:
            row = pieces[:, start : start + size].reshape(1, -1)
            rows.append(jnp.pad(row, ((0, 0), (0, FF - row.shape[1]))))
            start += size
        count = jnp.sum(pieces[:, start:])
        vec = jnp.concatenate([*rows, jnp.full((8, FF), devices * SEQ / count, f32)])
        full = [lax.all_gather(w, AXES, axis=0, tiled=True) for w in shards]
        special = (
            vec,
            *(w.reshape(16, 3, 16, -1) for w in full[:3]),
            full[3].reshape(16, 2, 96, D),
        )
    layer, *saved, vec, depth_rows = forward((*common, history), special, shared)
    input_grad, *grads, vec_grads = backward(
        (*common, vec, depth_rows, maps), saved, shared
    )
    if shared:
        arrays = (layer, input_grad, *grads)
        written = write_results(
            lengths, depth_weights, vec, cot, vec_grads, arrays, [*sizes, HIST + 1]
        )
        layer, input_grad, *grads, history_grad = written[:7]
        outs = [row[0] for row in written[7:]]
        return (
            *(layer[None], input_grad[None], history_grad[:, None]),
            *(grads[0], outs[0], grads[1]),
            *(*outs[1:6], grads[2], outs[6], grads[3], outs[7], outs[8]),
        )
    factor = vec[8, 0]
    positions = jnp.arange(SEQ, dtype=jnp.int32)
    seed = jnp.where(positions[:, None] < lengths[0], cot.astype(f32), 0.0) * factor
    history_gradient = depth_weights[:HIST, None, None, None] * seed[None, None]
    depth_terms = jnp.sum(depth_rows[: HIST + 1], axis=1)
    grads = [lax.psum_scatter(g, AXES, scatter_dimension=0, tiled=True) for g in grads]
    cols = [vec_grads[i, : size * devices].reshape(devices, size) for i, size in enumerate(sizes)]
    cols.append(jnp.broadcast_to(depth_terms[None], (devices, HIST + 1)))
    total = lax.psum_scatter(
        jnp.concatenate(cols, axis=1), AXES, scatter_dimension=0, tiled=False
    )
    outs, start = [], 0
    for size in [*sizes, HIST + 1]:
        outs.append(total[start : start + size])
        start += size
    return (
        layer[None],
        input_grad[None],
        history_gradient,
        grads[0],
        outs[0],
        grads[1],
        *outs[1:6],
        grads[2],
        outs[6],
        grads[3],
        outs[7],
        outs[8],
    )


def solution(mesh):
    row, vector = P(AXES, None), P(AXES)
    tokens, levels = P(AXES, None, None), P(None, AXES, None, None)
    return jax.shard_map(
        local,
        mesh=mesh,
        in_specs=(
            *(tokens, levels, tokens, vector),
            *(row, vector, row, vector),
            *(vector, vector, vector, vector),
            *(row, vector, row, vector, P()),
        ),
        out_specs=(
            *(tokens, tokens, levels),
            *(row, vector, row, vector),
            *(vector, vector, vector, vector),
            *(row, vector, row, vector, P()),
        ),
        check_vma=False,
    )
```

```python
import functools
import math
import types

import jax
import jax.numpy as jnp
import numpy as np
from jax import lax
from jax.experimental import pallas as pl
from jax.experimental.pallas import tpu as pltpu
from jax.sharding import PartitionSpec as P

D = 768
HEADS = 12
HEAD_DIM = 64
FF = 3072
SEQ = 1024
HIST = 4
AXES = ("dp", "fsdp")
EPS = 1e-05
NEG = -1e30
LIFT = 80
QB = 256
C0 = math.sqrt(2.0 / math.pi)
C1 = 0.044715

f32 = jnp.float32
bf16 = jnp.bfloat16
ANY = pl.BlockSpec(memory_space=pl.ANY)
VM = pl.BlockSpec(memory_space=pltpu.VMEM)
SM = pl.BlockSpec(memory_space=pltpu.SMEM)

MESH = pl.DeviceIdType.MESH
HALF = D // 2
PACK = D + HALF
PARTS = 8
CHUNKS = 12
SLOTS = 8
NEAR = 4

JOINT_BIAS, OUTPUT_BIAS, GAIN_1, SHIFT_1, GAIN_2, SHIFT_2, UP_BIAS, DOWN_BIAS = range(8)


def dot(left, right, left_dim=1, right_dim=0):
    return lax.dot_general(
        left, right, (((left_dim,), (right_dim,)), ((), ())), preferred_element_type=f32
    )


def at(start, size, unit=128):
    return pl.ds(pl.multiple_of(start, unit), size)


def normalize(values):
    mean = jnp.mean(values, axis=-1, keepdims=True)
    centred = values - mean
    variance = jnp.mean(centred * centred, axis=-1, keepdims=True)
    scale = lax.rsqrt(variance + EPS)
    return centred * scale, scale


def fold(values):
    rows, cols = values.shape
    return jnp.sum(values.reshape(rows // 8, 8, cols), axis=0)


def split_three(row):
    high = row.astype(bf16).astype(f32)
    rest = row - high
    mid = rest.astype(bf16).astype(f32)
    return high, mid, rest - mid


def tail(rows, width):
    index = lax.broadcasted_iota(jnp.int32, (16, width), 0)
    out = jnp.zeros((16, width), f32)
    for place, row in enumerate(rows):
        out = jnp.where(index == place, row, out)
    return out.astype(bf16)


def position():
    dp, fsdp = lax.axis_index("dp"), lax.axis_index("fsdp")
    return dp // 2, dp % 2, fsdp // 2, fsdp % 2


def device(x, c, z, y):
    return (x * 2 + c, z * 2 + y)


class Links:
    def __init__(self, send_sem, recv_sem, *rulers):
        x, c, z, y = position()
        self.send_sem, self.recv_sem = send_sem, recv_sem
        self.rulers = {jnp.dtype(ruler.dtype): ruler for ruler in rulers}
        self.x, self.c, self.z, self.y = x, c, z, y
        self.nx, self.nc, self.ny = 1 - x, 1 - c, 1 - y
        self.zs = (z + 1 - 2 * (z % 2), (z + 2) % 4, 3 - z)
        self.q, self.r = x * 2 + c, (1 - x) * 2 + c
        self.other_x = device(1 - x, c, z, y)
        self.other_y = device(x, c, z, 1 - y)
        self.other_c = device(x, 1 - c, z, y)
        self.along_z = [device(x, c, other, y) for other in self.zs]
        self.sent = {}

    def greet(self):
        barrier = pltpu.get_barrier_semaphore()
        peers = [self.other_x, self.other_y, self.other_c, *self.along_z]
        for peer in peers:
            pl.semaphore_signal(barrier, inc=1, device_id=peer, device_id_type=MESH)
        pl.semaphore_wait(barrier, len(peers))

    def copy(self, source, target, sem, peer):
        return pltpu.make_async_remote_copy(
            src_ref=source,
            dst_ref=target,
            send_sem=self.send_sem.at[sem],
            recv_sem=self.recv_sem.at[sem],
            device_id=peer,
            device_id_type=MESH,
        )

    def send(self, pairs, sem, peer):
        for source, target in pairs():
            self.copy(source, target, sem, peer).start()
        self.sent.setdefault(sem, []).append(pairs)

    def whole(self, refs, sem):
        size = sum(math.prod(ref.shape) for ref in refs)
        ruler = self.rulers[jnp.dtype(refs[0].dtype)]
        rows = 16
        while size % (rows * 128) or size // rows > ruler.shape[1]:
            rows += 16
        part = ruler.at[pl.ds(0, rows), pl.ds(0, size // rows)]
        return self.copy(part, part, sem, self.other_c)

    def arrived(self, targets, sem):
        self.whole(targets, sem).wait_recv()

    def left(self, sem):
        sources = [pair[0] for pairs in self.sent.pop(sem, []) for pair in pairs()]
        if sources:
            self.whole(sources, sem).wait_send()

    def finish(self):
        for sem in list(self.sent):
            self.left(sem)


DOWN = (PARTS, PARTS + 1)
VECTORS = PARTS + 2
WIDE = 512


class Gather:
    def __init__(self, links, parts, rests, down, pieces):
        self.links = links
        self.parts, self.rests, self.down, self.pieces = parts, rests, down, pieces

    def refs(self, item, q, y, z, color):
        if item == VECTORS:
            if color == 1:
                return []
            first = (q * 8 + y * 4 + (0 if z is None else z)) * 16
            return [self.pieces.at[at(first, 64 if z is None else 16, 16)]]
        rows = pl.ds(q * 4, 4) if z is None else q * 4 + z
        if item in DOWN:
            first, last = (0, 4) if item == PARTS else (4, 6)
            mid = (first + last) // 2
            first, last = {None: (first, last), 0: (first, mid), 1: (mid, last)}[color]
            return [self.down.at[rows, y, pl.ds(first, last - first)]]
        wide = {None: pl.ds(0, D), 0: pl.ds(0, HALF), 1: pl.ds(HALF, HALF)}[color]
        cut = 2 if item % 2 else 1
        narrow = {None: pl.ds(0, 3), 0: pl.ds(0, cut), 1: pl.ds(cut, 3 - cut)}[color]
        some = pl.ds(0, 4) if z is None else z
        return [
            self.parts.at[item, rows, 2 * y, :, wide],
            self.rests.at[item, q, y, narrow, some],
        ]

    def send(self, item, stage, peer, quads, z=None):
        def pairs():
            refs = []
            for q, y, color in quads:
                refs += self.refs(item, getattr(self.links, q), getattr(self.links, y), z, color)
            return [(ref, ref) for ref in refs]

        self.links.send(pairs, item * 4 + stage, peer)

    def start(self, item):
        links = self.links
        if item in DOWN:
            self.send(item, 0, links.other_x, [("q", "y", 0)], links.z)
            self.send(item, 0, links.other_y, [("q", "y", 1)], links.z)
            return
        for peer in links.along_z:
            self.send(item, 0, peer, [("q", "y", None)], links.z)

    def second(self, item):
        links = self.links
        if item in DOWN:
            refs = self.refs(item, links.r, links.y, links.z, 0)
            links.arrived(refs + self.refs(item, links.q, links.ny, links.z, 1), item * 4)
            quads = [("q", "y", 0), ("r", "y", 0), ("q", "y", 1), ("q", "ny", 1)]
            for peer in links.along_z:
                self.send(item, 1, peer, quads, links.z)
            return
        refs = [self.refs(item, links.q, links.y, z, None) for z in links.zs]
        links.arrived(sum(refs, []), item * 4)
        self.send(item, 1, links.other_x, [("q", "y", 0)])
        self.send(item, 1, links.other_y, [("q", "y", 1)])

    def third(self, item):
        links = self.links
        if item in DOWN:
            quads = [(links.q, links.y, 0), (links.r, links.y, 0)]
            quads += [(links.q, links.y, 1), (links.q, links.ny, 1)]
            refs = [self.refs(item, q, y, z, k) for q, y, k in quads for z in links.zs]
            links.arrived(sum(refs, []), item * 4 + 1)
        else:
            refs = self.refs(item, links.r, links.y, None, 0)
            links.arrived(refs + self.refs(item, links.q, links.ny, None, 1), item * 4 + 1)
        first = [("q", "y", 0), ("r", "y", 0)]
        second = [("q", "y", 1), ("q", "ny", 1)]
        self.send(item, 2, links.other_y, first)
        self.send(item, 2, links.other_x, second)
        self.send(item, 3, links.other_c, first + second)

    def fourth(self, item):
        links = self.links
        quads = [("q", "ny", 0), ("r", "ny", 0), ("r", "y", 1), ("r", "ny", 1)]
        refs = [self.refs(item, getattr(links, q), getattr(links, y), None, k) for q, y, k in quads]
        links.arrived(sum(refs, []), item * 4 + 2)
        self.send(item, 3, links.other_c, quads)

    def ready(self, item):
        links = self.links
        refs = []
        for xx in (0, 1):
            for yy in (0, 1):
                for color in (0, 1):
                    refs += self.refs(item, xx * 2 + links.nc, yy, None, color)
        links.arrived(refs, item * 4 + 3)
        if item < PARTS:

            def merge(p, carry):
                q, z = p // 4, p % 4
                for i in range(3):
                    even = self.rests[item, q, 0, i, z].astype(f32)
                    odd = self.rests[item, q, 1, i, z].astype(f32)
                    for k in (0, 1):
                        first = k * HALF + i * 128
                        half = slice(k * 8, k * 8 + 8)
                        self.parts[item, p, 1, :, first : first + 128] = jnp.concatenate(
                            [even[half], odd[half]], axis=0
                        ).astype(bf16)
                return carry

            lax.fori_loop(0, 16, merge, 0)

    def own(self, item, shard):
        links = self.links
        full = shard.astype(f32)
        even = links.y == 0
        main = jnp.where(even, full[0:16], full[8:24])
        rest = jnp.where(even, full[16:24], full[0:8])
        self.parts[item, links.q * 4 + links.z, 2 * links.y] = main.astype(bf16)
        for i in range(3):
            left, right = rest[:, i * 128 : (i + 1) * 128], rest[:, HALF + i * 128 :][:, :128]
            self.rests[item, links.q, links.y, i, links.z] = jnp.concatenate(
                [left, right], axis=0
            ).astype(bf16)


def block_order():
    index = lax.broadcasted_iota(jnp.int32, (32, 1), 0)
    return (index & 24) + (index & 3) * 2 + ((index >> 2) & 1)


def spread(maps_ref, size):
    row = {24: 0, 72: 2, 96: 4}[size]
    wide = 32 * size
    owner = maps_ref[row : row + 1, :wide] == block_order()
    lane = maps_ref[row + 1 : row + 2, :wide] == lax.broadcasted_iota(jnp.int32, (128, 1), 0)
    return owner, jnp.where(lane, 1.0, 0.0).astype(bf16)


VECTOR_SIZES = (72, 24, 24, 24, 24, 24, 96, 24)


def join_vectors(pieces_ref, maps_ref, vec_ref):
    for size in (24, 72, 96):
        owner, lane = spread(maps_ref, size)
        for row, own in enumerate(VECTOR_SIZES):
            if own == size:
                piece = pieces_ref[pl.ds(row, 32, stride=16), :].astype(bf16)
                full = jnp.where(owner, dot(piece, lane), 0.0)
                vec_ref[row : row + 1, : 32 * size] = jnp.sum(full, axis=0, keepdims=True)
    counts = pieces_ref[pl.ds(8, 32, stride=16), :]
    count = jnp.sum(jnp.sum(counts, axis=0, keepdims=True), axis=1, keepdims=True)
    vec_ref[8:16, :] = jnp.broadcast_to((32 * SEQ) / count, (8, FF))


def cut_vectors(vec_ref, maps_ref, pieces_ref):
    for size in (24, 72, 96):
        owner, lane = spread(maps_ref, size)
        for row, own in enumerate(VECTOR_SIZES):
            if own == size:
                full = jnp.where(owner, vec_ref[row : row + 1, : 32 * size], 0.0)
                high = full.astype(bf16)
                low = (full - high.astype(f32)).astype(bf16)
                pieces_ref[pl.ds(row, 32, stride=16), :] = dot(high, lane, 1, 1) + dot(
                    low, lane, 1, 1
                )


class Scatter:
    def __init__(self, links, base, credit, packed, near, one, two, three):
        self.links, self.base, self.credit = links, base, credit
        self.packed, self.near = packed, near
        self.one, self.two, self.three = one, two, three
        self.wide = packed.shape[3]

    def columns(self, chunk):
        mid = (self.wide + 1 - chunk % 2) // 2
        return pl.ds(0, mid), pl.ds(mid, self.wide - mid)

    def send(self, chunk, stage, peer, pairs, cols=None):
        if cols is None or cols.size:
            self.links.send(pairs, self.base + chunk * 4 + stage, peer)

    def start(self, chunk):
        links = self.links
        if self.credit is not None and chunk >= NEAR:
            pl.semaphore_wait(self.credit, 1)

        def pairs():
            return [
                (
                    self.packed.at[chunk % SLOTS, xx * 2 + links.nc],
                    self.near.at[chunk % NEAR, xx],
                )
                for xx in (0, 1)
            ]

        self.send(chunk, 0, links.other_c, pairs)

    def first(self, chunk):
        links = self.links
        slot, near = chunk % SLOTS, chunk % NEAR
        links.arrived([self.near.at[near, xx] for xx in (0, 1)], self.base + chunk * 4)

        def add(i, carry):
            xx, yy = i // 2, i % 2
            mine = self.packed[slot, xx * 2 + links.c, yy]
            self.packed[slot, xx * 2 + links.c, yy] = mine + self.near[near, xx, yy]
            return carry

        lax.fori_loop(0, 4, add, 0)
        if self.credit is not None and chunk + NEAR < CHUNKS:
            pl.semaphore_signal(self.credit, inc=1, device_id=links.other_c, device_id_type=MESH)
        here, there = self.columns(chunk)

        def by_y():
            return [
                (self.packed.at[slot, k * 2 + links.c, links.ny, here], self.one.at[chunk, k, here])
                for k in (0, 1)
            ]

        def by_x():
            return [
                (self.packed.at[slot, links.r, k, there], self.one.at[chunk, k, there])
                for k in (0, 1)
            ]

        self.send(chunk, 1, links.other_y, by_y, here)
        self.send(chunk, 1, links.other_x, by_x, there)

    def second(self, chunk):
        links = self.links
        slot = chunk % SLOTS
        links.arrived([self.one.at[chunk, k] for k in (0, 1)], self.base + chunk * 4 + 1)
        here, there = self.columns(chunk)
        for k in (0, 1):
            for cols, q, y in ((here, k * 2 + links.c, links.y), (there, links.q, k)):
                if cols.size:
                    mine = self.packed[slot, q, y, cols]
                    self.one[chunk, k, cols] = mine + self.one[chunk, k, cols]
        self.send(
            chunk,
            2,
            links.other_x,
            lambda: [(self.one.at[chunk, links.nx, here], self.two.at[chunk, here])],
            here,
        )
        self.send(
            chunk,
            2,
            links.other_y,
            lambda: [(self.one.at[chunk, links.ny, there], self.two.at[chunk, there])],
            there,
        )

    def third(self, chunk):
        links = self.links
        links.arrived([self.two.at[chunk]], self.base + chunk * 4 + 2)
        for cols, mine in zip(self.columns(chunk), (links.x, links.y)):
            if cols.size:
                self.two[chunk, cols] = self.one[chunk, mine, cols] + self.two[chunk, cols]
        for k in range(3):

            def pairs(k=k):
                return [(self.two.at[chunk, :, links.zs[k]], self.three.at[chunk, k])]

            self.send(chunk, 3, links.along_z[k], pairs)

    def total(self, chunk):
        links = self.links
        links.arrived([self.three.at[chunk, k] for k in range(3)], self.base + chunk * 4 + 3)
        parts = [self.two[chunk, :, links.z]] + [self.three[chunk, k] for k in range(3)]
        parts = [part.astype(f32) for part in parts]
        return (parts[0] + parts[1]) + (parts[2] + parts[3])

    def free(self, chunk):
        self.links.left(self.base + chunk * 4)
        self.links.left(self.base + chunk * 4 + 1)


def weight(parts_ref, item):
    return parts_ref[item].reshape(D, D)


def masked(cot_ref, rows, start, count, length):
    index = lax.broadcasted_iota(jnp.int32, (count, 1), 0) + start
    return jnp.where(index < length, cot_ref[rows, :].astype(f32), 0.0)


def causal():
    shape = (QB, QB)
    return lax.broadcasted_iota(jnp.int32, shape, 0) <= lax.broadcasted_iota(jnp.int32, shape, 1)


FORWARD_PLAN = {
    (0, 7): ((Gather.second, 10), (Gather.second, 8), (Gather.second, 9), (Gather.second, 0), (Gather.third, 10), (Gather.second, 1), (Gather.third, 0), (Gather.fourth, 10), (Gather.second, 2)),
    (1, 7): ((Gather.third, 1),),
    (2, 0, 0): ((Gather.second, 3), (Gather.fourth, 0), (Gather.third, 2), (Gather.second, 4)),
    (3, 1): ((Gather.fourth, 1), (Gather.second, 5)),
    (3, 2): ((Gather.third, 3),),
    (3, 3): ((Gather.second, 6), (Gather.fourth, 2)),
    (2, 1, 3): ((Gather.third, 4),),
    (3, 4): ((Gather.second, 7), (Gather.third, 5)),
    (3, 6): ((Gather.fourth, 3),),
    (3, 7): ((Gather.third, 6),),
    (3, 8): ((Gather.fourth, 4),),
    (3, 9): ((Gather.third, 7),),
    (3, 10): ((Gather.fourth, 5),),
    (5, 1): ((Gather.fourth, 6), (Gather.third, 8)),
    (6, 1): ((Gather.fourth, 7),),
    (6, 4): ((Gather.third, 9),),
    (6, 7): ((Gather.fourth, 8),),
    (7, 8): ((Gather.fourth, 9),),
}


def forward_steps(r, shared):
    length = r.length[0]
    hb = 128

    def hist_copy(step, slot):
        return pltpu.make_async_copy(
            r.history.at[:, 0, pl.ds(step * hb, hb)], r.hist.at[slot], r.hist_sem.at[slot]
        )

    first_loads = [
        pltpu.make_async_copy(r.cot_in, r.cot, r.load_sem.at[22]),
        pltpu.make_async_copy(r.x_in, r.x, r.load_sem.at[23]),
    ]
    first_loads[0].start()
    hist_copy(0, 0).start()
    hist_copy(1, 1).start()
    first_loads[1].start()
    if shared:
        links = Links(r.send_sem, r.recv_sem, r.hidden, r.earlier)
        gather = Gather(links, r.parts, r.rests, r.down, r.pieces)
        links.greet()
        place = (links.q * 8 + links.y * 4 + links.z) * 16
        r.pieces[at(place, 16, 16), :] = r.piece[...]
        gather.start(VECTORS)
        for part in range(3):
            own = [r.wj_in[:, i * D + part * 256 :][:, :256] for i in range(3)]
            gather.own(part, jnp.concatenate(own, axis=1))
            gather.start(part)
        gather.own(3, r.wo_in[...])
        gather.start(3)
        for part in range(4):
            gather.own(4 + part, r.wu_in[:, part * D : (part + 1) * D])
            gather.start(4 + part)
        for i in range(6):
            r.down[links.q * 4 + links.z, links.y, i] = r.wd_in[:, i * 128 : (i + 1) * 128]
        for item in DOWN:
            gather.start(item)
        ready = gather.ready
    else:
        plain = [(r.wo_in, 0)] + [(r.wu_in, n * D) for n in range(4)]
        pairs = [
            [
                (r.wj_in.at[:, :, :, pl.ds(i * D + g * 256, 256)], r.parts.at[g, :, :, :, pl.ds(i * 256, 256)])
                for i in range(3)
            ]
            for g in range(3)
        ]
        for n, (source, first) in enumerate(plain):
            pairs.append([(source.at[:, :, :, pl.ds(first, D)], r.parts.at[3 + n])])
        pairs.append(
            [(r.wd_in.at[:, :, :, pl.ds(i * 128, 128)], r.down.at[:, :, i]) for i in range(6)]
        )
        loads, used = [], 0
        for pair in pairs:
            loads.append([])
            for source, target in pair:
                loads[-1].append(pltpu.make_async_copy(source, target, r.load_sem.at[used]))
                loads[-1][-1].start()
                used += 1
        r.vec[...] = r.vec_in[...]

        def ready(item):
            if item != DOWN[1]:
                for load in loads[item]:
                    load.wait()

    def steps(*key):
        if shared:
            for stage, item in FORWARD_PLAN.get(key, ()):
                stage(gather, item)

    def steps_at(now, count, *key):
        for place in range(count if shared else 0):
            if (*key, place) in FORWARD_PLAN:

                @pl.when(now == place)
                def _(place=place):
                    steps(*key, place)

    r.depth_acc[...] = jnp.zeros_like(r.depth_acc)
    first_loads[0].wait()
    for step in range(SEQ // hb):
        slot = step % 2
        hist_copy(step, slot).wait()

        def part(i, carry, slot=slot, step=step):
            rows = pl.ds(pl.multiple_of(i * 32, 32), 32)
            here = pl.ds(pl.multiple_of(step * hb + i * 32, 32), 32)
            seed = masked(r.cot, here, step * hb + i * 32, 32, length)
            total = jnp.zeros((32, D), f32)
            for j in range(HIST):
                part_hist = r.hist[slot, j, rows, :].astype(f32)
                total = total + r.depth[j] * part_hist
                r.depth_acc[j] = r.depth_acc[j] + fold(seed * part_hist)
            r.earlier[here, :] = total
            return carry

        lax.fori_loop(0, hb // 32, part, 0)
        if step + 2 < SEQ // hb:
            hist_copy(step + 2, slot).start()
        steps(0, step)
    if shared:
        ready(VECTORS)
        join_vectors(r.pieces, r.maps, r.vec)
    factor = r.vec[8:9, :D]

    first_loads[1].wait()
    for i in range(SEQ // 128):
        rows = slice(i * 128, (i + 1) * 128)
        unit, _ = normalize(r.x[rows, :].astype(f32))
        full = unit * r.vec[GAIN_1 : GAIN_1 + 1, :D] + r.vec[SHIFT_1 : SHIFT_1 + 1, :D]
        r.normed[:, rows] = full.T.astype(bf16)
        steps(1, i)
    saves = []

    def save(source, target):
        copy = pltpu.make_async_copy(source, target, r.save_sem.at[len(saves)])
        copy.start()
        saves.append(copy)

    save(r.normed, r.normed_out)

    keys_at = lax.broadcasted_iota(jnp.int32, (1, SEQ), 1)
    key_bias = jnp.where(keys_at < length, 0.0, NEG)
    one = jnp.ones((1, SEQ), f32)
    bias_cols = r.vec[0:8, : 3 * D].T
    kinds = ((r.q, (one,)), (r.k, (key_bias, one, one, one)), (r.v, (one, one, one)))
    for target, rows in kinds:
        extra = tail(rows, SEQ)
        for h in range(HEADS):
            target[h, 64:80, :] = extra

    def four_heads(group):
        steps(2, group, 0)
        ready(group)
        for kind, (target, _) in enumerate(kinds):
            cols = slice(kind * 256, (kind + 1) * 256)
            joined = dot(r.parts[group, :, :, :, cols].reshape(D, 256), r.normed[...], 0, 0)
            first = kind * D + group * 256
            joined = joined + bias_cols[first : first + 256, 0:1]
            for h in range(4):
                upper = joined[h * 64 : h * 64 + 32]
                lower = joined[h * 64 + 32 : h * 64 + 64]
                if kind < 2:
                    cosine, sine = r.cos[...], r.sin[...]
                    upper, lower = upper * cosine - lower * sine, lower * cosine + upper * sine
                both = jnp.concatenate([upper, lower], axis=0).astype(bf16)
                if kind == 0:
                    both = both * jnp.asarray(0.125, bf16)
                target[group * 4 + h, 0:64, :] = both
            steps(2, group, kind + 1)

    diagonal = causal()

    def one_head(h, carry):
        for group in range(3):

            @pl.when(h == group * 4)
            def _(group=group):
                four_heads(group)

        keys, queries, values = r.k[h].T, r.q[h], r.v[h]
        outs, tails = [], []
        for i in range(SEQ // QB):
            cols = slice(i * QB, (i + 1) * QB)
            seen = (i + 1) * QB
            scores = dot(keys[:seen], queries[:, cols])
            last = jnp.where(diagonal, scores[seen - QB :], NEG)
            scores = jnp.concatenate([scores[: seen - QB], last], axis=0) if i else last
            top = jnp.max(scores, axis=0, keepdims=True)
            weights = jnp.exp(scores - top).astype(bf16)
            out = dot(values[:, :seen], weights)
            total = out[64:65]
            outs.append((out[:64] / total).astype(bf16))
            log_total = -(top + jnp.log(total))
            tails.append(tail((jnp.ones((1, QB), f32), *split_three(log_total)), QB))
        r.heads[at(h * 64, 64, 64), :] = jnp.concatenate(outs, axis=1)
        r.q[h, 64:80, :] = jnp.concatenate(tails, axis=1)
        steps_at(h, HEADS, 3)
        return carry

    lax.fori_loop(0, HEADS, one_head, 0)
    save(r.parts.at[pl.ds(0, 3)], r.parts_out.at[pl.ds(0, 3)])
    save(r.q, r.q_out)
    save(r.k, r.k_out)
    save(r.v, r.v_out)
    save(r.heads, r.heads_out)

    steps(4, 0)
    ready(3)

    def project(i, carry):
        rows = at(i * 256, 256)
        out = dot(r.heads[:, rows], weight(r.parts, 3), 0, 0)
        mid = r.x[rows, :].astype(f32) + (out + r.vec[OUTPUT_BIAS : OUTPUT_BIAS + 1, :D])
        r.middle[rows, :] = mid
        unit, _ = normalize(mid)
        r.n2[rows, :] = (
            unit * r.vec[GAIN_2 : GAIN_2 + 1, :D] + r.vec[SHIFT_2 : SHIFT_2 + 1, :D]
        ).astype(bf16)
        steps_at(i, 4, 5)
        return carry

    lax.fori_loop(0, SEQ // 256, project, 0)
    save(r.middle, r.middle_out)
    save(r.n2, r.n2_out)
    def upward(i, carry):
        steps_at(i, 8, 6)
        for n in range(4):

            @pl.when(i == n)
            def _(n=n):
                ready(4 + n)

        rows = at((i // 4) * 512, 512)
        cols = at((i % 4) * D, D)
        up = dot(r.n2[rows, :], weight(r.parts, 4 + i % 4))
        up = up + r.vec[UP_BIAS : UP_BIAS + 1, cols]
        square = up * up
        turn = jnp.tanh(up * (C0 + (C0 * C1) * square))
        half = 0.5 + 0.5 * turn
        r.hidden[rows, cols] = (up * half).astype(bf16)
        bent = (2.0 * up) * (C0 + (3.0 * C0 * C1) * square)
        r.slope[rows, cols] = (half + bent * (half * (1.0 - half))).astype(bf16)
        return carry

    lax.fori_loop(0, 8, upward, 0)
    save(r.parts.at[pl.ds(3, 5)], r.parts_out.at[pl.ds(3, 5)])
    save(r.slope, r.slope_out)
    for n in range(3):
        save(r.hidden.at[:, pl.ds(n * SEQ, SEQ)], r.hidden_out.at[n])

    def downward(cols, i, carry):
        rows = at(i * 256, 256)
        blocks = range(cols.start // 128, cols.stop // 128)
        down = [r.down[:, :, n].reshape(FF, 128) for n in blocks]
        out = dot(r.hidden[rows, :], jnp.concatenate(down, axis=1))
        block = r.middle[rows, cols] + (out + r.vec[DOWN_BIAS : DOWN_BIAS + 1, cols])
        r.layer[rows, cols] = (r.earlier[rows, cols] + r.depth[HIST] * block).astype(bf16)
        index = lax.broadcasted_iota(jnp.int32, (256, 1), 0) + i * 256
        seed = jnp.where(index < length, r.cot[rows, cols].astype(f32), 0.0)
        r.depth_acc[HIST, :, cols] = r.depth_acc[HIST, :, cols] + fold(seed * block)
        steps_at(i, 4, 8, cols.start)
        return carry

    for item in DOWN:
        steps(7, item)
        ready(item)
        cols = slice(0, WIDE) if item == PARTS else slice(WIDE, D)
        blocks = pl.ds(cols.start // 128, (cols.stop - cols.start) // 128)
        save(r.down.at[:, :, blocks], r.down_out.at[:, :, blocks])
        lax.fori_loop(0, SEQ // 256, functools.partial(downward, cols), 0)
    save(r.layer, r.layer_out)
    r.depth_out[...] = jnp.zeros_like(r.depth_out)
    for j in range(HIST + 1):
        r.depth_out[j : j + 1, :] = jnp.sum(r.depth_acc[j], axis=0, keepdims=True) * factor
    if shared:
        links.finish()
    for copy in saves:
        copy.wait()


def forward_shared(
    length, depth, x_in, cot_in, cos, sin, history, maps, piece, wj_in, wo_in, wu_in, wd_in, layer_out, normed_out,
    q_out, k_out, v_out, heads_out, middle_out, n2_out, hidden_out, slope_out, parts_out, down_out, vec,
    depth_out, x, cot, parts, down, hist, earlier, normed, q, k, v, heads, middle, n2, hidden, slope, layer,
    depth_acc, load_sem, hist_sem, save_sem, rests, pieces, send_sem, recv_sem,
):
    forward_steps(types.SimpleNamespace(**locals()), True)


def forward_alone(
    length, depth, x_in, cot_in, cos, sin, history, vec_in, wj_in, wo_in, wu_in, wd_in, layer_out, normed_out,
    q_out, k_out, v_out, heads_out, middle_out, n2_out, hidden_out, slope_out, parts_out, down_out, vec,
    depth_out, x, cot, parts, down, hist, earlier, normed, q, k, v, heads, middle, n2, hidden, slope, layer,
    depth_acc, load_sem, hist_sem, save_sem,
):
    forward_steps(types.SimpleNamespace(**locals()), False)


def shape(dims, dtype=bf16):
    return jax.ShapeDtypeStruct(dims, dtype)


LIFTED = (HEADS, LIFT, SEQ)
SAVED = (
    shape((D, SEQ)),
    *(shape(LIFTED), shape(LIFTED), shape(LIFTED)),
    shape((D, SEQ)),
    shape((SEQ, D), f32),
    shape((SEQ, D)),
    shape((3, SEQ, SEQ)),
    shape((SEQ, FF)),
    shape((PARTS, 16, 3, 16, D)),
    shape((16, 2, 6, 96, 128)),
)


def vmem(dims, dtype=bf16):
    return pltpu.VMEM(dims, dtype)


def forward(common, special, shared):
    dma = pltpu.SemaphoreType.DMA
    scratch = [
        *(vmem((SEQ, D)), vmem((SEQ, D))),
        *(vmem(s.shape, s.dtype) for s in SAVED[-2:]),
        vmem((2, HIST, 128, D)),
        vmem((SEQ, D), f32),
        *(vmem(s.shape, s.dtype) for s in SAVED[:7]),
        *(vmem((SEQ, FF)), vmem((SEQ, FF)), vmem((SEQ, D))),
        vmem((HIST + 1, 8, D), f32),
        *(dma((24,)), dma((2,)), dma((24,))),
    ]
    if shared:
        scratch += [vmem((PARTS, 4, 2, 3, 4, 16, 128)), vmem((512, 128), f32)]
        scratch += [dma((44,)), dma((44,))]
    return pl.pallas_call(
        forward_shared if shared else forward_alone,
        name="forward_block",
        out_shape=[shape((SEQ, D)), *SAVED, shape((16, FF), f32), shape((8, D), f32)],
        in_specs=[SM, SM, ANY, ANY, VM, VM, ANY] + ([VM] * 6 if shared else [VM] + [ANY] * 4),
        out_specs=[ANY] * (1 + len(SAVED)) + [VM, VM],
        scratch_shapes=scratch,
        compiler_params=pltpu.CompilerParams(
            vmem_limit_bytes=62 << 20,
            collective_id=0 if shared else None,
            has_side_effects=shared,
        ),
    )(*common, *special)


BACKWARD_PLAN = {
    (1, 3): ((Scatter.first, 0),),
    (9, 0): ((Scatter.first, 1),),
    (9, 1): ((Scatter.first, 2), (Scatter.first, 3)),
    (9, 3): ((Scatter.second, 0),),
    (2, 0): ((Scatter.second, 1),),
    (2, 1): ((Scatter.first, 4), (Scatter.second, 2), (Scatter.first, 5)),
    (2, 2): ((Scatter.first, 6), (Scatter.second, 3), (Scatter.first, 7), (Scatter.third, 0)),
    (2, 3): ((Scatter.third, 1),),
    (4, 0): ((Scatter.second, 4),),
    (4, 2): ((None, 0), (Scatter.third, 2)),
    (5, 0): ((Scatter.first, 8),),
    (5, 1): ((None, 1), (Scatter.second, 5)),
    (5, 2): ((None, 2), (Scatter.second, 6)),
    (8, 9): ((Scatter.third, 3),),
    (5, 3): ((Scatter.second, 7),),
    (5, 4): ((Scatter.third, 4),),
    (5, 5): ((Scatter.first, 9), (None, 3), (Scatter.second, 8)),
    (5, 6): ((Scatter.third, 5),),
    (8, 10): ((Scatter.third, 6), (None, 4), (Scatter.third, 7)),
    (5, 8): ((Scatter.second, 9), (None, 5)),
    (5, 9): ((Scatter.third, 8), (Scatter.first, 10), (None, 6)),
    (5, 10): ((Scatter.third, 9),),
    (8, 11): ((None, 7),),
    (5, 11): ((Scatter.second, 10), (None, 8)),
    (6, 1): ((None, 9), (Scatter.first, 11), (Scatter.third, 10)),
    (7, 0): ((Scatter.second, 11), (None, 10), (Scatter.first, 12), (Scatter.third, 11), (Scatter.second, 12), (Scatter.third, 12), (None, 11)),
}


def backward_steps(r, shared):
    length = r.length[0]
    factor = r.vec[8:9, :D]
    loads = {}

    def load(name, source, target):
        loads[name] = pltpu.make_async_copy(source, target, r.load_sem.at[len(loads)])
        loads[name].start()

    def ready(*keys):
        for key in keys:
            loads[key].wait()

    for i in range(6):
        load(i, r.down_in.at[:, :, i], r.lower.at[:, :, :, pl.ds(i * 128, 128)])
    load("slope", r.slope_in, r.slope)
    load("n2", r.n2_in, r.n2)
    load("hidden", r.hidden_in, r.hidden)
    load("upper", r.parts_in.at[pl.ds(4, 4)], r.upper)
    load("middle", r.middle_in, r.middle)
    load("heads", r.heads_in, r.heads)
    load("k", r.k_in, r.k)
    load("q", r.q_in, r.q)
    load("v", r.v_in, r.v)
    load("normed", r.normed_in, r.normed)
    r.vec_grad[...] = jnp.zeros_like(r.vec_grad)

    if shared:
        links = Links(r.send_sem, r.recv_sem, r.slope, r.middle)
        links.greet()
        scatter = Scatter(links, 0, r.credit, r.packed, r.near, r.one, r.two, r.three)
        small = Scatter(
            links,
            CHUNKS * 4,
            None,
            *(r.vec_packed, r.vec_near, r.vec_one, r.vec_two, r.vec_three),
        )
    waiting = {}
    count = [0]

    def put_out(value, target):
        slot = count[0] % 2
        count[0] += 1
        if slot in waiting:
            waiting.pop(slot).wait()
        rows, cols = value.shape
        r.stage[slot, :rows, :cols] = value
        source = r.stage.at[slot, pl.ds(0, rows), pl.ds(0, cols)]
        copy = pltpu.make_async_copy(source, target, r.stage_sem.at[slot])
        copy.start()
        waiting[slot] = copy

    def place(chunk, half, value):
        slot = chunk % SLOTS
        for i in range(8):
            p = half * 8 + i
            block = value[i * 48 : (i + 1) * 48]
            for y in (0, 1):
                main = block[32 * y : 32 * y + 16].astype(bf16)
                rest = block[16 + 8 * y : 24 + 8 * y]
                rest = jnp.concatenate([rest[:, :HALF], rest[:, HALF:]], axis=0).astype(bf16)
                whole = jnp.concatenate([main, rest], axis=1)
                for n in range(PACK // 128):
                    r.packed[slot, p // 4, y, n, p % 4] = whole[:, n * 128 : (n + 1) * 128]

    def place_down(tile, value):
        for i in range(value.shape[0] // 16):
            owner, t = divmod(tile + i, 6)
            q, z, y = owner // 8, owner % 8 // 2, owner % 2
            block = value[i * 16 : (i + 1) * 16].astype(bf16)
            for n in range(6):
                chunk, col = divmod(t * 6 + n, PACK // 128)
                r.packed[4 + chunk, q, y, col, z] = block[:, n * 128 : (n + 1) * 128]

    def put_part(chunk, make, targets):
        if not shared:
            for half in (0, 1):
                value = make(half)
                for n, target in enumerate(targets):
                    wide = D // len(targets)
                    rows = pl.ds(half * 384, 384)
                    put_out(value[:, n * wide : (n + 1) * wide], target.at[rows])
            return
        steps(8, chunk)
        if chunk >= SLOTS:
            scatter.free(chunk - SLOTS)
        for half in (0, 1):
            place(chunk, half, make(half))
        scatter.start(chunk)

    def finish(chunk):
        total = scatter.total(chunk)
        if 4 <= chunk < 8:
            for n in range(PACK // 128):
                t, col = divmod((chunk - 4) * (PACK // 128) + n, 6)
                r.gd[t * 16 : (t + 1) * 16, col * 128 : (col + 1) * 128] = total[n]
            return
        even = links.y == 0
        for n in range(6):
            rest = total[6 + n % 3][n // 3 * 8 : n // 3 * 8 + 8]
            upper, lower = total[n][0:8], total[n][8:16]
            if chunk < 4:
                target, first = r.gu, chunk * D + n * 128
            elif chunk == 8:
                target, first = r.go, n * 128
            else:
                target, first = r.gj, n // 2 * D + (chunk - 9) * 256 + n % 2 * 128
            cols = slice(first, first + 128)
            target[0:8, cols] = jnp.where(even, upper, rest)
            target[8:16, cols] = jnp.where(even, lower, upper)
            target[16:24, cols] = jnp.where(even, rest, lower)

    def steps(*key):
        if shared:
            for stage, chunk in BACKWARD_PLAN.get(key, ()):
                if stage is None:
                    finish(chunk)
                elif chunk < CHUNKS:
                    stage(scatter, chunk)
                else:
                    stage(small, 0)

    def steps_at(now, count, *key):
        for place in range(count if shared else 0):
            if (*key, place) in BACKWARD_PLAN:

                @pl.when(now == place)
                def _(place=place):
                    steps(*key, place)

    def add_row(row, cols, value):
        r.vec_grad[row : row + 1, cols] += jnp.sum(value, axis=0, keepdims=True)

    for i in range(SEQ // 128):
        rows = slice(i * 128, (i + 1) * 128)
        seed = masked(r.cot, rows, i * 128, 128, length) * factor
        top = (r.depth[HIST] * seed).astype(bf16)
        r.low[rows, :] = top
        add_row(DOWN_BIAS, slice(0, D), top.astype(f32))

    ready("slope", *range(6))

    def up_low(i, carry):
        cols = at((i % 4) * D, D)
        rows = at((i // 4) * 512, 512)
        back = dot(r.low[rows, :], r.lower[pl.ds((i % 4) * 4, 4)].reshape(D, D), 1, 1)
        out = (back * r.slope[rows, cols].astype(f32)).astype(bf16)
        r.slope[rows, cols] = out
        add_row(UP_BIAS, cols, out.astype(f32))
        steps_at(i, 8, 0)
        return carry

    lax.fori_loop(0, 8, up_low, 0)
    load("joint", r.parts_in.at[pl.ds(0, 4)], r.lower.reshape(4, 16, 3, 16, D))

    ready("n2")
    for n in range(4):
        put_part(
            n,
            lambda half, n=n: dot(
                r.n2[:, half * 384 : half * 384 + 384], r.slope[:, n * D : (n + 1) * D], 0, 0
            ),
            None if shared else [r.gu.at[:, pl.ds(n * D, D)]],
        )
        steps(1, n)

    ready("hidden")
    for n in range(6):
        value = dot(r.hidden[n // 2, :, n % 2 * 512 : n % 2 * 512 + 512], r.low[...], 0, 0)
        if shared:
            place_down(n * 32, value)
        else:
            put_out(value, r.gd.at[pl.ds(n * 512, 512)])
        steps(9, n)
    for chunk in range(4, 8 if shared else 4):
        scatter.start(chunk)

    ready("upper", "middle")
    def second_norm(i, carry):
        rows = at(i * 256, 256)
        back = jnp.zeros((256, D), f32)
        for n in range(4):
            back = back + dot(r.slope[rows, n * D : (n + 1) * D], weight(r.upper, n), 1, 1)
        unit, scale = normalize(r.middle[rows, :])
        add_row(GAIN_2, slice(0, D), back * unit)
        add_row(SHIFT_2, slice(0, D), back)
        back = back * r.vec[GAIN_2 : GAIN_2 + 1, :D]
        along = jnp.mean(back * unit, axis=-1, keepdims=True)
        across = jnp.mean(back, axis=-1, keepdims=True)
        seed = masked(r.cot, rows, i * 256, 256, length) * factor
        out = r.depth[HIST] * seed + scale * (back - across - unit * along)
        r.middle[rows, :] = out
        out_low = out.astype(bf16)
        r.low[rows, :] = out_low
        add_row(OUTPUT_BIAS, slice(0, D), out_low.astype(f32))
        steps_at(i, 4, 2)
        return carry

    lax.fori_loop(0, SEQ // 256, second_norm, 0)

    ready("heads", "joint")
    put_part(
        8,
        lambda half: dot(r.heads[half * 384 : half * 384 + 384, :], r.low[...]),
        None if shared else [r.go],
    )
    steps(3, 0)

    def heads_back(i, carry):
        rows = at(i * 256, 256)
        flat = r.lower.reshape(3072 // 16, 16, D)[pl.ds(144 + i * 16, 16)].reshape(256, D)
        back = dot(flat, r.low[...], 1, 1).astype(bf16)
        r.grad[at(i * 4, 4, 4), 0:64, :] = back.reshape(4, 64, SEQ)
        product = back.astype(f32) * r.heads[rows, :].astype(f32)
        for h in range(4):
            total = jnp.sum(product[h * 64 : (h + 1) * 64], axis=0, keepdims=True)
            r.grad[i * 4 + h, 64:80, :] = tail(split_three(-total), SEQ)
        steps_at(i, 3, 4)
        return carry

    lax.fori_loop(0, 3, heads_back, 0)

    ready("k", "q", "v", "normed")
    load("x", r.x_in, r.n2)
    diagonal = causal()

    def turn_back(value):
        upper, lower = value[:32], value[32:]
        cosine, sine = r.cos[...], r.sin[...]
        return jnp.concatenate(
            [upper * cosine + lower * sine, lower * cosine - upper * sine], axis=0
        ).astype(bf16)

    def joint_part(part):
        put_part(
            9 + part,
            lambda half: dot(
                r.normed[half * 384 : half * 384 + 384, :], r.hidden[part, 0:D, :], 1, 1
            ),
            None if shared else [r.gj.at[:, pl.ds(n * D + part * 256, 256)] for n in range(3)],
        )
        sums = jnp.sum(r.hidden[part, 0:D, :].astype(f32), axis=1, keepdims=True)
        sums = jnp.broadcast_to(sums, (D, 8)).T
        for n in range(3):
            first = n * D + part * 256
            r.vec_grad[JOINT_BIAS : JOINT_BIAS + 1, first : first + 256] = sums[
                0:1, n * 256 : (n + 1) * 256
            ]

    def one_head(h, carry):
        keys = r.k[h].T
        values = r.v[h].T
        group = h // 4
        query_rows, key_rows, value_rows = (at(n * 256 + h % 4 * 64, 64, 64) for n in range(3))
        query_grad = jnp.zeros((64, SEQ), f32)
        key_grads = []
        for j in range(SEQ // QB):
            here = slice(j * QB, (j + 1) * QB)
            scores = dot(keys[here], r.q[h, :, j * QB :])
            probs = jnp.exp(scores)
            front = jnp.where(diagonal, probs[:, :QB], 0.0)
            probs = jnp.concatenate([front, probs[:, QB:]], axis=1) if j < 3 else front
            probs_grad = dot(values[here], r.grad[h, :, j * QB :])
            scores_low = (probs * probs_grad).astype(bf16)
            value_grad = dot(r.grad[h, 0:64, j * QB :], probs.astype(bf16), 1, 1)
            r.hidden[group, value_rows, here] = value_grad.astype(bf16)
            key_grads.append(dot(r.q[h, 0:64, j * QB :], scores_low, 1, 1))
            step = dot(r.k[h, 0:64, here], scores_low)
            if j:
                step = jnp.concatenate([jnp.zeros((64, j * QB), f32), step], axis=1)
            query_grad = query_grad + step
        r.hidden[group, query_rows, :] = turn_back(query_grad * 0.125)
        r.hidden[group, key_rows, :] = turn_back(jnp.concatenate(key_grads, axis=1))
        if shared:
            for n in range(3):

                @pl.when(h == n * 4 + 3)
                def _(n=n):
                    joint_part(n)

        steps_at(h, HEADS, 5)
        return carry

    lax.fori_loop(0, HEADS, one_head, 0)
    if not shared:
        for part in range(3):
            joint_part(part)

    ready("x")

    def first_norm(i, carry):
        rows = at(i * 256, 256)
        back = jnp.zeros((256, D), f32)
        for part in range(3):
            flat = r.hidden[part, 0:D, rows].T
            joint = r.lower.reshape(4, 16, 3, 16, D)[part].reshape(D, D)
            back = back + dot(flat, joint, 1, 1)
        unit, scale = normalize(r.n2[rows, :].astype(f32))
        add_row(GAIN_1, slice(0, D), back * unit)
        add_row(SHIFT_1, slice(0, D), back)
        back = back * r.vec[GAIN_1 : GAIN_1 + 1, :D]
        along = jnp.mean(back * unit, axis=-1, keepdims=True)
        across = jnp.mean(back, axis=-1, keepdims=True)
        r.middle[rows, :] = r.middle[rows, :] + scale * (back - across - unit * along)
        steps_at(i, 4, 6)
        return carry

    lax.fori_loop(0, SEQ // 256, first_norm, 0)
    last = pltpu.make_async_copy(r.middle, r.input_grad, r.save_sem.at[0])
    last.start()
    if shared:
        cut_vectors(r.vec_grad, r.maps, r.pieces)
        lane = lax.broadcasted_iota(jnp.int32, (1, 128), 1)
        row = jnp.zeros((1, 128), f32)
        for j in range(HIST + 1):
            total = jnp.sum(r.depth_rows[j : j + 1, :], axis=1, keepdims=True)
            row = jnp.where(lane == j, total, row)
        r.pieces[pl.ds(8, 32, stride=16), :] = jnp.broadcast_to(row, (32, 128))
        for i in range(7):
            r.pieces[pl.ds(9 + i, 32, stride=16), :] = jnp.zeros((32, 128), f32)
        r.vec_packed[0] = r.pieces[...].reshape(4, 2, 1, 4, 16, 128)
        small.start(0)
        steps(7, 0)
        r.pieces_out[...] = small.total(0)[0]
        links.finish()
    for copy in waiting.values():
        copy.wait()
    last.wait()


def backward_shared(
    length, depth, x_in, cot, cos, sin, vec, depth_rows, maps, normed_in, q_in, k_in, v_in, heads_in,
    middle_in, n2_in, hidden_in, slope_in, parts_in, down_in, input_grad, gj, go, gu, gd, pieces_out, upper,
    lower, normed, q, k, v, heads, middle, n2, hidden, slope, low, grad, load_sem, save_sem, packed, near,
    one, two, three, pieces, vec_packed, vec_near, vec_one, vec_two, vec_three, vec_grad, send_sem, recv_sem,
    credit,
):
    backward_steps(types.SimpleNamespace(**locals()), True)


def backward_alone(
    length, depth, x_in, cot, cos, sin, vec, depth_rows, maps, normed_in, q_in, k_in, v_in, heads_in,
    middle_in, n2_in, hidden_in, slope_in, parts_in, down_in, input_grad, gj, go, gu, gd, vec_grad, upper,
    lower, normed, q, k, v, heads, middle, n2, hidden, slope, low, grad, load_sem, save_sem, stage, stage_sem,
):
    backward_steps(types.SimpleNamespace(**locals()), False)


def backward(common, saved, shared):
    dma = pltpu.SemaphoreType.DMA
    local_sizes = SAVED[:9]
    scratch = [
        vmem((4, 16, 3, 16, D)),
        vmem((16, 2, 96, D)),
        *(vmem(s.shape, s.dtype) for s in local_sizes),
        vmem((SEQ, D)),
        vmem(LIFTED),
        *(dma((20,)), dma((1,))),
    ]
    if shared:
        outs = [(24, 3 * D), (24, D), (24, FF), (96, D), (16, 128)]
        scratch += [
            vmem((SLOTS, 4, 2, PACK // 128, 4, 16, 128)),
            vmem((NEAR, 2, 2, PACK // 128, 4, 16, 128)),
            vmem((CHUNKS, 2, PACK // 128, 4, 16, 128)),
            vmem((CHUNKS, PACK // 128, 4, 16, 128)),
            vmem((CHUNKS, 3, PACK // 128, 16, 128)),
            vmem((512, 128), f32),
            vmem((1, 4, 2, 1, 4, 16, 128), f32),
            vmem((1, 2, 2, 1, 4, 16, 128), f32),
            vmem((1, 2, 1, 4, 16, 128), f32),
            vmem((1, 1, 4, 16, 128), f32),
            vmem((1, 3, 1, 16, 128), f32),
            vmem((8, FF), f32),
            *(dma((CHUNKS * 4 + 4,)), dma((CHUNKS * 4 + 4,))),
            pltpu.SemaphoreType.REGULAR,
        ]
    else:
        outs = [(D, 3 * D), (D, D), (D, FF), (FF, D), (8, FF)]
        scratch += [vmem((2, 512, D), f32), dma((2,))]
    return pl.pallas_call(
        backward_shared if shared else backward_alone,
        name="backward_block",
        out_shape=[shape((SEQ, D), f32), *(shape(dims, f32) for dims in outs)],
        in_specs=[SM, SM, ANY] + [VM] * 6 + [ANY] * len(SAVED),
        out_specs=[ANY] + ([VM] * 5 if shared else [ANY] * 4 + [VM]),
        scratch_shapes=scratch,
        compiler_params=pltpu.CompilerParams(
            vmem_limit_bytes=64 << 20,
            collective_id=1 if shared else None,
            has_side_effects=shared,
        ),
    )(*common, *saved)


def results(length, depth, vec, cot_in, pieces, *refs):
    sources, targets, history_grad, rest = refs[:6], refs[6:12], refs[12], refs[13:]
    vectors, held, rest = rest[:-12], rest[-12:-6], rest[-6:]
    cot, stage, cot_sem, in_sem, out_sem, stage_sem = rest
    quarters = [
        pltpu.make_async_copy(
            cot_in.at[pl.ds(i * 256, 256)], cot.at[pl.ds(i * 256, 256)], cot_sem.at[i]
        )
        for i in range(4)
    ]
    for copy in quarters:
        copy.start()
    inward = [
        pltpu.make_async_copy(source, place, in_sem.at[i])
        for i, (source, place) in enumerate(zip(sources, held))
    ]
    outward = [
        pltpu.make_async_copy(place, target, out_sem.at[i])
        for i, (place, target) in enumerate(zip(held, targets))
    ]
    for copy in inward:
        copy.start()
    for i, vector in enumerate(vectors):
        vector[...] = pieces[i : i + 1, : vector.shape[1]]
    factor = vec[8:9, :D]
    waiting = {}
    for i in range(SEQ // 128):
        slot = i % 3
        if i % 2 == 0:
            quarters[i // 2].wait()
        if slot in waiting:
            waiting.pop(slot).wait()
        seed = masked(cot, slice(i * 128, (i + 1) * 128), i * 128, 128, length[0]) * factor
        for j in range(HIST):
            stage[slot, j] = depth[j] * seed
        target = history_grad.at[:, pl.ds(i * 128, 128)]
        waiting[slot] = pltpu.make_async_copy(stage.at[slot], target, stage_sem.at[slot])
        waiting[slot].start()
        if i == 2:
            for copy, onward in zip(inward, outward):
                copy.wait()
                onward.start()
    for copy in [*waiting.values(), *outward]:
        copy.wait()


def write_results(length, depth, vec, cot, pieces, arrays, sizes):
    dma = pltpu.SemaphoreType.DMA
    outs = [shape(a.shape, a.dtype) for a in arrays]
    return pl.pallas_call(
        results,
        out_shape=[
            *(*outs, shape((HIST, SEQ, D), f32)),
            *(shape((1, size), f32) for size in sizes),
        ],
        in_specs=[SM, SM, VM, ANY, VM] + [ANY] * 6,
        out_specs=[ANY] * 7 + [VM] * len(sizes),
        scratch_shapes=[
            *(vmem(s.shape, s.dtype) for s in outs),
            *(vmem((SEQ, D)), vmem((3, HIST, 128, D), f32)),
            *(dma((4,)), dma((6,)), dma((6,)), dma((3,))),
        ],
        compiler_params=pltpu.CompilerParams(vmem_limit_bytes=62 << 20),
    )(length, depth, vec, cot, pieces, *arrays)


def turning_tables():
    half = HEAD_DIM // 2
    frequency = np.power(10000.0, np.arange(half, dtype=np.float64) * (-2.0 / HEAD_DIM))
    angles = frequency[:, None] * np.arange(SEQ, dtype=np.float64)[None, :]
    return np.cos(angles).astype(np.float32), np.sin(angles).astype(np.float32)


def lane_maps():
    maps = np.full((8, FF), -1, np.int32)
    for row, size in ((0, 24), (2, 72), (4, 96)):
        lanes = np.arange(32 * size)
        maps[row, : 32 * size] = lanes // size
        maps[row + 1, : 32 * size] = lanes % size
    return maps


def local(
    inputs,
    history,
    cotangent,
    lengths,
    joint_weight,
    joint_bias,
    output_weight,
    output_bias,
    first_gain,
    first_shift,
    second_gain,
    second_shift,
    upward_weight,
    upward_bias,
    downward_weight,
    downward_bias,
    depth_weights,
):
    devices = lax.axis_size(AXES)
    shared = (lax.axis_size("dp"), lax.axis_size("fsdp")) == (4, 8)
    vectors = (
        joint_bias,
        output_bias,
        first_gain,
        first_shift,
        second_gain,
        second_shift,
        upward_bias,
        downward_bias,
    )
    sizes = [vector.shape[0] for vector in vectors]
    shards = (joint_weight, output_weight, upward_weight, downward_weight)
    x, cot = inputs[0], cotangent[0]
    cosine, sine = turning_tables()
    maps = lane_maps()
    common = (lengths, depth_weights, x, cot, cosine, sine)
    if shared:
        piece = jnp.zeros(16 * 128, f32)
        for i, v in enumerate((*vectors, lengths)):
            after = (15 - i) * 128 + 128 - v.shape[0]
            piece = piece + lax.pad(v.astype(f32), jnp.float32(0), [(i * 128, after, 0)])
        piece = piece.reshape(16, 128)
        special = (maps, piece, *shards)
    else:
        piece = jnp.concatenate([v.astype(f32) for v in (*vectors, lengths)])
        pieces = lax.all_gather(piece, AXES, axis=0, tiled=False).reshape(devices, -1)
        rows, start = [], 0
        for size in sizes:
            row = pieces[:, start : start + size].reshape(1, -1)
            rows.append(jnp.pad(row, ((0, 0), (0, FF - row.shape[1]))))
            start += size
        count = jnp.sum(pieces[:, start:])
        vec = jnp.concatenate([*rows, jnp.full((8, FF), devices * SEQ / count, f32)])
        full = [lax.all_gather(w, AXES, axis=0, tiled=True) for w in shards]
        special = (
            vec,
            *(w.reshape(16, 3, 16, -1) for w in full[:3]),
            full[3].reshape(16, 2, 96, D),
        )
    layer, *saved, vec, depth_rows = forward((*common, history), special, shared)
    input_grad, *grads, vec_grads = backward(
        (*common, vec, depth_rows, maps), saved, shared
    )
    if shared:
        arrays = (layer, input_grad, *grads)
        written = write_results(
            lengths, depth_weights, vec, cot, vec_grads, arrays, [*sizes, HIST + 1]
        )
        layer, input_grad, *grads, history_grad = written[:7]
        outs = [row[0] for row in written[7:]]
        return (
            *(layer[None], input_grad[None], history_grad[:, None]),
            *(grads[0], outs[0], grads[1]),
            *(*outs[1:6], grads[2], outs[6], grads[3], outs[7], outs[8]),
        )
    factor = vec[8, 0]
    positions = jnp.arange(SEQ, dtype=jnp.int32)
    seed = jnp.where(positions[:, None] < lengths[0], cot.astype(f32), 0.0) * factor
    history_gradient = depth_weights[:HIST, None, None, None] * seed[None, None]
    depth_terms = jnp.sum(depth_rows[: HIST + 1], axis=1)
    grads = [lax.psum_scatter(g, AXES, scatter_dimension=0, tiled=True) for g in grads]
    cols = [vec_grads[i, : size * devices].reshape(devices, size) for i, size in enumerate(sizes)]
    cols.append(jnp.broadcast_to(depth_terms[None], (devices, HIST + 1)))
    total = lax.psum_scatter(
        jnp.concatenate(cols, axis=1), AXES, scatter_dimension=0, tiled=False
    )
    outs, start = [], 0
    for size in [*sizes, HIST + 1]:
        outs.append(total[start : start + size])
        start += size
    return (
        layer[None],
        input_grad[None],
        history_gradient,
        grads[0],
        outs[0],
        grads[1],
        *outs[1:6],
        grads[2],
        outs[6],
        grads[3],
        outs[7],
        outs[8],
    )


def solution(mesh):
    row, vector = P(AXES, None), P(AXES)
    tokens, levels = P(AXES, None, None), P(None, AXES, None, None)
    return jax.shard_map(
        local,
        mesh=mesh,
        in_specs=(
            *(tokens, levels, tokens, vector),
            *(row, vector, row, vector),
            *(vector, vector, vector, vector),
            *(row, vector, row, vector, P()),
        ),
        out_specs=(
            *(tokens, tokens, levels),
            *(row, vector, row, vector),
            *(vector, vector, vector, vector),
            *(row, vector, row, vector, P()),
        ),
        check_vma=False,
    )
```
